32 devices in a mesh: dp: 8 (over y, x, core), pipe: 4 (over z).
Axes of the slice: x: 2, y: 2, z: 4, core: 2. Of those that a mesh axis runs over, the one named last changes fastest.
Arguments:
- tokens: bfloat16 [2, 4, 1024, 768], P(None, 'pipe', 'dp'), may hold values from -6 to 6
- lengths: int32 [2, 4, 1], P(None, 'pipe'), may hold values from 960 to 1024, as said below
- cotangent: bfloat16 [2, 4, 1024, 768], P(None, 'pipe', 'dp'), may hold values from -6 to 6
- gain_attn: bfloat16 [768], P('dp'), may hold values from 0.5 to 1.5
- w_query: bfloat16 [768, 768], P('dp'), may hold values from -0.21875 to 0.21875
- w_key: bfloat16 [768, 768], P('dp'), may hold values from -0.21875 to 0.21875
- w_value: bfloat16 [768, 768], P('dp'), may hold values from -0.21875 to 0.21875
- w_out: bfloat16 [768, 768], P('dp'), may hold values from -3 to 3
- gain_mlp: bfloat16 [768], P('dp'), may hold values from 0.5 to 1.5
- w_up: bfloat16 [768, 3072], P('dp'), may hold values from -0.21875 to 0.21875
- w_down: bfloat16 [3072, 768], P('dp'), may hold values from -0.109375 to 0.109375
- pos_bias: bfloat16 [1024, 1024], P('dp'), may hold values from -4 to 4
Outputs:
- output: bfloat16 [2, 4, 1024, 768], P(None, 'pipe', 'dp')
- grad_tokens: bfloat16 [2, 4, 1024, 768], P(None, 'pipe', 'dp')
- grad_gain_attn: float32 [768], P('dp')
- grad_w_query: float32 [768, 768], P('dp')
- grad_w_key: float32 [768, 768], P('dp')
- grad_w_value: float32 [768, 768], P('dp')
- grad_w_out: float32 [768, 768], P('dp')
- grad_gain_mlp: float32 [768], P('dp')
- grad_w_up: float32 [768, 3072], P('dp')
- grad_w_down: float32 [3072, 768], P('dp')
- grad_pos_bias: float32 [1024, 1024], P('dp')
The draws below stay inside these ranges and needn't reach their ends.
Inputs may be any that keep to these rules, and one draw needn't show every extreme that they name: `lengths`: every sequence has 960 real tokens or more; in every draw some sequence is full and some has exactly that least count.
All inputs are finite; a program needn't handle non-finite values.
Results may differ from the reference program's by a relative error of at most 0.012.
Values may be sent and summed in bfloat16 or wider, within the bound.
A program may use at most 192 MiB of HBM per device.

```python
import jax
import jax.numpy as jnp
from jax import lax

D = 768
FF = 3072
SEQ = 1024
WIN = 256
MBATCH = 2
TOK_MB = 128
GROUPS = 4
GROUP_TOK = 1024
GSEQ = 1


def draw_lengths(key, part):
    key = jax.random.fold_in(key, 11)
    least_len = SEQ - TOK_MB // 2
    seq_total = MBATCH * GROUPS * GSEQ
    key_lengths, key_order = jax.random.split(key)
    drawn = jax.random.randint(key_lengths, (seq_total,), least_len, SEQ + 1)
    order = jax.random.permutation(key_order, seq_total)
    drawn = drawn.at[order[0]].set(SEQ).at[order[1]].set(least_len)
    return drawn.reshape(MBATCH, GROUPS, GSEQ).astype(jnp.int32)


def block_levels(own_key, extent, cuts, least, top_value):
    loudness, own = 1.0, jax.random.fold_in(own_key, 6)
    for dim, shards_of in cuts:
        heights = jnp.exp(jax.random.uniform(jax.random.fold_in(own, dim), (shards_of,), jnp.float32, least / len(cuts), top_value / len(cuts)))
        loudness = loudness * jnp.repeat(heights, extent[dim] // shards_of).reshape([-1 if axis == dim else 1 for axis in range(len(extent))])
    return loudness


def centred(rng, extent, scale, limit, cuts=(), kind=jnp.bfloat16):
    array = jax.random.normal(rng, extent, jnp.float32) * scale
    if len(cuts) > 0:
        array = block_levels(rng, extent, cuts, -0.22, 0.18) * array
    return jnp.clip(array, min=-limit, max=limit).astype(kind)


def setup_inputs(seed: int = 0) -> dict:
    seeds = jax.random.split(jax.random.key(seed), 13)
    return {
        "tokens": centred(seeds[0], (MBATCH, GROUPS, GROUP_TOK, D), 1.0, 6.0, ((1, 4), (2, 8))),
        "lengths": draw_lengths(jax.random.fold_in(seeds[12], 71), 0),
        "cotangent": centred(seeds[2], (MBATCH, GROUPS, GROUP_TOK, D), 1.0, 6.0, ((1, 4), (2, 8))),
        "gain_attn": jnp.clip(1.0 + 0.1 * jax.random.normal(seeds[3], (D,), jnp.float32), 0.5, 1.5).astype(jnp.bfloat16),
        "w_query": centred(seeds[4], (D, D), D ** -0.5, 0.21875, ((0, 8),)),
        "w_key": centred(seeds[5], (D, D), D ** -0.5, 0.21875, ((0, 8),)),
        "w_value": centred(seeds[6], (D, D), D ** -0.5, 0.21875, ((0, 8),)),
        "w_out": centred(seeds[7], (D, D), (max(1, D // 192)) ** -0.5, 3.0, ((0, 8),)),
        "gain_mlp": jnp.clip(1.0 + 0.1 * jax.random.normal(seeds[8], (D,), jnp.float32), 0.5, 1.5).astype(jnp.bfloat16),
        "w_up": centred(seeds[9], (D, FF), D ** -0.5, 0.21875, ((0, 8),)),
        "w_down": centred(seeds[10], (FF, D), FF ** -0.5, 0.109375, ((0, 8),)),
        "pos_bias": centred(seeds[11], (SEQ, SEQ), 1.0, 4.0, ((0, 8),)),
    }


@jax.custom_vjp
def low(v):
    return lax.optimization_barrier(v.astype(jnp.bfloat16)).astype(jnp.float32)

@jax.custom_vjp
def low_back(v):
    return v

def low_keep(v):
    return (low(v), None)

def low_pass(kept, grad):
    return (grad,)

def back_keep(v):
    return (v, None)

def back_low(kept, grad):
    return (low(grad),)
low.defvjp(low_keep, low_pass)
low_back.defvjp(back_keep, back_low)
EPSILON = 1e-05

def product(left, right):
    return jnp.dot(left, right, precision=lax.Precision.HIGHEST, preferred_element_type=jnp.float32)

def normalize(values, gain):
    centre = values - lax.optimization_barrier(jnp.mean(values, axis=-1, keepdims=True))
    spread = lax.optimization_barrier(jnp.mean(centre * centre, axis=-1, keepdims=True))
    return centre * lax.rsqrt(spread + EPSILON) * gain

def band_ones():
    row_ids = jnp.arange(WIN)[:, None]
    col_ids = jnp.arange(3 * WIN)[None, :]
    return (jnp.abs(col_ids - WIN - row_ids) < WIN).astype(jnp.float32)

def band_blocks(bias):
    padded = jnp.pad(bias, ((0, 0), (WIN, WIN)))
    return jnp.stack([padded[block * WIN:(block + 1) * WIN, block * WIN:block * WIN + 3 * WIN] for block in range(SEQ // WIN)])

def windows(operand):
    padded = jnp.pad(operand, ((WIN, WIN), (0, 0))).reshape(SEQ // WIN + 2, WIN, operand.shape[1])
    return jnp.concatenate([padded[:-2], padded[1:-1], padded[2:]], axis=1)

def to_columns(matrix):
    return matrix.reshape(GSEQ, SEQ, D).transpose(1, 0, 2).reshape(SEQ, GSEQ * D)

def from_columns(matrix):
    return matrix.reshape(SEQ, GSEQ, D).transpose(1, 0, 2).reshape(GSEQ * SEQ, D)

def layer(inputs, valid, params):
    gain_a, query_w, key_w, value_w, out_w, gain_m, up_w, down_w, bias = params
    normed = low(normalize(inputs, gain_a))
    query = low_back(product(normed, query_w))
    keys = low_back(low(product(normed, key_w)))
    values = low_back(low(product(normed, value_w)))
    valid_cols = jnp.broadcast_to(valid.T[:, :, None], (SEQ, GSEQ, D)).reshape(SEQ, GSEQ * D)
    weighted = jnp.exp(to_columns(keys)) * valid_cols
    operand = jnp.concatenate([low(weighted * to_columns(values)), low(weighted)], axis=1)
    kernel = low((jnp.exp(band_blocks(bias)) - 1.0) * band_ones())
    banded = jnp.einsum('nqk,nkc->nqc', kernel, windows(operand), precision=lax.Precision.HIGHEST).reshape(SEQ, 2 * GSEQ * D)
    result = banded + lax.optimization_barrier(jnp.sum(operand, axis=0))[None, :]
    numerator = low_back(result[:, :GSEQ * D])
    denominator = low_back(result[:, GSEQ * D:]) + 1.0 - valid_cols
    mixed = from_columns(low_back(low(numerator / denominator * valid_cols)))
    gated = low(jax.nn.sigmoid(query) * mixed)
    resid = inputs + low_back(product(gated, out_w))
    normed_two = low(normalize(resid, gain_m))
    hidden = low(jax.nn.gelu(low_back(product(normed_two, up_w)), approximate=True))
    return resid + product(hidden, down_w)

def reference(tokens, lengths, cotangent, gain_attn, w_query, w_key, w_value, w_out, gain_mlp, w_up, w_down, pos_bias):
    params = tuple((param_value.astype(jnp.float32) for param_value in (gain_attn, w_query, w_key, w_value, w_out, gain_mlp, w_up, w_down, pos_bias)))
    flat_tokens = tokens.reshape(MBATCH * GROUPS, GROUP_TOK, D)
    flat_cot = cotangent.reshape(MBATCH * GROUPS, GROUP_TOK, D)
    flat_lengths = lengths.reshape(MBATCH * GROUPS, GSEQ)
    positions = jnp.arange(SEQ).astype(jnp.int32)

    def step(totals, inputs):
        block_tokens, block_lengths, block_cot = inputs
        valid = (positions[None, :] < block_lengths[:, None].astype(jnp.int32)).astype(jnp.float32)

        def forward(values, weights):
            return layer(values, valid, weights)
        result, pullback = jax.vjp(forward, block_tokens.astype(jnp.float32), params)
        grad_in, grads = pullback(block_cot.astype(jnp.float32))
        totals = jax.tree.map(lambda running, update: running + update, totals, grads)
        return (totals, (result.astype(jnp.bfloat16), grad_in.astype(jnp.bfloat16)))
    zeros_init = jax.tree.map(jnp.zeros_like, params)
    totals, (outputs, grads_in) = lax.scan(step, zeros_init, (flat_tokens, flat_lengths, flat_cot))
    return (outputs.reshape(tokens.shape), grads_in.reshape(tokens.shape), totals[0], totals[1], totals[2], totals[3], totals[4], totals[5], totals[6], totals[7], totals[8])
```

```python
import types

import jax
import jax.numpy as jnp
from jax import lax
from jax.experimental import pallas as pl
from jax.experimental.pallas import tpu as pltpu
from jax.sharding import PartitionSpec as P

D = 768
FF = 3072
SEQ = 1024
WIN = 256


EPSILON = 1e-05
GELU_SCALE = 0.7978845608028654
GELU_CUBE = 0.044715
VMEM_BYTES = 63 * 2**20


def normalize(values, gain):
    centre = values - jnp.mean(values, axis=-1, keepdims=True)
    spread = jnp.mean(centre * centre, axis=-1, keepdims=True)
    return centre * lax.rsqrt(spread + EPSILON) * gain


def gelu_tanh(values):
    return jax.nn.gelu(values, approximate=True)


def band_ones(width):
    row_ids = jnp.arange(width)[:, None]
    col_ids = jnp.arange(3 * width)[None, :]
    return (jnp.abs(col_ids - width - row_ids) < width).astype(jnp.float32)


def band_blocks(bias, width):
    length = bias.shape[0]
    padded = jnp.pad(bias, ((0, 0), (width, width)))
    return jnp.stack(
        [
            padded[block * width : (block + 1) * width, block * width : block * width + 3 * width]
            for block in range(length // width)
        ]
    )


def windows(operand, width):
    blocks = operand.shape[0] // width
    padded = jnp.pad(operand, ((width, width), (0, 0))).reshape(blocks + 2, width, operand.shape[1])
    return jnp.concatenate([padded[:-2], padded[1:-1], padded[2:]], axis=1)


def unwindow(grad_windows, width):
    blocks = grad_windows.shape[0]
    leading = jnp.pad(grad_windows[:, :width], ((0, 2), (0, 0), (0, 0)))
    middle = jnp.pad(grad_windows[:, width : 2 * width], ((1, 1), (0, 0), (0, 0)))
    trailing = jnp.pad(grad_windows[:, 2 * width :], ((2, 0), (0, 0), (0, 0)))
    summed = leading + middle + trailing
    return summed[1:-1].reshape(blocks * width, grad_windows.shape[2])


def to_columns(matrix, seq_count, length):
    channels = matrix.shape[1]
    return (
        matrix.reshape(seq_count, length, channels)
        .transpose(1, 0, 2)
        .reshape(length, seq_count * channels)
    )


def from_columns(matrix, seq_count, length):
    channels = matrix.shape[1] // seq_count
    return (
        matrix.reshape(length, seq_count, channels)
        .transpose(1, 0, 2)
        .reshape(seq_count * length, channels)
    )


def outer_sum(left, right):
    return lax.dot_general(
        left, right, (((0,), (0,)), ((), ())), preferred_element_type=jnp.float32
    )


def times_transpose(left, right):
    return lax.dot_general(
        left, right, (((1,), (1,)), ((), ())), preferred_element_type=jnp.float32
    )


def local(
    tokens,
    lengths,
    cotangent,
    gain_attn,
    w_query,
    w_key,
    w_value,
    w_out,
    gain_mlp,
    w_up,
    w_down,
    pos_bias,
):
    gathered = (
        lax.all_gather(gain_attn, "dp", axis=0, tiled=True),
        lax.all_gather(w_query, "dp", axis=0, tiled=True),
        lax.all_gather(w_key, "dp", axis=0, tiled=True),
        lax.all_gather(w_value, "dp", axis=0, tiled=True),
        lax.all_gather(w_out, "dp", axis=0, tiled=True),
        lax.all_gather(gain_mlp, "dp", axis=0, tiled=True),
        lax.all_gather(w_up, "dp", axis=0, tiled=True),
        lax.all_gather(w_down, "dp", axis=0, tiled=True),
        lax.all_gather(pos_bias, "dp", axis=0, tiled=True),
    )
    gain_a = gathered[0].astype(jnp.float32)
    query_w, key_w, value_w, out_w = (gathered[1], gathered[2], gathered[3], gathered[4])
    gain_m = gathered[5].astype(jnp.float32)
    up_w, down_w = (gathered[6], gathered[7])
    bias_full = gathered[8].astype(jnp.float32)
    group_size = lax.axis_size("dp")
    tok_rows = tokens.shape[2]
    seq_count = group_size * tok_rows // SEQ
    band_mask = band_ones(WIN)
    bias_blocks = jnp.exp(band_blocks(bias_full, WIN))
    exp_band = bias_blocks * band_mask
    kernel = ((bias_blocks - 1.0) * band_mask).astype(jnp.bfloat16)
    positions = jnp.arange(SEQ)
    grad_gain_a = jnp.zeros((D,), jnp.float32)
    grad_gain_m = jnp.zeros((D,), jnp.float32)
    grad_query_w = jnp.zeros((D, D), jnp.float32)
    grad_key_w = jnp.zeros((D, D), jnp.float32)
    grad_value_w = jnp.zeros((D, D), jnp.float32)
    grad_out_w = jnp.zeros((D, D), jnp.float32)
    grad_up_w = jnp.zeros((D, FF), jnp.float32)
    grad_down_w = jnp.zeros((FF, D), jnp.float32)
    grad_kernel = jnp.zeros(exp_band.shape, jnp.float32)
    outputs_list = []
    grads_in_list = []
    for micro in range(tokens.shape[0]):
        inputs_f = tokens[micro, 0].astype(jnp.float32)
        normed_f, norm_back_a = jax.vjp(normalize, inputs_f, gain_a)
        normed = normed_f.astype(jnp.bfloat16)
        query = jnp.dot(normed, query_w, preferred_element_type=jnp.float32)
        keys = jnp.dot(normed, key_w, preferred_element_type=jnp.float32).astype(jnp.bfloat16)
        values = jnp.dot(normed, value_w, preferred_element_type=jnp.float32).astype(jnp.bfloat16)
        key_chan, value_chan = (
            lax.all_to_all(keys, "dp", split_axis=1, concat_axis=0, tiled=True),
            lax.all_to_all(values, "dp", split_axis=1, concat_axis=0, tiled=True),
        )
        seq_lengths = lengths[micro, 0]
        channels = key_chan.shape[1]
        valid_seq = (positions[:, None] < seq_lengths[None, :]).astype(jnp.float32)
        valid_cols = jnp.broadcast_to(valid_seq[:, :, None], (SEQ, seq_count, channels)).reshape(
            SEQ, seq_count * channels
        )
        key_cols = to_columns(key_chan, seq_count, SEQ).astype(jnp.float32)
        value_cols = to_columns(value_chan, seq_count, SEQ).astype(jnp.float32)
        weighted = jnp.exp(key_cols) * valid_cols
        col_count = weighted.shape[1]
        operand = jnp.concatenate(
            [(weighted * value_cols).astype(jnp.bfloat16), weighted.astype(jnp.bfloat16)], axis=1
        )
        windowed = windows(operand, WIN)
        banded = jnp.einsum(
            "nqk,nkc->nqc", kernel, windowed, preferred_element_type=jnp.float32
        ).reshape(SEQ, 2 * col_count)
        result = banded + jnp.sum(operand, axis=0, dtype=jnp.float32)[None, :]
        numerator = result[:, :col_count]
        denominator = result[:, col_count:] + 1.0 - valid_cols
        mixed_cols = numerator / denominator * valid_cols
        mixed_tok = lax.all_to_all(
            from_columns(mixed_cols.astype(jnp.bfloat16), seq_count, SEQ),
            "dp",
            split_axis=0,
            concat_axis=1,
            tiled=True,
        )
        sigmoid_q = jax.nn.sigmoid(query)
        mixed_f = mixed_tok.astype(jnp.float32)
        gated = (sigmoid_q * mixed_f).astype(jnp.bfloat16)
        resid = inputs_f + jnp.dot(gated, out_w, preferred_element_type=jnp.float32)
        normed_two_f, norm_back_m = jax.vjp(normalize, resid, gain_m)
        normed_two = normed_two_f.astype(jnp.bfloat16)
        upper = jnp.dot(normed_two, up_w, preferred_element_type=jnp.float32)
        hidden_f, gelu_back = jax.vjp(gelu_tanh, upper)
        hidden = hidden_f.astype(jnp.bfloat16)
        outputs_list.append(
            (resid + jnp.dot(hidden, down_w, preferred_element_type=jnp.float32)).astype(
                jnp.bfloat16
            )
        )
        grad_out = cotangent[micro, 0]
        grad_down_w = grad_down_w + outer_sum(hidden, grad_out)
        grad_hidden = times_transpose(grad_out, down_w)
        grad_upper = gelu_back(grad_hidden)[0].astype(jnp.bfloat16)
        grad_up_w = grad_up_w + outer_sum(normed_two, grad_upper)
        grad_normed_two = times_transpose(grad_upper, up_w)
        grad_resid_norm, grad_gain_part_m = norm_back_m(grad_normed_two)
        grad_gain_m = grad_gain_m + grad_gain_part_m
        grad_resid = grad_out.astype(jnp.float32) + grad_resid_norm
        grad_attn = grad_resid.astype(jnp.bfloat16)
        grad_out_w = grad_out_w + outer_sum(gated, grad_attn)
        grad_gated = times_transpose(grad_attn, out_w)
        grad_mixed = (grad_gated * sigmoid_q).astype(jnp.bfloat16)
        grad_query = (grad_gated * mixed_f * sigmoid_q * (1.0 - sigmoid_q)).astype(jnp.bfloat16)
        grad_mixed_chan = lax.all_to_all(grad_mixed, "dp", split_axis=1, concat_axis=0, tiled=True)
        grad_mixed_cols = to_columns(grad_mixed_chan, seq_count, SEQ).astype(jnp.float32)
        grad_numerator = grad_mixed_cols * valid_cols / denominator
        grad_denominator = -grad_numerator * (numerator / denominator)
        grad_flat = jnp.concatenate(
            [grad_numerator.astype(jnp.bfloat16), grad_denominator.astype(jnp.bfloat16)], axis=1
        )
        grad_result = grad_flat.reshape(SEQ // WIN, WIN, 2 * col_count)
        grad_windowed = jnp.einsum(
            "nqk,nqc->nkc", kernel, grad_result, preferred_element_type=jnp.float32
        )
        grad_kernel = grad_kernel + jnp.einsum(
            "nqc,nkc->nqk", grad_result, windowed, preferred_element_type=jnp.float32
        )
        grad_operand = (
            unwindow(grad_windowed, WIN) + jnp.sum(grad_flat, axis=0, dtype=jnp.float32)[None, :]
        )
        grad_key_value = grad_operand[:, :col_count]
        grad_key_weight = grad_operand[:, col_count:]
        grad_keys_cols = (grad_key_value * value_cols + grad_key_weight) * weighted
        grad_values_cols = grad_key_value * weighted
        grad_keys, grad_values = (
            lax.all_to_all(
                from_columns(grad_keys_cols.astype(jnp.bfloat16), seq_count, SEQ),
                "dp",
                split_axis=0,
                concat_axis=1,
                tiled=True,
            ),
            lax.all_to_all(
                from_columns(grad_values_cols.astype(jnp.bfloat16), seq_count, SEQ),
                "dp",
                split_axis=0,
                concat_axis=1,
                tiled=True,
            ),
        )
        grad_query_w = grad_query_w + outer_sum(normed, grad_query)
        grad_key_w = grad_key_w + outer_sum(normed, grad_keys)
        grad_value_w = grad_value_w + outer_sum(normed, grad_values)
        grad_normed = (
            times_transpose(grad_query, query_w)
            + times_transpose(grad_keys, key_w)
            + times_transpose(grad_values, value_w)
        )
        grad_input_norm, grad_gain_part_a = norm_back_a(grad_normed)
        grad_gain_a = grad_gain_a + grad_gain_part_a
        grads_in_list.append((grad_resid + grad_input_norm).astype(jnp.bfloat16))
    grad_kernel_bias = grad_kernel * exp_band
    grad_bias_pad = jnp.zeros((SEQ, SEQ + 2 * WIN), jnp.float32)
    for block in range(SEQ // WIN):
        grad_bias_pad = grad_bias_pad.at[
            block * WIN : (block + 1) * WIN, block * WIN : block * WIN + 3 * WIN
        ].add(grad_kernel_bias[block])
    grad_bias = grad_bias_pad[:, WIN : WIN + SEQ]
    shares = (
        lax.psum_scatter(grad_gain_a, "dp", scatter_dimension=0, tiled=True),
        lax.psum_scatter(grad_query_w, "dp", scatter_dimension=0, tiled=True),
        lax.psum_scatter(grad_key_w, "dp", scatter_dimension=0, tiled=True),
        lax.psum_scatter(grad_value_w, "dp", scatter_dimension=0, tiled=True),
        lax.psum_scatter(grad_out_w, "dp", scatter_dimension=0, tiled=True),
        lax.psum_scatter(grad_gain_m, "dp", scatter_dimension=0, tiled=True),
        lax.psum_scatter(grad_up_w, "dp", scatter_dimension=0, tiled=True),
        lax.psum_scatter(grad_down_w, "dp", scatter_dimension=0, tiled=True),
        lax.psum_scatter(grad_bias, "dp", scatter_dimension=0, tiled=True),
    )
    reduced = lax.psum(
        (
            shares[0],
            shares[1],
            shares[2],
            shares[3],
            shares[4],
            shares[5],
            shares[6],
            shares[7],
            shares[8],
        ),
        "pipe",
    )
    final_grads = (
        reduced[0],
        reduced[1],
        reduced[2],
        reduced[3],
        reduced[4],
        reduced[5],
        reduced[6],
        reduced[7],
        reduced[8],
    )
    output = jnp.stack(outputs_list)[:, None]
    grad_tokens = jnp.stack(grads_in_list)[:, None]
    return (
        output,
        grad_tokens,
        final_grads[0],
        final_grads[1],
        final_grads[2],
        final_grads[3],
        final_grads[4],
        final_grads[5],
        final_grads[6],
        final_grads[7],
        final_grads[8],
    )


CHIPS = 4
CORES = 2
DEPTH = 4
LANES = 128
TOK = 128
BLK = CORES * TOK
ROWS = D // (CHIPS * CORES)
SL = D // CHIPS
SLP = -(-SL // LANES) * LANES
FS = FF // CHIPS
BAND = 5 * LANES
HALF = D // 2
MESH_ID = pl.DeviceIdType.MESH
F32 = jnp.float32
BF = jnp.bfloat16

SCRATCH = (
    ("tok", (BLK, D), BF),
    ("cot", (SEQ, D), BF),
    ("gains", (CHIPS * CORES, 16, LANES), BF),
    ("gain", (16, D), F32),
    ("wst", (3, ROWS, D), BF),
    ("wqs", (CHIPS, ROWS, 3 * SLP), BF),
    ("wqkv", (D, 3 * SLP), BF),
    ("wout", (CHIPS * SLP, D), BF),
    ("wup", (D, FS), BF),
    ("wdn", (FS, D), BF),
    ("pbw", (TOK, BAND), BF),
    ("kern", (CHIPS * CORES, TOK, BAND), BF),
    ("h1", (SEQ, D), BF),
    ("h2", (SEQ, D), BF),
    ("n1", (BLK, D), F32),
    ("r1", (BLK, LANES), F32),
    ("n2", (BLK, D), F32),
    ("r2", (BLK, LANES), F32),
    ("tmp", (HALF, D), F32),
    ("tmix", (TOK, 2 * SLP), F32),
    ("sums", (8, 2 * SLP), F32),
    ("sig", (SEQ, SLP), F32),
    ("wgt", (SEQ, SLP), F32),
    ("val", (SEQ, SLP), BF),
    ("op", (SEQ, 2 * SLP), BF),
    ("ratio", (SEQ, SLP), F32),
    ("rden", (SEQ, SLP), F32),
    ("mixed", (SEQ, SLP), BF),
    ("gated", (SEQ, SLP), BF),
    ("grecv", (CHIPS, BLK, SLP), BF),
    ("resid", (BLK, D), F32),
    ("hid", (SEQ, FS), BF),
    ("dge", (SEQ, FS), F32),
    ("gupr", (SEQ, FS), BF),
    ("pout", (CHIPS - 1, BLK, D), BF),
    ("pgh", (CHIPS - 1, BLK, D), BF),
    ("own", (BLK, D), F32),
    ("rbout", (6, TOK, D), BF),
    ("rbg2", (6, TOK, D), BF),
    ("rbg1", (6, TOK, D), BF),
    ("gresid", (BLK, D), F32),
    ("gattn", (BLK, D), BF),
    ("ggs", (CHIPS - 1, BLK, SLP), BF),
    ("ggr", (CHIPS, BLK, SLP), BF),
    ("gdo", (CHIPS, ROWS, D), F32),
    ("gds", (CHIPS, ROWS, D), BF),
    ("gdr", (CHIPS, ROWS, D), BF),
    ("guo", (CHIPS, ROWS, FS), F32),
    ("gus", (CHIPS, ROWS, FS), BF),
    ("gur", (CHIPS, ROWS, FS), BF),
    ("gqo", (CHIPS, ROWS, 3 * SLP), F32),
    ("gqs", (CHIPS, ROWS, 3 * SLP), BF),
    ("gqr", (CHIPS, ROWS, 3 * SLP), BF),
    ("goo", (CHIPS, ROWS, D), F32),
    ("gos", (CHIPS, ROWS, D), BF),
    ("gor", (CHIPS, ROWS, D), BF),
    ("po", (CHIPS - 1, ROWS, D), BF),
    ("rbo", (6, ROWS // 2, D), BF),
    ("gko", (CHIPS, TOK, BAND), F32),
    ("gks", (CHIPS, TOK, BAND), BF),
    ("gkr", (CHIPS, TOK, BAND), BF),
    ("pk", (CHIPS - 1, TOK, BAND), BF),
    ("rbk", (6, TOK // 2, BAND), BF),
    ("zb", (13, ROWS, D), BF),
    ("zr", (13, ROWS, D), BF),
    ("zt", (13, ROWS, D), BF),
    ("zkb", (TOK, BAND), BF),
    ("zkr", (TOK, BAND), BF),
    ("zkt", (TOK, BAND), BF),
    ("fout", (BLK, D), BF),
    ("fgt", (BLK, D), BF),
    ("gpb", (TOK, SEQ), F32),
)
N_REMOTE = 200
N_LOCAL = 24


def dot(left, right, left_dim, right_dim):
    return lax.dot_general(
        left, right, (((left_dim,), (right_dim,)), ((), ())), preferred_element_type=F32
    )


def rows_loop(count, step, body, unroll=1):
    def one(i, carry):
        body(pl.multiple_of(i * step, step))
        return carry

    lax.fori_loop(0, count // step, one, 0, unroll=unroll)


def plane_kernel(
    tok_in, len_in, cot_in, gains_in, wq_in, wk_in, wv_in, wout_in, wup_in, wdn_in, pb_in,
    out_out, gtok_out, gqkv_out, gwout_out, gup_out, gdn_out, gpb_out,
    *scratch,
):
    m = types.SimpleNamespace(**{entry[0]: ref for entry, ref in zip(SCRATCH, scratch)})
    send_sem, recv_sem, local_sem = scratch[len(SCRATCH):]
    r = lax.axis_index("dp")
    z = lax.axis_index("pipe")
    c = lax.rem(r, 2)
    x = lax.rem(r // 2, 2)
    y = r // 4
    b = r // 2
    length = len_in[c]

    def chip(k):
        return 2 * (1 - y if k // 2 else y) + (1 - x if k % 2 else x)

    def peer(k, other=0):
        return (2 * chip(k) + (1 - c if other else c), z)

    jx, jy, jd = chip(1), chip(2), chip(3)
    SIB, PX, PY, PD = peer(0, 1), peer(1), peer(2), peer(3)
    z_near = z + 1 - 2 * lax.rem(z, 2)
    z_far = 3 - z
    ZN, ZF = (r, z_near), (r, z_far)
    outer = z * (3 - z) == 0
    inner = z * (3 - z) != 0

    remote, locals_ = {}, []
    waited = set()

    def make(name, src, dst, to):
        assert name not in remote, name
        i = len(remote)
        cp = pltpu.make_async_remote_copy(
            src_ref=src, dst_ref=dst, send_sem=send_sem.at[i], recv_sem=recv_sem.at[i],
            device_id=to, device_id_type=MESH_ID,
        )
        remote[name] = cp
        return cp

    def send(name, src, dst, to):
        make(name, src, dst, to).start()

    def got(*names):
        for name in names:
            if name not in waited:
                waited.add(name)
                remote[name].wait_recv()

    def sent(*names):
        for name in names:
            if name + "/s" not in waited:
                waited.add(name + "/s")
                remote[name].wait_send()

    def local_copy(src, dst):
        cp = pltpu.make_async_copy(src, dst, local_sem.at[len(locals_)])
        locals_.append(cp)
        cp.start()
        return cp

    def ds(start, size, unit):
        return pl.ds(pl.multiple_of(start, unit), size)

    def band_at(d):
        return pl.multiple_of(jnp.minimum(jnp.maximum(d - 2, 0), 3) * LANES, LANES)

    def gather_start(name, blk):
        send(name + "X0", blk(b, 0), blk(b, 0), PX)
        send(name + "Y1", blk(b, 1), blk(b, 1), PY)
        send(name + "X1", blk(b, 1), blk(b, 1), PX)
        send(name + "Y0", blk(b, 0), blk(b, 0), PY)

    def gather_forward(name, blk):
        got(name + "X0")
        send(name + "F0", blk(jx, 0), blk(jx, 0), PY)
        got(name + "Y1")
        send(name + "F1", blk(jy, 1), blk(jy, 1), PX)

    def gather_wait(name, k):
        got(*{1: (name + "X0", name + "X1"), 2: (name + "Y0", name + "Y1"), 3: (name + "F0", name + "F1")}[k])

    def scatter_diagonal(name, part, buf, half):
        send(name + "0", part.at[2, pl.ds(half, half)], buf.at[0], PX)
        send(name + "1", part.at[2, pl.ds(0, half)], buf.at[1], PY)

    def scatter_direct_x(name, part, buf, half):
        send(name + "2", part.at[0, pl.ds(half, half)], buf.at[2], PX)

    def scatter_direct_y(name, part, buf, half):
        send(name + "3", part.at[1, pl.ds(0, half)], buf.at[3], PY)

    def scatter_combine(name, part, buf, half):
        got(name + "1")
        part[0, pl.ds(0, half), :] = (
            part[0, pl.ds(0, half), :].astype(F32) + buf[1].astype(F32)
        ).astype(BF)
        send(name + "4", part.at[0, pl.ds(0, half)], buf.at[4], PX)
        got(name + "0")
        part[1, pl.ds(half, half), :] = (
            part[1, pl.ds(half, half), :].astype(F32) + buf[0].astype(F32)
        ).astype(BF)
        send(name + "5", part.at[1, pl.ds(half, half)], buf.at[5], PY)

    def scatter_wait(name):
        got(name + "2", name + "3", name + "4", name + "5")

    def scatter_sum(buf, half, h, rows):
        if h == 0:
            return buf[3, rows, :].astype(F32) + buf[4, rows, :].astype(F32)
        return buf[2, rows, :].astype(F32) + buf[5, rows, :].astype(F32)

    zitems = {}

    def z_open(name, base, near, total):
        zitems[name] = (
            base,
            near,
            total,
            make(name + "a", base, near, ZN),
            make(name + "b", base, total, ZF),
            make(name + "c", total, total, ZN),
        )

    def z_start(name):
        item = zitems[name]

        @pl.when(outer)
        def _():
            item[3].start()

    def z_mid(name):
        base, near, total, into, across, back = zitems[name]

        @pl.when(inner)
        def _():
            into.wait_recv()
            base[...] = (base[...].astype(F32) + near[...].astype(F32)).astype(BF)
            across.start()

    def z_end(name):
        base, near, total, into, across, back = zitems[name]

        @pl.when(inner)
        def _():
            across.wait_recv()
            total[...] = (base[...].astype(F32) + total[...].astype(F32)).astype(BF)
            back.start()

        @pl.when(outer)
        def _():
            back.wait_recv()

    def z_close(name):
        base, near, total, into, across, back = zitems[name]

        @pl.when(outer)
        def _():
            into.wait_send()

        @pl.when(inner)
        def _():
            across.wait_send()
            back.wait_send()

    for i in range(13):
        z_open(f"z{i}", m.zb.at[i], m.zr.at[i], m.zt.at[i])
    z_open("zk", m.zkb, m.zkr, m.zkt)

    own_half = ds(c * TOK, TOK, TOK)
    l_gain = local_copy(gains_in, m.gains.at[r])
    l_w = [local_copy(w, m.wst.at[i]) for i, w in enumerate((wq_in, wk_in, wv_in))]
    l_tok = local_copy(tok_in.at[c], m.tok.at[own_half])
    l_pb = local_copy(pb_in.at[:, ds(band_at(r), BAND, LANES)], m.pbw)

    def wout_rows(j, core):
        return m.wout.at[ds(j * SLP + core * ROWS, ROWS, 32)]

    l_wout = local_copy(wout_in, wout_rows(b, c))
    up_rows = ds(r * ROWS, ROWS, 32)
    l_wup = local_copy(wup_in.at[:, ds(b * FS, FS, LANES)], m.wup.at[up_rows])
    dn_rows = ds(c * HALF, HALF, LANES)
    l_wdn = local_copy(wdn_in, m.wdn.at[dn_rows])
    cot_half = ds(b * BLK + c * TOK, TOK, TOK)
    l_cot = local_copy(cot_in.at[c], m.cot.at[cot_half])

    barrier = pltpu.get_barrier_semaphore()
    everyone = [peer(k, o) for k in range(CHIPS) for o in range(CORES) if (k, o) != (0, 0)] + [ZN, ZF]
    for other in everyone:
        pl.semaphore_signal(barrier, inc=1, device_id=other, device_id_type=MESH_ID)
    pl.semaphore_wait(barrier, len(everyone))

    send("tokS", tok_in.at[1 - c], m.tok.at[own_half], SIB)
    gain_names = []
    for k in range(CHIPS):
        for o in range(CORES):
            if (k, o) != (0, 0):
                gain_names.append(f"gain{k}{o}")
                send(gain_names[-1], gains_in, m.gains.at[r], peer(k, o))
    for cp in l_w:
        cp.wait()
    for i in range(3):
        w_rows = m.wst[i].astype(F32)
        for j in range(CHIPS):
            piece = w_rows[:, j * SL : (j + 1) * SL]
            m.wqs[j, :, i * SLP : (i + 1) * SLP] = jnp.concatenate(
                [piece, jnp.zeros((ROWS, SLP - SL), F32)], axis=1
            ).astype(BF)
    for k, to in ((1, PX), (2, PY), (3, PD)):
        send(f"wq{k}", m.wqs.at[chip(k)], m.wqkv.at[up_rows], to)
    send("wqS0", m.wqs.at[b], m.wqkv.at[up_rows], SIB)
    m.wqkv[up_rows, :] = m.wqs[b]

    l_gain.wait()
    got(*gain_names)
    m.gain[...] = jnp.concatenate(
        [m.gains[d].astype(F32)[:, :ROWS] for d in range(CHIPS * CORES)], axis=1
    )

    def norm(src, gain_row, n_ref, r_ref, dst, base):
        def body(i):
            rows = pl.ds(i, 32)
            values = src[rows, :].astype(F32)
            centre = values - jnp.mean(values, axis=-1, keepdims=True)
            spread = jnp.mean(centre * centre, axis=-1, keepdims=True)
            rinv = lax.rsqrt(spread + EPSILON)
            n = centre * rinv
            n_ref[rows, :] = n
            r_ref[rows, :] = jnp.broadcast_to(rinv, (32, LANES))
            dst[pl.ds(pl.multiple_of(base + i, 32), 32), :] = (
                n * m.gain[gain_row : gain_row + 1, :]
            ).astype(BF)

        rows_loop(BLK, 32, body)

    l_tok.wait()
    got("tokS")
    norm(m.tok, 0, m.n1, m.r1, m.h1, b * BLK)

    def h1_blk(j, h):
        return m.h1.at[ds(j * BLK + h * TOK, TOK, TOK)]

    gather_start("h1", h1_blk)

    l_pb.wait()
    t_ids = r * TOK + lax.broadcasted_iota(jnp.int32, (TOK, BAND), 0)
    u_ids = band_at(r) + lax.broadcasted_iota(jnp.int32, (TOK, BAND), 1)
    in_band = jnp.abs(t_ids - u_ids) < WIN
    m.kern[r] = jnp.where(in_band, jnp.exp(m.pbw[...].astype(F32)) - 1.0, 0.0).astype(BF)

    def kern_blk(j, h):
        return m.kern.at[2 * j + c, pl.ds(h * (TOK // 2), TOK // 2)]

    gather_start("kn", kern_blk)
    send("knS0", m.kern.at[r], m.kern.at[r], SIB)

    for k in (1, 2, 3):
        got(f"wq{k}")
        rows = ds((2 * chip(k) + c) * ROWS, ROWS, 32)
        send(f"wqS{k}", m.wqkv.at[rows], m.wqkv.at[rows], SIB)
    got("wqS0", "wqS1", "wqS2", "wqS3")
    for j in range(CHIPS):
        m.wout[j * SLP + SL : (j + 1) * SLP, :] = jnp.zeros((SLP - SL, D), BF)

    def blk_rows(j):
        return ds(j * BLK, BLK, BLK)

    def project(j):
        m.tmp[0:BLK, :] = dot(m.h1[blk_rows(j), :], m.wqkv[...], 1, 0)

        def body(i):
            rows = pl.ds(i, 16)
            at = pl.multiple_of(j * BLK + i, 16)
            to = pl.ds(at, 16)
            q = m.tmp[rows, 0:SLP]
            m.sig[to, :] = 1.0 / (1.0 + jnp.exp(-q))
            keys = m.tmp[rows, SLP : 2 * SLP].astype(BF).astype(F32)
            values = m.tmp[rows, 2 * SLP : 3 * SLP].astype(BF)
            pos = at + lax.broadcasted_iota(jnp.int32, (16, SLP), 0)
            weighted = jnp.where(pos < length, jnp.exp(keys), 0.0)
            m.wgt[to, :] = weighted
            m.val[to, :] = values
            m.op[to, 0:SLP] = (weighted * values.astype(F32)).astype(BF)
            m.op[to, SLP : 2 * SLP] = weighted.astype(BF)

        rows_loop(BLK, 16, body, unroll=2)

    project(b)
    gather_forward("h1", h1_blk)
    gather_forward("kn", kern_blk)

    l_wout.wait()

    def wout_blk(j, h):
        return m.wout.at[ds(j * SLP + c * ROWS + h * (ROWS // 2), ROWS // 2, 16)]

    gather_start("wo", wout_blk)
    send("woS0", wout_rows(b, c), wout_rows(b, c), SIB)
    for k, to in ((1, PX), (2, PY), (3, PD)):
        send(f"wu{k}", wup_in.at[:, ds(chip(k) * FS, FS, LANES)], m.wup.at[up_rows], to)
    l_wup.wait()
    send("wuS0", m.wup.at[up_rows], m.wup.at[up_rows], SIB)
    l_wdn.wait()
    send("wdS", m.wdn.at[dn_rows], m.wdn.at[dn_rows], SIB)
    send("cotS", cot_in.at[1 - c], m.cot.at[cot_half], SIB)

    for k in (1, 2):
        gather_wait("h1", k)
        project(chip(k))
    for k in (1, 2, 3):
        gather_wait("kn", k)
        d = 2 * chip(k) + c
        send(f"knS{k}", m.kern.at[d], m.kern.at[d], SIB)
    gather_wait("h1", 3)
    project(jd)
    gather_forward("wo", wout_blk)

    got("knS0", "knS1", "knS2", "knS3")
    ones = jnp.ones((8, SEQ), BF)
    m.sums[...] = dot(ones, m.op[...], 1, 0)

    def mix(d):
        m.tmix[...] = dot(m.kern[d], m.op[pl.ds(band_at(d), BAND), :], 1, 0)

        def body(i):
            rows = pl.ds(i, 32)
            at = pl.multiple_of(d * TOK + i, 32)
            to = pl.ds(at, 32)
            pos = at + lax.broadcasted_iota(jnp.int32, (32, SLP), 0)
            valid = jnp.where(pos < length, 1.0, 0.0)
            num = m.tmix[rows, 0:SLP] + m.sums[0:1, 0:SLP]
            den = m.tmix[rows, SLP : 2 * SLP] + m.sums[0:1, SLP : 2 * SLP] + 1.0 - valid
            rden = 1.0 / den
            ratio = num * rden
            mixed = (ratio * valid).astype(BF)
            m.ratio[to, :] = ratio
            m.rden[to, :] = rden * valid
            m.mixed[to, :] = mixed
            m.gated[to, :] = (m.sig[to, :] * mixed.astype(F32)).astype(BF)

        rows_loop(TOK, 32, body, unroll=2)

    def mix_block(j):
        def one(i, carry):
            mix(2 * j + i)
            return carry

        lax.fori_loop(0, CORES, one, 0)

    for k, to in ((3, PD), (1, PX), (2, PY)):
        j = chip(k)
        mix_block(j)
        send(f"ga{k}", m.gated.at[blk_rows(j)], m.grecv.at[k], to)
    mix_block(b)
    m.grecv[0] = m.gated[blk_rows(b), :]

    for k in (1, 2, 3):
        gather_wait("wo", k)
        send(f"woS{k}", wout_rows(chip(k), c), wout_rows(chip(k), c), SIB)
    for k in (1, 2, 3):
        got(f"wu{k}")
        rows = ds((2 * chip(k) + c) * ROWS, ROWS, 32)
        send(f"wuS{k}", m.wup.at[rows], m.wup.at[rows], SIB)
    l_cot.wait()
    got("cotS")

    def cot_blk(j, h):
        return m.cot.at[ds(j * BLK + h * TOK, TOK, TOK)]

    gather_start("ct", cot_blk)

    got("woS0", "woS1", "woS2", "woS3")
    m.resid[...] = m.tok[...].astype(F32)
    for k in (0, 1, 2, 3):
        if k:
            got(f"ga{k}")
        m.resid[...] += dot(m.grecv[k], m.wout[ds(chip(k) * SLP, SLP, SLP), :], 1, 0)
    norm(m.resid, 1, m.n2, m.r2, m.h2, b * BLK)

    def h2_blk(j, h):
        return m.h2.at[ds(j * BLK + h * TOK, TOK, TOK)]

    gather_start("h2", h2_blk)

    got("wuS0", "wuS1", "wuS2", "wuS3", "wdS")

    def ff_forward(k):
        j = chip(k)
        m.tmp[0:BLK, :] = dot(m.h2[blk_rows(j), :], m.wup[...], 1, 0)

        def body(i):
            v = m.tmp[pl.ds(i, 16), :]
            to = pl.ds(pl.multiple_of(j * BLK + i, 16), 16)
            cube = v * v
            t = jnp.tanh(GELU_SCALE * v * (1.0 + GELU_CUBE * cube))
            half = 0.5 * (1.0 + t)
            m.hid[to, :] = (v * half).astype(BF)
            m.dge[to, :] = half + 0.5 * v * (1.0 - t * t) * (
                GELU_SCALE * (1.0 + 3.0 * GELU_CUBE * cube)
            )

        rows_loop(BLK, 16, body, unroll=2)
        part = dot(m.hid[blk_rows(j), :], m.wdn[...], 1, 0)
        if k == 0:
            m.resid[...] += part
        else:
            m.pout[k - 1] = part.astype(BF)

    ff_forward(0)
    gather_forward("h2", h2_blk)
    gather_forward("ct", cot_blk)
    for k in (1, 2, 3):
        gather_wait("h2", k)
        ff_forward(k)

    def ff_backward(k):
        j = chip(k)
        m.tmp[0:BLK, :] = dot(m.cot[blk_rows(j), :], m.wdn[...], 1, 1)

        def body(i):
            to = pl.ds(pl.multiple_of(j * BLK + i, 16), 16)
            m.gupr[to, :] = (m.tmp[pl.ds(i, 16), :] * m.dge[to, :]).astype(BF)

        rows_loop(BLK, 16, body, unroll=2)
        part = dot(m.gupr[blk_rows(j), :], m.wup[...], 1, 1)
        if k == 0:
            m.own[...] = part
        else:
            m.pgh[k - 1] = part.astype(BF)

    gather_wait("ct", 3)
    ff_backward(3)
    scatter_diagonal("g2", m.pgh, m.rbg2, TOK)
    gather_wait("ct", 1)
    ff_backward(1)
    scatter_direct_x("g2", m.pgh, m.rbg2, TOK)
    gather_wait("ct", 2)
    ff_backward(2)
    scatter_direct_y("g2", m.pgh, m.rbg2, TOK)
    scatter_combine("g2", m.pgh, m.rbg2, TOK)
    ff_backward(0)
    scatter_diagonal("ou", m.pout, m.rbout, TOK)
    scatter_direct_x("ou", m.pout, m.rbout, TOK)
    scatter_direct_y("ou", m.pout, m.rbout, TOK)

    other_cols = ds((1 - c) * HALF, HALF, LANES)
    own_cols = ds(c * HALF, HALF, LANES)
    m.tmp[...] = dot(m.hid[:, other_cols], m.cot[...], 0, 0)
    for j in range(CHIPS):
        m.gds[j] = m.tmp[j * ROWS : (j + 1) * ROWS, :].astype(BF)
    send("gdS", m.gds, m.gdr, SIB)
    scatter_combine("ou", m.pout, m.rbout, TOK)
    m.tmp[...] = dot(m.hid[:, own_cols], m.cot[...], 0, 0)
    for j in range(CHIPS):
        m.gdo[j] = m.tmp[j * ROWS : (j + 1) * ROWS, :]

    def split_rows(left, right, kept, leaving):
        for i in range(2):
            m.tmp[...] = dot(left[:, i * HALF : (i + 1) * HALF], right[...], 0, 0)
            for q in range(2):
                kept[2 * i + q] = m.tmp[ds((2 * q + c) * ROWS, ROWS, 32), :]
                leaving[2 * i + q] = m.tmp[ds((2 * q + 1 - c) * ROWS, ROWS, 32), :].astype(BF)

    split_rows(m.h2, m.gupr, m.guo, m.gus)
    send("guS", m.gus, m.gur, SIB)

    def pair_sum(kept, came, first):
        for j in range(CHIPS):
            m.zb[first + j] = (kept[j] + came[j].astype(F32)).astype(BF)
            z_start(f"z{first + j}")

    got("gdS")
    pair_sum(m.gdo, m.gdr, 0)

    scatter_wait("g2")

    def norm_back(total, gain_row, n_ref, r_ref, i, half, base):
        rows = pl.ds(i, 32)
        e = total * m.gain[gain_row : gain_row + 1, :]
        n = n_ref[rows, :]
        mean_e = jnp.mean(e, axis=-1, keepdims=True)
        mean_en = jnp.mean(e * n, axis=-1, keepdims=True)
        return base + r_ref[rows, 0:1] * (e - mean_e - n * mean_en)

    for h in range(2):

        def back_two(i, h=h):
            at = pl.multiple_of(h * TOK + i, 32)
            rows = pl.ds(at, 32)
            total = m.own[rows, :] + scatter_sum(m.rbg2, TOK, h, pl.ds(i, 32))
            base = m.cot[pl.ds(pl.multiple_of(b * BLK + at, 32), 32), :].astype(F32)
            g = norm_back(total, 1, m.n2, m.r2, at, TOK, base)
            m.gresid[rows, :] = g
            m.gattn[rows, :] = g.astype(BF)

        rows_loop(TOK, 32, back_two)

    for k, to in ((3, PD), (1, PX), (2, PY)):
        m.ggs[k - 1] = dot(m.gattn[...], m.wout[ds(chip(k) * SLP, SLP, SLP), :], 1, 1).astype(BF)
        send(f"gg{k}", m.ggs.at[k - 1], m.ggr.at[k], to)
    m.ggr[0] = dot(m.gattn[...], m.wout[ds(b * SLP, SLP, SLP), :], 1, 1).astype(BF)
    got("guS")
    pair_sum(m.guo, m.gur, 4)
    for k in range(CHIPS):
        m.tmp[0:SLP, :] = dot(m.grecv[k], m.gattn[...], 0, 0)
        m.goo[k] = m.tmp[ds(c * ROWS, ROWS, 32), :]
        m.gos[k] = m.tmp[ds((1 - c) * ROWS, ROWS, 32), :].astype(BF)
    send("goS", m.gos, m.gor, SIB)

    scatter_wait("ou")
    for h in range(2):

        def out_rows(i, h=h):
            rows = pl.ds(pl.multiple_of(h * TOK + i, 32), 32)
            m.fout[rows, :] = (
                m.resid[rows, :] + scatter_sum(m.rbout, TOK, h, pl.ds(i, 32))
            ).astype(BF)

        rows_loop(TOK, 32, out_rows)
    other_half = ds((1 - c) * TOK, TOK, TOK)
    send("outS", m.fout.at[other_half], out_out.at[c], SIB)
    local_copy(m.fout.at[own_half], out_out.at[c])

    got("goS")
    for k in (1, 2, 3):
        m.po[k - 1] = (m.goo[k] + m.gor[k].astype(F32)).astype(BF)
    scatter_diagonal("wo_s", m.po, m.rbo, ROWS // 2)
    scatter_direct_x("wo_s", m.po, m.rbo, ROWS // 2)
    scatter_direct_y("wo_s", m.po, m.rbo, ROWS // 2)
    for i in range(4):
        z_mid(f"z{i}")

    gqkv = m.hid
    gres = m.h2
    gop = m.dge
    sent("h2X0", "h2X1", "h2Y0", "h2Y1", "h2F0", "h2F1")

    def mix_back(k):
        j = chip(k)

        def body(i):
            at = pl.multiple_of(j * BLK + i, 16)
            rows = pl.ds(at, 16)
            gg = m.ggr[k, pl.ds(i, 16), :].astype(F32)
            sig = m.sig[rows, :]
            gm = (gg * sig).astype(BF).astype(F32)
            gqkv[rows, 0:SLP] = (
                gg * m.mixed[rows, :].astype(F32) * sig * (1.0 - sig)
            ).astype(BF)
            gnum = gm * m.rden[rows, :]
            gres[rows, 0:SLP] = gnum.astype(BF)
            gres[rows, SLP : 2 * SLP] = (-gnum * m.ratio[rows, :]).astype(BF)

        rows_loop(BLK, 16, body, unroll=2)

    mix_back(0)
    for k in (1, 2, 3):
        got(f"gg{k}")
        mix_back(k)
    scatter_combine("wo_s", m.po, m.rbo, ROWS // 2)
    m.sums[...] = dot(ones, gres[:, 0 : 2 * SLP], 1, 0)
    gop[:, 0 : 2 * SLP] = jnp.broadcast_to(m.sums[0:1, :], (SEQ, 2 * SLP))

    def mix_t(d, carry):
        at = pl.ds(band_at(d), BAND)
        gop[at, 0 : 2 * SLP] += dot(m.kern[d], gres[ds(d * TOK, TOK, TOK), 0 : 2 * SLP], 0, 0)
        return carry

    lax.fori_loop(0, CHIPS * CORES, mix_t, 0)

    def keys_back(i):
        rows = pl.ds(i, 16)
        gkv = gop[rows, 0:SLP]
        w = m.wgt[rows, :]
        gqkv[rows, SLP : 2 * SLP] = (
            (gkv * m.val[rows, :].astype(F32) + gop[rows, SLP : 2 * SLP]) * w
        ).astype(BF)
        gqkv[rows, 2 * SLP : 3 * SLP] = (gkv * w).astype(BF)

    rows_loop(SEQ, 16, keys_back, unroll=2)

    sent("g20", "g21", "g22", "g23", "g24", "g25")
    for k in (3, 1, 2, 0):
        part = dot(gqkv[blk_rows(chip(k)), :], m.wqkv[...], 1, 1)
        if k == 0:
            m.own[...] = part
        else:
            m.pgh[k - 1] = part.astype(BF)
        if k == 3:
            scatter_diagonal("g1", m.pgh, m.rbg1, TOK)
        if k == 1:
            scatter_direct_x("g1", m.pgh, m.rbg1, TOK)
        if k == 2:
            scatter_direct_y("g1", m.pgh, m.rbg1, TOK)
    split_rows(m.h1, gqkv, m.gqo, m.gqs)
    send("gqS", m.gqs, m.gqr, SIB)
    scatter_combine("g1", m.pgh, m.rbg1, TOK)

    for k in range(CHIPS):
        for side, keep in ((c, True), (1 - c, False)):
            d = 2 * chip(k) + side
            part = dot(
                gres[ds(d * TOK, TOK, TOK), 0 : 2 * SLP], m.op[pl.ds(band_at(d), BAND), :], 1, 1
            )
            if keep:
                m.gko[k] = part
            else:
                m.gks[k] = part.astype(BF)
    send("gkS", m.gks, m.gkr, SIB)
    got("gqS")
    pair_sum(m.gqo, m.gqr, 9)
    for i in range(4):
        z_end(f"z{i}")
    for i in range(4):
        z_mid(f"z{4 + i}")
    scatter_wait("wo_s")
    for h in range(2):
        n = ROWS // 2
        rows = pl.ds(h * n, n)
        m.zb[8, rows, :] = (
            m.goo[0, rows, :] + m.gor[0, rows, :].astype(F32) + scatter_sum(m.rbo, n, h, pl.ds(0, n))
        ).astype(BF)
    z_start("z8")
    got("gkS")
    for k in (1, 2, 3):
        m.pk[k - 1] = (m.gko[k] + m.gkr[k].astype(F32)).astype(BF)
    scatter_diagonal("kg", m.pk, m.rbk, TOK // 2)
    scatter_direct_x("kg", m.pk, m.rbk, TOK // 2)
    scatter_direct_y("kg", m.pk, m.rbk, TOK // 2)

    local_copy(m.zt.at[pl.ds(0, 4)], gdn_out)
    for i in range(4):
        z_end(f"z{4 + i}")

    def spread(name, first, out):
        for k, to in ((3, PD), (1, PX), (2, PY)):
            send(f"{name}{k}", m.zt.at[first + chip(k)], out.at[b], to)
        local_copy(m.zt.at[first + b], out.at[b])

    spread("fu", 4, gup_out)
    scatter_combine("kg", m.pk, m.rbk, TOK // 2)

    scatter_wait("g1")
    for h in range(2):

        def back_one(i, h=h):
            at = pl.multiple_of(h * TOK + i, 32)
            rows = pl.ds(at, 32)
            total = m.own[rows, :] + scatter_sum(m.rbg1, TOK, h, pl.ds(i, 32))
            m.fgt[rows, :] = norm_back(total, 0, m.n1, m.r1, at, TOK, m.gresid[rows, :]).astype(BF)

        rows_loop(TOK, 32, back_one)
    send("gtS", m.fgt.at[other_half], gtok_out.at[c], SIB)
    local_copy(m.fgt.at[own_half], gtok_out.at[c])

    scatter_wait("kg")
    for h in range(2):
        n = TOK // 2
        rows = pl.ds(h * n, n)
        m.zkb[rows, :] = (
            m.gko[0, rows, :] + m.gkr[0, rows, :].astype(F32) + scatter_sum(m.rbk, n, h, pl.ds(0, n))
        ).astype(BF)
    z_start("zk")
    for i in range(4):
        z_mid(f"z{9 + i}")
    z_mid("z8")
    z_mid("zk")
    for i in range(4):
        z_end(f"z{9 + i}")
    spread("fq", 9, gqkv_out)
    z_end("z8")
    local_copy(m.zt.at[8], gwout_out)
    z_end("zk")
    m.gpb[...] = jnp.zeros((TOK, SEQ), F32)
    m.gpb[:, ds(band_at(r), BAND, LANES)] = jnp.where(
        in_band, m.zkt[...].astype(F32) * jnp.exp(m.pbw[...].astype(F32)), 0.0
    )
    local_copy(m.gpb, gpb_out)

    started = (l_gain, l_tok, l_pb, l_wout, l_wup, l_wdn, l_cot, *l_w)
    for cp in locals_:
        if all(cp is not done for done in started):
            cp.wait()
    for name in remote:
        if name[:-1] in zitems:
            continue
        got(name)
        sent(name)
    for name in zitems:
        z_close(name)


def plane_program(
    tokens, lengths, cotangent, gain_attn, w_query, w_key, w_value, w_out, gain_mlp, w_up, w_down, pos_bias
):
    gains = jnp.pad(jnp.stack([gain_attn, gain_mlp]), ((0, 14), (0, LANES - ROWS)))
    anywhere = pl.BlockSpec(memory_space=pl.ANY)
    struct = jax.ShapeDtypeStruct
    results = pl.pallas_call(
        plane_kernel,
        out_shape=(
            struct((2, TOK, D), BF),
            struct((2, TOK, D), BF),
            struct((CHIPS, ROWS, 3 * SLP), BF),
            struct((ROWS, D), BF),
            struct((CHIPS, ROWS, FS), BF),
            struct((CHIPS, ROWS, D), BF),
            struct((TOK, SEQ), F32),
        ),
        in_specs=[anywhere, pl.BlockSpec(memory_space=pltpu.SMEM)] + [anywhere] * 9,
        out_specs=(anywhere,) * 7,
        scratch_shapes=[pltpu.VMEM(shape, kind) for _, shape, kind in SCRATCH]
        + [
            pltpu.SemaphoreType.DMA((N_REMOTE,)),
            pltpu.SemaphoreType.DMA((N_REMOTE,)),
            pltpu.SemaphoreType.DMA((N_LOCAL,)),
        ],
        compiler_params=pltpu.CompilerParams(
            collective_id=0, has_side_effects=True, vmem_limit_bytes=VMEM_BYTES
        ),
        cost_estimate=pl.CostEstimate(
            flops=15_000_000_000, bytes_accessed=8_000_000, transcendentals=4_000_000
        ),
        name="aft_layer",
    )(
        tokens.reshape(2, TOK, D), lengths.reshape(2), cotangent.reshape(2, TOK, D), gains,
        w_query, w_key, w_value, w_out, w_up, w_down, pos_bias,
    )
    out, gtok, gqkv, gwout, gup, gdn, gpb = results
    gqkv = gqkv.astype(F32)
    grad_q, grad_k, grad_v = (
        gqkv[:, :, i * SLP : i * SLP + SL].transpose(1, 0, 2).reshape(ROWS, D) for i in range(3)
    )
    grad_up = gup.astype(F32).transpose(1, 0, 2).reshape(ROWS, FF)
    paired = sum(
        jnp.sum(g * w.astype(F32), axis=1)
        for g, w in ((grad_q, w_query), (grad_k, w_key), (grad_v, w_value))
    )
    grad_gain_a = paired / gain_attn.astype(F32)
    grad_gain_m = jnp.sum(grad_up * w_up.astype(F32), axis=1) / gain_mlp.astype(F32)
    return (
        out.reshape(tokens.shape),
        gtok.reshape(tokens.shape),
        grad_gain_a,
        grad_q,
        grad_k,
        grad_v,
        gwout.astype(F32),
        grad_gain_m,
        grad_up,
        gdn.astype(F32).reshape(FF // (CHIPS * CORES), D),
        gpb,
    )


def solution(mesh):
    in_specs = (
        P(None, "pipe", "dp", None),
        P(None, "pipe", None),
        P(None, "pipe", "dp", None),
        P("dp"),
        P("dp", None),
        P("dp", None),
        P("dp", None),
        P("dp", None),
        P("dp"),
        P("dp", None),
        P("dp", None),
        P("dp", None),
    )
    out_specs = (
        P(None, "pipe", "dp", None),
        P(None, "pipe", "dp", None),
        P("dp"),
        P("dp", None),
        P("dp", None),
        P("dp", None),
        P("dp", None),
        P("dp"),
        P("dp", None),
        P("dp", None),
        P("dp", None),
    )
    fits = mesh.shape["dp"] == CHIPS * CORES and mesh.shape["pipe"] == DEPTH
    return jax.shard_map(plane_program if fits else local, mesh=mesh, in_specs=in_specs, out_specs=out_specs, check_vma=False)
```

```python
import types

import jax
import jax.numpy as jnp
from jax import lax
from jax.experimental import pallas as pl
from jax.experimental.pallas import tpu as pltpu
from jax.sharding import PartitionSpec as P

D = 768
FF = 3072
SEQ = 1024
WIN = 256


EPSILON = 1e-05
GELU_SCALE = 0.7978845608028654
GELU_CUBE = 0.044715
VMEM_BYTES = 63 * 2**20


def normalize(values, gain):
    centre = values - jnp.mean(values, axis=-1, keepdims=True)
    spread = jnp.mean(centre * centre, axis=-1, keepdims=True)
    return centre * lax.rsqrt(spread + EPSILON) * gain


def gelu_tanh(values):
    return jax.nn.gelu(values, approximate=True)


def band_ones(width):
    row_ids = jnp.arange(width)[:, None]
    col_ids = jnp.arange(3 * width)[None, :]
    return (jnp.abs(col_ids - width - row_ids) < width).astype(jnp.float32)


def band_blocks(bias, width):
    length = bias.shape[0]
    padded = jnp.pad(bias, ((0, 0), (width, width)))
    return jnp.stack(
        [
            padded[block * width : (block + 1) * width, block * width : block * width + 3 * width]
            for block in range(length // width)
        ]
    )


def windows(operand, width):
    blocks = operand.shape[0] // width
    padded = jnp.pad(operand, ((width, width), (0, 0))).reshape(blocks + 2, width, operand.shape[1])
    return jnp.concatenate([padded[:-2], padded[1:-1], padded[2:]], axis=1)


def unwindow(grad_windows, width):
    blocks = grad_windows.shape[0]
    leading = jnp.pad(grad_windows[:, :width], ((0, 2), (0, 0), (0, 0)))
    middle = jnp.pad(grad_windows[:, width : 2 * width], ((1, 1), (0, 0), (0, 0)))
    trailing = jnp.pad(grad_windows[:, 2 * width :], ((2, 0), (0, 0), (0, 0)))
    summed = leading + middle + trailing
    return summed[1:-1].reshape(blocks * width, grad_windows.shape[2])


def to_columns(matrix, seq_count, length):
    channels = matrix.shape[1]
    return (
        matrix.reshape(seq_count, length, channels)
        .transpose(1, 0, 2)
        .reshape(length, seq_count * channels)
    )


def from_columns(matrix, seq_count, length):
    channels = matrix.shape[1] // seq_count
    return (
        matrix.reshape(length, seq_count, channels)
        .transpose(1, 0, 2)
        .reshape(seq_count * length, channels)
    )


def outer_sum(left, right):
    return lax.dot_general(
        left, right, (((0,), (0,)), ((), ())), preferred_element_type=jnp.float32
    )


def times_transpose(left, right):
    return lax.dot_general(
        left, right, (((1,), (1,)), ((), ())), preferred_element_type=jnp.float32
    )


def local(
    tokens,
    lengths,
    cotangent,
    gain_attn,
    w_query,
    w_key,
    w_value,
    w_out,
    gain_mlp,
    w_up,
    w_down,
    pos_bias,
):
    gathered = (
        lax.all_gather(gain_attn, "dp", axis=0, tiled=True),
        lax.all_gather(w_query, "dp", axis=0, tiled=True),
        lax.all_gather(w_key, "dp", axis=0, tiled=True),
        lax.all_gather(w_value, "dp", axis=0, tiled=True),
        lax.all_gather(w_out, "dp", axis=0, tiled=True),
        lax.all_gather(gain_mlp, "dp", axis=0, tiled=True),
        lax.all_gather(w_up, "dp", axis=0, tiled=True),
        lax.all_gather(w_down, "dp", axis=0, tiled=True),
        lax.all_gather(pos_bias, "dp", axis=0, tiled=True),
    )
    gain_a = gathered[0].astype(jnp.float32)
    query_w, key_w, value_w, out_w = (gathered[1], gathered[2], gathered[3], gathered[4])
    gain_m = gathered[5].astype(jnp.float32)
    up_w, down_w = (gathered[6], gathered[7])
    bias_full = gathered[8].astype(jnp.float32)
    group_size = lax.axis_size("dp")
    tok_rows = tokens.shape[2]
    seq_count = group_size * tok_rows // SEQ
    band_mask = band_ones(WIN)
    bias_blocks = jnp.exp(band_blocks(bias_full, WIN))
    exp_band = bias_blocks * band_mask
    kernel = ((bias_blocks - 1.0) * band_mask).astype(jnp.bfloat16)
    positions = jnp.arange(SEQ)
    grad_gain_a = jnp.zeros((D,), jnp.float32)
    grad_gain_m = jnp.zeros((D,), jnp.float32)
    grad_query_w = jnp.zeros((D, D), jnp.float32)
    grad_key_w = jnp.zeros((D, D), jnp.float32)
    grad_value_w = jnp.zeros((D, D), jnp.float32)
    grad_out_w = jnp.zeros((D, D), jnp.float32)
    grad_up_w = jnp.zeros((D, FF), jnp.float32)
    grad_down_w = jnp.zeros((FF, D), jnp.float32)
    grad_kernel = jnp.zeros(exp_band.shape, jnp.float32)
    outputs_list = []
    grads_in_list = []
    for micro in range(tokens.shape[0]):
        inputs_f = tokens[micro, 0].astype(jnp.float32)
        normed_f, norm_back_a = jax.vjp(normalize, inputs_f, gain_a)
        normed = normed_f.astype(jnp.bfloat16)
        query = jnp.dot(normed, query_w, preferred_element_type=jnp.float32)
        keys = jnp.dot(normed, key_w, preferred_element_type=jnp.float32).astype(jnp.bfloat16)
        values = jnp.dot(normed, value_w, preferred_element_type=jnp.float32).astype(jnp.bfloat16)
        key_chan, value_chan = (
            lax.all_to_all(keys, "dp", split_axis=1, concat_axis=0, tiled=True),
            lax.all_to_all(values, "dp", split_axis=1, concat_axis=0, tiled=True),
        )
        seq_lengths = lengths[micro, 0]
        channels = key_chan.shape[1]
        valid_seq = (positions[:, None] < seq_lengths[None, :]).astype(jnp.float32)
        valid_cols = jnp.broadcast_to(valid_seq[:, :, None], (SEQ, seq_count, channels)).reshape(
            SEQ, seq_count * channels
        )
        key_cols = to_columns(key_chan, seq_count, SEQ).astype(jnp.float32)
        value_cols = to_columns(value_chan, seq_count, SEQ).astype(jnp.float32)
        weighted = jnp.exp(key_cols) * valid_cols
        col_count = weighted.shape[1]
        operand = jnp.concatenate(
            [(weighted * value_cols).astype(jnp.bfloat16), weighted.astype(jnp.bfloat16)], axis=1
        )
        windowed = windows(operand, WIN)
        banded = jnp.einsum(
            "nqk,nkc->nqc", kernel, windowed, preferred_element_type=jnp.float32
        ).reshape(SEQ, 2 * col_count)
        result = banded + jnp.sum(operand, axis=0, dtype=jnp.float32)[None, :]
        numerator = result[:, :col_count]
        denominator = result[:, col_count:] + 1.0 - valid_cols
        mixed_cols = numerator / denominator * valid_cols
        mixed_tok = lax.all_to_all(
            from_columns(mixed_cols.astype(jnp.bfloat16), seq_count, SEQ),
            "dp",
            split_axis=0,
            concat_axis=1,
            tiled=True,
        )
        sigmoid_q = jax.nn.sigmoid(query)
        mixed_f = mixed_tok.astype(jnp.float32)
        gated = (sigmoid_q * mixed_f).astype(jnp.bfloat16)
        resid = inputs_f + jnp.dot(gated, out_w, preferred_element_type=jnp.float32)
        normed_two_f, norm_back_m = jax.vjp(normalize, resid, gain_m)
        normed_two = normed_two_f.astype(jnp.bfloat16)
        upper = jnp.dot(normed_two, up_w, preferred_element_type=jnp.float32)
        hidden_f, gelu_back = jax.vjp(gelu_tanh, upper)
        hidden = hidden_f.astype(jnp.bfloat16)
        outputs_list.append(
            (resid + jnp.dot(hidden, down_w, preferred_element_type=jnp.float32)).astype(
                jnp.bfloat16
            )
        )
        grad_out = cotangent[micro, 0]
        grad_down_w = grad_down_w + outer_sum(hidden, grad_out)
        grad_hidden = times_transpose(grad_out, down_w)
        grad_upper = gelu_back(grad_hidden)[0].astype(jnp.bfloat16)
        grad_up_w = grad_up_w + outer_sum(normed_two, grad_upper)
        grad_normed_two = times_transpose(grad_upper, up_w)
        grad_resid_norm, grad_gain_part_m = norm_back_m(grad_normed_two)
        grad_gain_m = grad_gain_m + grad_gain_part_m
        grad_resid = grad_out.astype(jnp.float32) + grad_resid_norm
        grad_attn = grad_resid.astype(jnp.bfloat16)
        grad_out_w = grad_out_w + outer_sum(gated, grad_attn)
        grad_gated = times_transpose(grad_attn, out_w)
        grad_mixed = (grad_gated * sigmoid_q).astype(jnp.bfloat16)
        grad_query = (grad_gated * mixed_f * sigmoid_q * (1.0 - sigmoid_q)).astype(jnp.bfloat16)
        grad_mixed_chan = lax.all_to_all(grad_mixed, "dp", split_axis=1, concat_axis=0, tiled=True)
        grad_mixed_cols = to_columns(grad_mixed_chan, seq_count, SEQ).astype(jnp.float32)
        grad_numerator = grad_mixed_cols * valid_cols / denominator
        grad_denominator = -grad_numerator * (numerator / denominator)
        grad_flat = jnp.concatenate(
            [grad_numerator.astype(jnp.bfloat16), grad_denominator.astype(jnp.bfloat16)], axis=1
        )
        grad_result = grad_flat.reshape(SEQ // WIN, WIN, 2 * col_count)
        grad_windowed = jnp.einsum(
            "nqk,nqc->nkc", kernel, grad_result, preferred_element_type=jnp.float32
        )
        grad_kernel = grad_kernel + jnp.einsum(
            "nqc,nkc->nqk", grad_result, windowed, preferred_element_type=jnp.float32
        )
        grad_operand = (
            unwindow(grad_windowed, WIN) + jnp.sum(grad_flat, axis=0, dtype=jnp.float32)[None, :]
        )
        grad_key_value = grad_operand[:, :col_count]
        grad_key_weight = grad_operand[:, col_count:]
        grad_keys_cols = (grad_key_value * value_cols + grad_key_weight) * weighted
        grad_values_cols = grad_key_value * weighted
        grad_keys, grad_values = (
            lax.all_to_all(
                from_columns(grad_keys_cols.astype(jnp.bfloat16), seq_count, SEQ),
                "dp",
                split_axis=0,
                concat_axis=1,
                tiled=True,
            ),
            lax.all_to_all(
                from_columns(grad_values_cols.astype(jnp.bfloat16), seq_count, SEQ),
                "dp",
                split_axis=0,
                concat_axis=1,
                tiled=True,
            ),
        )
        grad_query_w = grad_query_w + outer_sum(normed, grad_query)
        grad_key_w = grad_key_w + outer_sum(normed, grad_keys)
        grad_value_w = grad_value_w + outer_sum(normed, grad_values)
        grad_normed = (
            times_transpose(grad_query, query_w)
            + times_transpose(grad_keys, key_w)
            + times_transpose(grad_values, value_w)
        )
        grad_input_norm, grad_gain_part_a = norm_back_a(grad_normed)
        grad_gain_a = grad_gain_a + grad_gain_part_a
        grads_in_list.append((grad_resid + grad_input_norm).astype(jnp.bfloat16))
    grad_kernel_bias = grad_kernel * exp_band
    grad_bias_pad = jnp.zeros((SEQ, SEQ + 2 * WIN), jnp.float32)
    for block in range(SEQ // WIN):
        grad_bias_pad = grad_bias_pad.at[
            block * WIN : (block + 1) * WIN, block * WIN : block * WIN + 3 * WIN
        ].add(grad_kernel_bias[block])
    grad_bias = grad_bias_pad[:, WIN : WIN + SEQ]
    shares = (
        lax.psum_scatter(grad_gain_a, "dp", scatter_dimension=0, tiled=True),
        lax.psum_scatter(grad_query_w, "dp", scatter_dimension=0, tiled=True),
        lax.psum_scatter(grad_key_w, "dp", scatter_dimension=0, tiled=True),
        lax.psum_scatter(grad_value_w, "dp", scatter_dimension=0, tiled=True),
        lax.psum_scatter(grad_out_w, "dp", scatter_dimension=0, tiled=True),
        lax.psum_scatter(grad_gain_m, "dp", scatter_dimension=0, tiled=True),
        lax.psum_scatter(grad_up_w, "dp", scatter_dimension=0, tiled=True),
        lax.psum_scatter(grad_down_w, "dp", scatter_dimension=0, tiled=True),
        lax.psum_scatter(grad_bias, "dp", scatter_dimension=0, tiled=True),
    )
    reduced = lax.psum(
        (
            shares[0],
            shares[1],
            shares[2],
            shares[3],
            shares[4],
            shares[5],
            shares[6],
            shares[7],
            shares[8],
        ),
        "pipe",
    )
    final_grads = (
        reduced[0],
        reduced[1],
        reduced[2],
        reduced[3],
        reduced[4],
        reduced[5],
        reduced[6],
        reduced[7],
        reduced[8],
    )
    output = jnp.stack(outputs_list)[:, None]
    grad_tokens = jnp.stack(grads_in_list)[:, None]
    return (
        output,
        grad_tokens,
        final_grads[0],
        final_grads[1],
        final_grads[2],
        final_grads[3],
        final_grads[4],
        final_grads[5],
        final_grads[6],
        final_grads[7],
        final_grads[8],
    )


CHIPS = 4
CORES = 2
DEPTH = 4
LANES = 128
TOK = 128
BLK = CORES * TOK
ROWS = D // (CHIPS * CORES)
SL = D // CHIPS
SLP = -(-SL // LANES) * LANES
FS = FF // CHIPS
BAND = 5 * LANES
HALF = D // 2
PACK = ROWS + ROWS // 2
MESH_ID = pl.DeviceIdType.MESH
F32 = jnp.float32
BF = jnp.bfloat16

SCRATCH = dict(
    tok=((BLK, D), BF),
    cot=((SEQ, D), BF),
    gains=((CHIPS * CORES, 16, LANES), BF),
    gain=((16, D), F32),
    wst=((3, ROWS, D), BF),
    wqs=((CHIPS, ROWS, 3 * SLP), BF),
    wqkv=((D, 3 * SLP), BF),
    wout=((CHIPS * SLP, D), BF),
    wup=((D, FS), BF),
    wdn=((FS, D), BF),
    pbw=((TOK, BAND), BF),
    kern=((CHIPS * CORES, TOK, BAND), BF),
    h1=((SEQ, D), BF),
    h2=((SEQ, D), BF),
    n1=((BLK, D), F32),
    r1=((BLK, LANES), F32),
    n2=((BLK, D), F32),
    r2=((BLK, LANES), F32),
    tmp=((HALF, D), F32),
    tmix=((TOK, 2 * SLP), F32),
    sums=((8, 2 * SLP), F32),
    sig=((SEQ, SLP), F32),
    wgt=((SEQ, SLP), F32),
    val=((SEQ, SLP), BF),
    op=((SEQ, 2 * SLP), BF),
    ratio=((SEQ, SLP), F32),
    rden=((SEQ, SLP), F32),
    mixed=((SEQ, SLP), BF),
    gated=((SEQ, SLP), BF),
    grecv=((CHIPS, BLK, SLP), BF),
    resid=((BLK, D), F32),
    hid=((SEQ, FS), BF),
    dge=((BLK, FS), F32),
    gop=((SEQ, 2 * SLP), F32),
    gupr=((SEQ, FS), BF),
    pout=((CHIPS - 1, BLK, D), BF),
    pgh=((CHIPS - 1, BLK, D), BF),
    own=((BLK, D), F32),
    rbout=((6, TOK, D), BF),
    rbg2=((6, TOK, D), BF),
    rbg1=((6, TOK, D), BF),
    gresid=((BLK, D), F32),
    gattn=((BLK, D), BF),
    ggs=((CHIPS - 1, BLK, SLP), BF),
    ggr=((CHIPS, BLK, SLP), BF),
    gdo=((HALF, D), F32),
    gdx=((HALF, D), F32),
    gds=((CHIPS, ROWS, D), BF),
    gdr=((CHIPS, ROWS, D), BF),
    guo=((D, FS), F32),
    gus=((CHIPS, ROWS, FS), BF),
    gur=((CHIPS, ROWS, FS), BF),
    gqo=((CHIPS, ROWS, SLP), F32),
    gqs=((CHIPS, ROWS, SLP), BF),
    gqr=((CHIPS, ROWS, SLP), BF),
    gvo=((CHIPS, ROWS, 2 * SLP), F32),
    gvs=((CHIPS, ROWS, 2 * SLP), BF),
    gvr=((CHIPS, ROWS, 2 * SLP), BF),
    goo=((CHIPS, ROWS, D), F32),
    gos=((CHIPS, ROWS, D), BF),
    gor=((CHIPS, ROWS, D), BF),
    po=((CHIPS - 1, ROWS, D), BF),
    rbo=((6, ROWS // 2, D), BF),
    gko=((CHIPS, TOK, BAND), F32),
    gks=((CHIPS, TOK, BAND), BF),
    gkr=((CHIPS, TOK, BAND), BF),
    pk=((CHIPS - 1, TOK, BAND), BF),
    rbk=((6, TOK // 2, BAND), BF),
    zdb=((CHIPS, ROWS, D), BF),
    zdr=((CHIPS, ROWS, D), BF),
    zdt=((CHIPS, ROWS, D), BF),
    zub=((CHIPS, ROWS, FS), BF),
    zur=((CHIPS, ROWS, FS), BF),
    zut=((CHIPS, ROWS, FS), BF),
    zqb=((CHIPS, PACK, LANES), BF),
    zqr=((CHIPS, PACK, LANES), BF),
    zqt=((CHIPS, PACK, LANES), BF),
    zvb=((CHIPS, 2 * PACK, LANES), BF),
    zvr=((CHIPS, 2 * PACK, LANES), BF),
    zvt=((CHIPS, 2 * PACK, LANES), BF),
    zob=((ROWS, D), BF),
    zor=((ROWS, D), BF),
    zot=((ROWS, D), BF),
    zkb=((TOK, BAND), BF),
    zkr=((TOK, BAND), BF),
    zkt=((TOK, BAND), BF),
    fout=((BLK, D), BF),
    fgt=((BLK, D), BF),
)
N_REMOTE = 200
N_LOCAL = 40


def dot(left, right, left_dim, right_dim):
    return lax.dot_general(
        left, right, (((left_dim,), (right_dim,)), ((), ())), preferred_element_type=F32
    )


def rows_loop(count, step, body, unroll=1):
    def one(i, carry):
        body(pl.multiple_of(i * step, step))
        return carry

    lax.fori_loop(0, count // step, one, 0, unroll=unroll)


def plane_kernel(
    tok_in, len_in, cot_in, gains_in, wq_in, wk_in, wv_in, wout_in, wup_in, wdn_in, pb_in,
    out_out, gtok_out, gq_out, gv_out, gwout_out, gup_out, gdn_out, gpb_out,
    *scratch,
):
    m = types.SimpleNamespace(**dict(zip(SCRATCH, scratch)))
    send_sem, recv_sem, local_sem = scratch[len(SCRATCH):]
    r = lax.axis_index("dp")
    z = lax.axis_index("pipe")
    c = lax.rem(r, 2)
    x = lax.rem(r // 2, 2)
    y = r // 4
    b = r // 2
    length = len_in[c]

    def chip(k):
        return 2 * (1 - y if k // 2 else y) + (1 - x if k % 2 else x)

    def peer(k, other=0):
        return (2 * chip(k) + (1 - c if other else c), z)

    jx, jy, jd = chip(1), chip(2), chip(3)
    SIB, PX, PY, PD = peer(0, 1), peer(1), peer(2), peer(3)
    z_near = z + 1 - 2 * lax.rem(z, 2)
    z_far = 3 - z
    ZN, ZF = (r, z_near), (r, z_far)
    outer = z * (3 - z) == 0
    inner = z * (3 - z) != 0

    remote, locals_ = {}, []
    waited = set()
    begun = []

    def make(name, src, dst, to):
        assert name not in remote, name
        i = len(remote)
        cp = pltpu.make_async_remote_copy(
            src_ref=src, dst_ref=dst, send_sem=send_sem.at[i], recv_sem=recv_sem.at[i],
            device_id=to, device_id_type=MESH_ID,
        )
        remote[name] = cp
        return cp

    def send(name, src, dst, to):
        make(name, src, dst, to)
        start(name)

    def start(*names):
        for name in names:
            begun.append(name)
            remote[name].start()

    def got(*names):
        for name in names:
            if name not in waited:
                waited.add(name)
                remote[name].wait_recv()

    def sent(*names):
        for name in names:
            if name + "/s" not in waited:
                waited.add(name + "/s")
                remote[name].wait_send()

    def local_copy(src, dst):
        cp = pltpu.make_async_copy(src, dst, local_sem.at[len(locals_)])
        locals_.append(cp)
        cp.start()
        return cp

    def ds(start, size, unit):
        return pl.ds(pl.multiple_of(start, unit), size)

    def band_at(d):
        return pl.multiple_of(jnp.minimum(jnp.maximum(d - 2, 0), 3) * LANES, LANES)

    def gather_open(name, blk):
        make(name + "X0", blk(b, 0), blk(b, 0), PX)
        make(name + "Y1", blk(b, 1), blk(b, 1), PY)
        make(name + "X1", blk(b, 1), blk(b, 1), PX)
        make(name + "Y0", blk(b, 0), blk(b, 0), PY)
        make(name + "F0", blk(jx, 0), blk(jx, 0), PY)
        make(name + "F1", blk(jy, 1), blk(jy, 1), PX)

    def gather_start(name):
        start(name + "X0", name + "Y1", name + "X1", name + "Y0")

    def gather_forward(name):
        got(name + "X0")
        start(name + "F0")
        got(name + "Y1")
        start(name + "F1")

    def gather_wait(name, k):
        got(*{1: (name + "X0", name + "X1"), 2: (name + "Y0", name + "Y1"), 3: (name + "F0", name + "F1")}[k])

    fetch = lax.rem(z, 2) == c
    passed = lax.rem(z, 2) != c
    in_fetch = []

    def relay_open(name, place):
        for k in (1, 2, 3):
            make(f"{name}Z{k}", place(k), place(k), ZN)
            in_fetch.append(f"{name}Z{k}")

    def relay(name, place, arrive):
        for k in (1, 2, 3):

            @pl.when(fetch)
            def _(k=k):
                arrive(k)
                start(f"{name}Z{k}")

            @pl.when(passed)
            def _(k=k):
                remote[f"{name}Z{k}"].wait_recv()

            waited.add(f"{name}Z{k}")
            send(f"{name}S{k}", place(k), place(k), SIB)

    def scatter_diagonal(name, part, buf, half):
        send(name + "0", part.at[2, pl.ds(half, half)], buf.at[0], PX)
        send(name + "1", part.at[2, pl.ds(0, half)], buf.at[1], PY)

    def scatter_direct_x(name, part, buf, half):
        send(name + "2", part.at[0, pl.ds(half, half)], buf.at[2], PX)

    def scatter_direct_y(name, part, buf, half):
        send(name + "3", part.at[1, pl.ds(0, half)], buf.at[3], PY)

    def scatter_combine(name, part, buf, half):
        got(name + "1")
        part[0, pl.ds(0, half), :] = (
            part[0, pl.ds(0, half), :].astype(F32) + buf[1].astype(F32)
        ).astype(BF)
        send(name + "4", part.at[0, pl.ds(0, half)], buf.at[4], PX)
        got(name + "0")
        part[1, pl.ds(half, half), :] = (
            part[1, pl.ds(half, half), :].astype(F32) + buf[0].astype(F32)
        ).astype(BF)
        send(name + "5", part.at[1, pl.ds(half, half)], buf.at[5], PY)

    def scatter_wait(name):
        got(name + "2", name + "3", name + "4", name + "5")

    def scatter_sum(buf, half, h, rows):
        if h == 0:
            return buf[3, rows, :].astype(F32) + buf[4, rows, :].astype(F32)
        return buf[2, rows, :].astype(F32) + buf[5, rows, :].astype(F32)

    zitems = {}

    def z_open(name, base, near, total):
        zitems[name] = (
            base,
            near,
            total,
            make(name + "a", base, near, ZN),
            make(name + "b", base, total, ZF),
            make(name + "c", total, total, ZN),
        )

    def z_start(name):
        item = zitems[name]

        @pl.when(outer)
        def _():
            item[3].start()

    def z_mid(name):
        base, near, total, into, across, back = zitems[name]

        @pl.when(inner)
        def _():
            into.wait_recv()
            base[...] = (base[...].astype(F32) + near[...].astype(F32)).astype(BF)
            across.start()

    def z_end(name):
        base, near, total, into, across, back = zitems[name]

        @pl.when(inner)
        def _():
            across.wait_recv()
            total[...] = (base[...].astype(F32) + total[...].astype(F32)).astype(BF)
            back.start()

        @pl.when(outer)
        def _():
            back.wait_recv()

    def z_close(name):
        base, near, total, into, across, back = zitems[name]

        @pl.when(outer)
        def _():
            into.wait_send()

        @pl.when(inner)
        def _():
            across.wait_send()
            back.wait_send()

    for k in range(CHIPS):
        j = chip(k)
        z_open(f"zd{k}", m.zdb.at[j], m.zdr.at[j], m.zdt.at[j])
        z_open(f"zu{k}", m.zub.at[j], m.zur.at[j], m.zut.at[j])
        z_open(f"zq{k}", m.zqb.at[j], m.zqr.at[j], m.zqt.at[j])
        z_open(f"zv{k}", m.zvb.at[j], m.zvr.at[j], m.zvt.at[j])
    z_open("zo", m.zob, m.zor, m.zot)
    z_open("zk", m.zkb, m.zkr, m.zkt)
    ORDER = (3, 1, 2, 0)

    own_half = ds(c * TOK, TOK, TOK)
    other_half = ds((1 - c) * TOK, TOK, TOK)
    l_gain = local_copy(gains_in, m.gains.at[r])
    l_tok = local_copy(tok_in.at[c], m.tok.at[own_half])
    l_w = [local_copy(w, m.wst.at[i]) for i, w in enumerate((wq_in, wk_in, wv_in))]
    l_pb = local_copy(pb_in.at[:, ds(band_at(r), BAND, LANES)], m.pbw)

    def wout_rows(j, core):
        return m.wout.at[ds(j * SLP + core * ROWS, ROWS, 32)]

    l_wout = local_copy(wout_in, wout_rows(b, c))
    up_rows = ds(r * ROWS, ROWS, 32)
    l_wup = local_copy(wup_in.at[:, ds(b * FS, FS, LANES)], m.wup.at[up_rows])
    dn_rows = ds(c * HALF, HALF, LANES)
    l_wdn = local_copy(wdn_in, m.wdn.at[dn_rows])
    cot_half = ds(b * BLK + c * TOK, TOK, TOK)
    l_cot = local_copy(cot_in.at[c], m.cot.at[cot_half])

    barrier = pltpu.get_barrier_semaphore()
    everyone = [peer(k, o) for k in range(CHIPS) for o in range(CORES) if (k, o) != (0, 0)] + [ZN, ZF]
    for other in everyone:
        pl.semaphore_signal(barrier, inc=1, device_id=other, device_id_type=MESH_ID)
    pl.semaphore_wait(barrier, len(everyone))

    send("tokS", tok_in.at[1 - c], m.tok.at[own_half], SIB)
    gain_names = []
    for k in range(CHIPS):
        for o in range(CORES):
            if (k, o) != (0, 0):
                gain_names.append(f"gain{k}{o}")
                send(gain_names[-1], gains_in, m.gains.at[r], peer(k, o))
    for cp in l_w:
        cp.wait()
    for i in range(3):
        w_rows = m.wst[i].astype(F32)
        for j in range(CHIPS):
            piece = w_rows[:, j * SL : (j + 1) * SL]
            m.wqs[j, :, i * SLP : (i + 1) * SLP] = jnp.concatenate(
                [piece, jnp.zeros((ROWS, SLP - SL), F32)], axis=1
            ).astype(BF)
    for k, to in ((1, PX), (2, PY), (3, PD)):
        make(f"wq{k}", m.wqs.at[chip(k)], m.wqkv.at[up_rows], to)
        in_fetch.append(f"wq{k}")

    @pl.when(fetch)
    def _():
        start("wq1", "wq2", "wq3")

    send("wqS0", m.wqs.at[b], m.wqkv.at[up_rows], SIB)
    m.wqkv[up_rows, :] = m.wqs[b]

    l_gain.wait()
    got(*gain_names)
    m.gain[...] = jnp.concatenate(
        [m.gains[d].astype(F32)[:, :ROWS] for d in range(CHIPS * CORES)], axis=1
    )

    def norm(src, gain_row, n_ref, r_ref, dst, base):
        def body(i):
            rows = pl.ds(i, 32)
            values = src[rows, :].astype(F32)
            centre = values - jnp.mean(values, axis=-1, keepdims=True)
            spread = jnp.mean(centre * centre, axis=-1, keepdims=True)
            rinv = lax.rsqrt(spread + EPSILON)
            n = centre * rinv
            n_ref[rows, :] = n
            r_ref[rows, :] = jnp.broadcast_to(rinv, (32, LANES))
            dst[pl.ds(pl.multiple_of(base + i, 32), 32), :] = (
                n * m.gain[gain_row : gain_row + 1, :]
            ).astype(BF)

        rows_loop(BLK, 32, body, unroll=2)

    l_tok.wait()
    got("tokS")
    norm(m.tok, 0, m.n1, m.r1, m.h1, b * BLK)

    def h1_blk(j, h):
        return m.h1.at[ds(j * BLK + h * TOK, TOK, TOK)]

    gather_open("h1", h1_blk)
    gather_start("h1")

    l_pb.wait()
    t_ids = r * TOK + lax.broadcasted_iota(jnp.int32, (TOK, BAND), 0)
    u_ids = band_at(r) + lax.broadcasted_iota(jnp.int32, (TOK, BAND), 1)
    in_band = jnp.abs(t_ids - u_ids) < WIN
    m.kern[r] = jnp.where(in_band, jnp.exp(m.pbw[...].astype(F32)) - 1.0, 0.0).astype(BF)

    def kern_blk(j, h):
        return m.kern.at[2 * j + c, pl.ds(h * (TOK // 2), TOK // 2)]

    gather_open("kn", kern_blk)
    in_fetch.extend("kn" + part for part in ("X0", "X1", "Y0", "Y1", "F0", "F1"))

    @pl.when(fetch)
    def _():
        gather_start("kn")

    send("knS0", m.kern.at[r], m.kern.at[r], SIB)

    def w_place(ref):
        return lambda k: ref.at[ds((2 * chip(k) + c) * ROWS, ROWS, 32)]

    wq_place = w_place(m.wqkv)
    relay_open("wq", wq_place)
    relay("wq", wq_place, lambda k: got(f"wq{k}"))
    gather_forward("h1")

    @pl.when(fetch)
    def _():
        gather_forward("kn")

    for j in range(CHIPS):
        m.wout[j * SLP + SL : (j + 1) * SLP, :] = jnp.zeros((SLP - SL, D), BF)

    l_wout.wait()

    def wout_blk(j, h):
        return m.wout.at[ds(j * SLP + c * ROWS + h * (ROWS // 2), ROWS // 2, 16)]

    gather_open("wo", wout_blk)
    in_fetch.extend("wo" + part for part in ("X0", "X1", "Y0", "Y1", "F0", "F1"))
    for k, to in ((1, PX), (2, PY), (3, PD)):
        make(f"wu{k}", wup_in.at[:, ds(chip(k) * FS, FS, LANES)], m.wup.at[up_rows], to)
        in_fetch.append(f"wu{k}")

    @pl.when(fetch)
    def _():
        gather_start("wo")
        start("wu1", "wu2", "wu3")

    send("woS0", wout_rows(b, c), wout_rows(b, c), SIB)
    l_wup.wait()
    send("wuS0", m.wup.at[up_rows], m.wup.at[up_rows], SIB)
    l_wdn.wait()
    send("wdS", m.wdn.at[dn_rows], m.wdn.at[dn_rows], SIB)
    send("cotS", cot_in.at[1 - c], m.cot.at[cot_half], SIB)
    got("wqS0", "wqS1", "wqS2", "wqS3")

    def blk_rows(j):
        return ds(j * BLK, BLK, BLK)

    def project(j):
        m.tmp[0:BLK, :] = dot(m.h1[blk_rows(j), :], m.wqkv[...], 1, 0)

        def body(i):
            rows = pl.ds(i, 16)
            at = pl.multiple_of(j * BLK + i, 16)
            to = pl.ds(at, 16)
            q = m.tmp[rows, 0:SLP]
            m.sig[to, :] = 1.0 / (1.0 + jnp.exp(-q))
            keys = m.tmp[rows, SLP : 2 * SLP].astype(BF).astype(F32)
            values = m.tmp[rows, 2 * SLP : 3 * SLP].astype(BF)
            pos = at + lax.broadcasted_iota(jnp.int32, (16, SLP), 0)
            weighted = jnp.where(pos < length, jnp.exp(keys), 0.0)
            m.wgt[to, :] = weighted
            m.val[to, :] = values
            m.op[to, 0:SLP] = (weighted * values.astype(F32)).astype(BF)
            m.op[to, SLP : 2 * SLP] = weighted.astype(BF)

        rows_loop(BLK, 16, body, unroll=2)

    project(b)
    for k in (1, 2):
        gather_wait("h1", k)
        project(chip(k))
    kn_place = lambda k: m.kern.at[2 * chip(k) + c]
    relay_open("kn", kn_place)
    relay("kn", kn_place, lambda k: gather_wait("kn", k))
    gather_wait("h1", 3)
    project(jd)

    @pl.when(fetch)
    def _():
        gather_forward("wo")

    l_cot.wait()
    got("cotS")

    def cot_blk(j, h):
        return m.cot.at[ds(j * BLK + h * TOK, TOK, TOK)]

    gather_open("ct", cot_blk)
    start("ctX0", "ctY1")

    got("knS0", "knS1", "knS2", "knS3")
    ones = jnp.ones((8, SEQ), BF)
    m.sums[...] = dot(ones, m.op[...], 1, 0)

    def mix(d):
        m.tmix[...] = dot(m.kern[d], m.op[pl.ds(band_at(d), BAND), :], 1, 0)

        def body(i):
            rows = pl.ds(i, 32)
            at = pl.multiple_of(d * TOK + i, 32)
            to = pl.ds(at, 32)
            pos = at + lax.broadcasted_iota(jnp.int32, (32, SLP), 0)
            valid = jnp.where(pos < length, 1.0, 0.0)
            num = m.tmix[rows, 0:SLP] + m.sums[0:1, 0:SLP]
            den = m.tmix[rows, SLP : 2 * SLP] + m.sums[0:1, SLP : 2 * SLP] + 1.0 - valid
            rden = 1.0 / den
            ratio = num * rden
            mixed = (ratio * valid).astype(BF)
            m.ratio[to, :] = ratio
            m.rden[to, :] = rden * valid
            m.mixed[to, :] = mixed
            m.gated[to, :] = (m.sig[to, :] * mixed.astype(F32)).astype(BF)

        rows_loop(TOK, 32, body, unroll=2)

    def mix_block(j):
        def one(i, carry):
            mix(2 * j + i)
            return carry

        lax.fori_loop(0, CORES, one, 0)

    for k, to in ((3, PD), (1, PX), (2, PY)):
        j = chip(k)
        mix_block(j)
        send(f"ga{k}", m.gated.at[blk_rows(j)], m.grecv.at[k], to)
    mix_block(b)
    m.grecv[0] = m.gated[blk_rows(b), :]

    gather_forward("ct")
    wo_place = lambda k: wout_rows(chip(k), c)
    relay_open("wo", wo_place)
    relay("wo", wo_place, lambda k: gather_wait("wo", k))
    wu_place = w_place(m.wup)
    relay_open("wu", wu_place)
    relay("wu", wu_place, lambda k: got(f"wu{k}"))

    got("woS0", "woS1", "woS2", "woS3")
    m.resid[...] = m.tok[...].astype(F32)
    for k in (0, 1, 2, 3):
        if k:
            got(f"ga{k}")
        m.resid[...] += dot(m.grecv[k], m.wout[ds(chip(k) * SLP, SLP, SLP), :], 1, 0)
    norm(m.resid, 1, m.n2, m.r2, m.h2, b * BLK)

    def h2_blk(j, h):
        return m.h2.at[ds(j * BLK + h * TOK, TOK, TOK)]

    gather_open("h2", h2_blk)
    gather_start("h2")
    start("ctX1", "ctY0")

    got("wuS0", "wuS1", "wuS2", "wuS3", "wdS")

    def feed_forward(k):
        j = chip(k)
        if k:
            gather_wait("h2", k)
        m.tmp[0:BLK, :] = dot(m.h2[blk_rows(j), :], m.wup[...], 1, 0)

        def gelu(i):
            rows = pl.ds(i, 16)
            v = m.tmp[rows, :]
            square = v * v
            t = jnp.tanh(GELU_SCALE * v * (1.0 + GELU_CUBE * square))
            half = 0.5 * (1.0 + t)
            m.hid[pl.ds(pl.multiple_of(j * BLK + i, 16), 16), :] = (v * half).astype(BF)
            m.dge[rows, :] = half + 0.5 * v * (1.0 - t * t) * (
                GELU_SCALE * (1.0 + 3.0 * GELU_CUBE * square)
            )

        rows_loop(BLK, 16, gelu, unroll=2)
        part = dot(m.hid[blk_rows(j), :], m.wdn[...], 1, 0)
        if k == 0:
            m.resid[...] += part
        else:
            m.pout[k - 1] = part.astype(BF)
            gather_wait("ct", k)
        m.tmp[0:BLK, :] = dot(m.cot[blk_rows(j), :], m.wdn[...], 1, 1)

        def back(i):
            rows = pl.ds(i, 16)
            m.gupr[pl.ds(pl.multiple_of(j * BLK + i, 16), 16), :] = (
                m.tmp[rows, :] * m.dge[rows, :]
            ).astype(BF)

        rows_loop(BLK, 16, back, unroll=2)
        part = dot(m.gupr[blk_rows(j), :], m.wup[...], 1, 1)
        if k == 0:
            m.own[...] = part
        else:
            m.pgh[k - 1] = part.astype(BF)

    other_cols = ds((1 - c) * HALF, HALF, LANES)
    own_cols = ds(c * HALF, HALF, LANES)

    def ff_grads(k):
        rows = blk_rows(chip(k))
        for dst, at, left, cols, right in (
            (m.gdx, 0, m.hid, other_cols, m.cot),
            (m.gdo, 0, m.hid, own_cols, m.cot),
            (m.guo, 0, m.h2, pl.ds(0, HALF), m.gupr),
            (m.guo, HALF, m.h2, pl.ds(HALF, HALF), m.gupr),
        ):
            part = dot(left[rows, cols], right[rows, :], 0, 0)
            to = pl.ds(at, HALF)
            if k == 0:
                dst[to, :] = part
            else:
                dst[to, :] += part

    feed_forward(0)
    gather_forward("h2")
    ff_grads(0)
    feed_forward(1)
    scatter_direct_x("g2", m.pgh, m.rbg2, TOK)
    ff_grads(1)
    feed_forward(2)
    scatter_direct_y("g2", m.pgh, m.rbg2, TOK)
    ff_grads(2)
    feed_forward(3)
    scatter_diagonal("g2", m.pgh, m.rbg2, TOK)
    ff_grads(3)

    for j in range(CHIPS):
        m.gds[j] = m.gdx[j * ROWS : (j + 1) * ROWS, :].astype(BF)
    send("gdS", m.gds, m.gdr, SIB)
    for j in range(CHIPS):
        m.gus[j] = m.guo[ds((2 * j + 1 - c) * ROWS, ROWS, 32), :].astype(BF)
    send("guS", m.gus, m.gur, SIB)

    def split_rows(left, right, kept, leaving):
        width = right.shape[1]
        for i in range(2):
            m.tmp[:, 0:width] = dot(left[:, i * HALF : (i + 1) * HALF], right[...], 0, 0)
            for q in range(2):
                kept[2 * i + q] = m.tmp[ds((2 * q + c) * ROWS, ROWS, 32), 0:width]
                leaving[2 * i + q] = m.tmp[ds((2 * q + 1 - c) * ROWS, ROWS, 32), 0:width].astype(BF)

    def pair_sum(name, kept, came, base):
        for k in ORDER:
            j = chip(k)
            base[j] = (kept(j) + came[j].astype(F32)).astype(BF)
            z_start(f"{name}{k}")

    def pack(dst, at, rows):
        n = rows.shape[0]
        dst[at : at + n, :] = rows[:, :LANES].astype(BF)
        dst[at + n : at + n + n // 2, :] = jnp.concatenate(
            [rows[: n // 2, LANES:SL], rows[n // 2 :, LANES:SL]], axis=1
        ).astype(BF)

    def pair_sum_packed(name, kept, came, base):
        for k in ORDER:
            j = chip(k)
            total = kept[j] + came[j].astype(F32)
            for i in range(total.shape[1] // SLP):
                pack(base.at[j], i * PACK, total[:, i * SLP : (i + 1) * SLP])
            z_start(f"{name}{k}")

    got("gdS")
    pair_sum("zd", lambda j: m.gdo[ds(j * ROWS, ROWS, 32), :], m.gdr, m.zdb)
    got("guS")
    pair_sum("zu", lambda j: m.guo[ds((2 * j + c) * ROWS, ROWS, 32), :], m.gur, m.zub)
    scatter_combine("g2", m.pgh, m.rbg2, TOK)
    scatter_diagonal("ou", m.pout, m.rbout, TOK)
    z_mid("zd3")

    scatter_wait("g2")

    def norm_back(total, gain_row, n_ref, r_ref, i, base):
        rows = pl.ds(i, 32)
        e = total * m.gain[gain_row : gain_row + 1, :]
        n = n_ref[rows, :]
        mean_e = jnp.mean(e, axis=-1, keepdims=True)
        mean_en = jnp.mean(e * n, axis=-1, keepdims=True)
        return base + r_ref[rows, 0:1] * (e - mean_e - n * mean_en)

    for h in range(2):

        def back_two(i, h=h):
            at = pl.multiple_of(h * TOK + i, 32)
            rows = pl.ds(at, 32)
            total = m.own[rows, :] + scatter_sum(m.rbg2, TOK, h, pl.ds(i, 32))
            base = m.cot[pl.ds(pl.multiple_of(b * BLK + at, 32), 32), :].astype(F32)
            g = norm_back(total, 1, m.n2, m.r2, at, base)
            m.gresid[rows, :] = g
            m.gattn[rows, :] = g.astype(BF)

        rows_loop(TOK, 32, back_two, unroll=2)
    z_mid("zd1")

    for k, to in ((3, PD), (1, PX), (2, PY)):
        m.ggs[k - 1] = dot(m.gattn[...], m.wout[ds(chip(k) * SLP, SLP, SLP), :], 1, 1).astype(BF)
        send(f"gg{k}", m.ggs.at[k - 1], m.ggr.at[k], to)
    m.ggr[0] = dot(m.gattn[...], m.wout[ds(b * SLP, SLP, SLP), :], 1, 1).astype(BF)
    for k in range(CHIPS):
        m.tmp[0:SLP, :] = dot(m.grecv[k], m.gattn[...], 0, 0)
        m.goo[k] = m.tmp[ds(c * ROWS, ROWS, 32), :]
        m.gos[k] = m.tmp[ds((1 - c) * ROWS, ROWS, 32), :].astype(BF)
    send("goS", m.gos, m.gor, SIB)
    z_mid("zd2")
    z_end("zd3")

    gqkv = m.hid
    gres = m.h2
    sent("h2X0", "h2X1", "h2Y0", "h2Y1", "h2F0", "h2F1")

    def mix_back(k):
        j = chip(k)

        def body(i):
            at = pl.multiple_of(j * BLK + i, 16)
            rows = pl.ds(at, 16)
            gg = m.ggr[k, pl.ds(i, 16), :].astype(F32)
            sig = m.sig[rows, :]
            gm = (gg * sig).astype(BF).astype(F32)
            gqkv[rows, 0:SLP] = (
                gg * m.mixed[rows, :].astype(F32) * sig * (1.0 - sig)
            ).astype(BF)
            gnum = gm * m.rden[rows, :]
            gres[rows, 0:SLP] = gnum.astype(BF)
            gres[rows, SLP : 2 * SLP] = (-gnum * m.ratio[rows, :]).astype(BF)

        rows_loop(BLK, 16, body, unroll=2)

    mix_back(0)
    got("goS")
    for k in (1, 2, 3):
        m.po[k - 1] = (m.goo[k] + m.gor[k].astype(F32)).astype(BF)
    scatter_diagonal("wg", m.po, m.rbo, ROWS // 2)
    scatter_direct_x("wg", m.po, m.rbo, ROWS // 2)
    scatter_direct_y("wg", m.po, m.rbo, ROWS // 2)
    scatter_direct_x("ou", m.pout, m.rbout, TOK)
    scatter_direct_y("ou", m.pout, m.rbout, TOK)
    z_mid("zd0")
    z_end("zd1")
    for k in (1, 2, 3):
        got(f"gg{k}")
        mix_back(k)
    z_end("zd2")
    z_mid("zu3")
    scatter_combine("wg", m.po, m.rbo, ROWS // 2)
    m.sums[...] = dot(ones, gres[:, 0 : 2 * SLP], 1, 0)
    m.gop[...] = jnp.broadcast_to(m.sums[0:1, :], (SEQ, 2 * SLP))

    def kernel_grad(d):
        return dot(
            gres[ds(d * TOK, TOK, TOK), 0 : 2 * SLP], m.op[pl.ds(band_at(d), BAND), :], 1, 1
        )

    for k in range(CHIPS):
        m.gks[k] = kernel_grad(2 * chip(k) + 1 - c).astype(BF)
    send("gkS", m.gks, m.gkr, SIB)
    z_end("zd0")
    split_rows(m.h1, gqkv.at[:, 0:SLP], m.gqo, m.gqs)
    send("gqS", m.gqs, m.gqr, SIB)
    for k in range(CHIPS):
        m.gko[k] = kernel_grad(2 * chip(k) + c)
    z_mid("zu1")
    got("gkS")
    for k in (1, 2, 3):
        m.pk[k - 1] = (m.gko[k] + m.gkr[k].astype(F32)).astype(BF)
    scatter_diagonal("kg", m.pk, m.rbk, TOK // 2)
    scatter_direct_x("kg", m.pk, m.rbk, TOK // 2)
    scatter_direct_y("kg", m.pk, m.rbk, TOK // 2)

    def mix_t(d, carry):
        at = pl.ds(band_at(d), BAND)
        m.gop[at, :] += dot(m.kern[d], gres[ds(d * TOK, TOK, TOK), 0 : 2 * SLP], 0, 0)
        return carry

    lax.fori_loop(0, CHIPS * CORES, mix_t, 0)
    z_mid("zu2")
    z_end("zu3")

    def keys_back(i):
        rows = pl.ds(i, 16)
        gkv = m.gop[rows, 0:SLP]
        w = m.wgt[rows, :]
        gqkv[rows, SLP : 2 * SLP] = (
            (gkv * m.val[rows, :].astype(F32) + m.gop[rows, SLP : 2 * SLP]) * w
        ).astype(BF)
        gqkv[rows, 2 * SLP : 3 * SLP] = (gkv * w).astype(BF)

    rows_loop(SEQ, 16, keys_back, unroll=2)
    z_end("zu1")

    def spread(name, k, total, landing):
        if k:
            send(f"{name}{k}", total.at[chip(k)], landing.at[b], peer(k))
        else:
            local_copy(total.at[b], landing.at[b])

    sent("g20", "g21", "g22", "g23", "g24", "g25")
    for k in ORDER:
        part = dot(gqkv[blk_rows(chip(k)), :], m.wqkv[...], 1, 1)
        if k == 0:
            m.own[...] = part
        else:
            m.pgh[k - 1] = part.astype(BF)
        if k == 3:
            scatter_diagonal("g1", m.pgh, m.rbg1, TOK)
        if k == 1:
            scatter_direct_x("g1", m.pgh, m.rbg1, TOK)
        if k == 2:
            scatter_direct_y("g1", m.pgh, m.rbg1, TOK)
    z_mid("zu0")
    got("gqS")
    pair_sum_packed("zq", m.gqo, m.gqr, m.zqb)

    def scattered(dst, mine, came, buf, half):
        for h in range(2):
            rows = pl.ds(h * half, half)
            dst[rows, :] = (
                mine[0, rows, :] + came[0, rows, :].astype(F32)
                + scatter_sum(buf, half, h, pl.ds(0, half))
            ).astype(BF)

    scatter_wait("wg")
    scattered(m.zob, m.goo, m.gor, m.rbo, ROWS // 2)
    z_start("zo")
    split_rows(m.h1, gqkv.at[:, SLP : 3 * SLP], m.gvo, m.gvs)
    send("gvS", m.gvs, m.gvr, SIB)
    z_end("zu2")
    scatter_combine("kg", m.pk, m.rbk, TOK // 2)
    scatter_combine("g1", m.pgh, m.rbg1, TOK)
    z_end("zu0")
    got("gvS")
    pair_sum_packed("zv", m.gvo, m.gvr, m.zvb)
    scatter_combine("ou", m.pout, m.rbout, TOK)
    for k in ORDER:
        spread("fu", k, m.zut, gup_out)
    for k in ORDER:
        z_mid(f"zq{k}")
    z_mid("zo")
    scatter_wait("kg")
    scattered(m.zkb, m.gko, m.gkr, m.rbk, TOK // 2)
    z_start("zk")
    local_copy(m.zdt, gdn_out)

    for k in ORDER:
        z_end(f"zq{k}")
        spread("fq", k, m.zqt, gq_out)
        z_mid(f"zv{k}")
    z_end("zo")
    local_copy(m.zot, gwout_out)
    for k in ORDER:
        z_end(f"zv{k}")
        spread("fv", k, m.zvt, gv_out)
    z_mid("zk")

    scatter_wait("ou")
    for h in range(2):

        def out_rows(i, h=h):
            rows = pl.ds(pl.multiple_of(h * TOK + i, 32), 32)
            m.fout[rows, :] = (
                m.resid[rows, :] + scatter_sum(m.rbout, TOK, h, pl.ds(i, 32))
            ).astype(BF)

        rows_loop(TOK, 32, out_rows)
    send("outS", m.fout.at[other_half], out_out.at[c], SIB)
    local_copy(m.fout.at[own_half], out_out.at[c])

    scatter_wait("g1")
    for h in range(2):

        def back_one(i, h=h):
            at = pl.multiple_of(h * TOK + i, 32)
            rows = pl.ds(at, 32)
            total = m.own[rows, :] + scatter_sum(m.rbg1, TOK, h, pl.ds(i, 32))
            m.fgt[rows, :] = norm_back(total, 0, m.n1, m.r1, at, m.gresid[rows, :]).astype(BF)

        rows_loop(TOK, 32, back_one, unroll=2)
    send("gtS", m.fgt.at[other_half], gtok_out.at[c], SIB)
    local_copy(m.fgt.at[own_half], gtok_out.at[c])
    z_end("zk")
    local_copy(m.zkt, gpb_out)

    for cp in locals_:
        if all(cp is not done for done in (l_gain, l_tok, l_pb, l_wout, l_wup, l_wdn, l_cot, *l_w)):
            cp.wait()
    for name in begun:
        if name not in in_fetch:
            got(name)
            sent(name)

    @pl.when(fetch)
    def _():
        for name in in_fetch:
            sent(name)

    for name in zitems:
        z_close(name)


FIN_IN = dict(
    gq=((CHIPS, PACK, LANES), BF),
    gv=((CHIPS, 2 * PACK, LANES), BF),
    gup=((CHIPS, ROWS, FS), BF),
    gdn=((FF // (CHIPS * CORES), D), BF),
    gwout=((ROWS, D), BF),
    gpb=((TOK, BAND), BF),
    wq=((ROWS, D), BF),
    wk=((ROWS, D), BF),
    wv=((ROWS, D), BF),
    wup=((ROWS, FF), BF),
    pb=((TOK, BAND), BF),
    out=((2, TOK, D), BF),
    gtok=((2, TOK, D), BF),
)
FIN_OUT = dict(
    q=((ROWS, D), F32),
    k=((ROWS, D), F32),
    v=((ROWS, D), F32),
    o=((ROWS, D), F32),
    up=((ROWS, FF), F32),
    dn=((FF // (CHIPS * CORES), D), F32),
    bias=((TOK, SEQ), F32),
)


def finish_kernel(
    out_in, gtok_in, gq_in, gv_in, gwout_in, gup_in, gdn_in, gpb_in, ga_in, gm_in,
    wq_in, wk_in, wv_in, wup_in, pb_in,
    out_out, gtok_out, ga_out, q_out, k_out, v_out, o_out, gm_out, up_out, dn_out, bias_out,
    *scratch,
):
    m = types.SimpleNamespace(**dict(zip((*FIN_IN, *FIN_OUT), scratch)))
    in_sem, out_sem = scratch[len(FIN_IN) + len(FIN_OUT):]
    start = pl.multiple_of(
        jnp.minimum(jnp.maximum(lax.axis_index("dp") - 2, 0), 3) * LANES, LANES
    )
    stores = []

    def store(src, dst):
        stores.append(pltpu.make_async_copy(src, dst, out_sem.at[len(stores)]))
        stores[-1].start()

    sources = dict(
        gdn=gdn_in, gup=gup_in, wup=wup_in, gq=gq_in, wq=wq_in, gv=gv_in, wk=wk_in, wv=wv_in, gwout=gwout_in,
        gpb=gpb_in, pb=pb_in.at[:, pl.ds(start, BAND)], out=out_in, gtok=gtok_in,
    )
    loads = types.SimpleNamespace(
        **{
            name: pltpu.make_async_copy(src, vars(m)[name], in_sem.at[i])
            for i, (name, src) in enumerate(sources.items())
        }
    )
    for cp in vars(loads).values():
        cp.start()

    loads.gdn.wait()
    m.dn[...] = m.gdn[...].astype(F32)
    store(m.dn, dn_out)

    def as_row(column, gain):
        square = jnp.broadcast_to(column, (ROWS, LANES))
        return jnp.transpose(square)[0:1, :] / gain[...].astype(F32)

    loads.gup.wait()
    loads.wup.wait()
    column = jnp.zeros((ROWS, 1), F32)
    for j in range(CHIPS):
        cols = slice(j * FS, (j + 1) * FS)
        g = m.gup[j].astype(F32)
        m.up[:, cols] = g
        column += jnp.sum(g * m.wup[:, cols].astype(F32), axis=1, keepdims=True)
    store(m.up, up_out)
    gm_out[...] = as_row(column, gm_in)

    def unpack(ref, j, at):
        low = ref[j, at : at + ROWS, :].astype(F32)
        high = ref[j, at + ROWS : at + PACK, :].astype(F32)
        rest = SL - LANES
        return jnp.concatenate(
            [low, jnp.concatenate([high[:, :rest], high[:, rest:]], axis=0)], axis=1
        )

    column = jnp.zeros((ROWS, 1), F32)
    for needs, ref, at, w, mine, dst in (
        ((loads.gq, loads.wq), m.gq, 0, m.wq, m.q, q_out),
        ((loads.gv, loads.wk), m.gv, 0, m.wk, m.k, k_out),
        ((loads.wv,), m.gv, PACK, m.wv, m.v, v_out),
    ):
        for cp in needs:
            cp.wait()
        g = jnp.concatenate([unpack(ref, j, at) for j in range(CHIPS)], axis=1)
        mine[...] = g
        store(mine, dst)
        column += jnp.sum(g * w[...].astype(F32), axis=1, keepdims=True)
    ga_out[...] = as_row(column, ga_in)

    loads.gwout.wait()
    m.o[...] = m.gwout[...].astype(F32)
    store(m.o, o_out)
    loads.gpb.wait()
    loads.pb.wait()
    t_ids = lax.axis_index("dp") * TOK + lax.broadcasted_iota(jnp.int32, (TOK, BAND), 0)
    u_ids = start + lax.broadcasted_iota(jnp.int32, (TOK, BAND), 1)
    m.bias[...] = jnp.zeros((TOK, SEQ), F32)
    m.bias[:, pl.ds(start, BAND)] = jnp.where(
        jnp.abs(t_ids - u_ids) < WIN, m.gpb[...].astype(F32) * jnp.exp(m.pb[...].astype(F32)), 0.0
    )
    store(m.bias, bias_out)
    loads.out.wait()
    store(m.out, out_out)
    loads.gtok.wait()
    store(m.gtok, gtok_out)
    for cp in stores:
        cp.wait()


def plane_program(
    tokens, lengths, cotangent, gain_attn, w_query, w_key, w_value, w_out, gain_mlp, w_up, w_down, pos_bias
):
    gains = jnp.pad(jnp.stack([gain_attn, gain_mlp]), ((0, 14), (0, LANES - ROWS)))
    anywhere = pl.BlockSpec(memory_space=pl.ANY)
    struct = jax.ShapeDtypeStruct
    results = pl.pallas_call(
        plane_kernel,
        out_shape=(
            struct((2, TOK, D), BF),
            struct((2, TOK, D), BF),
            struct((CHIPS, PACK, LANES), BF),
            struct((CHIPS, 2 * PACK, LANES), BF),
            struct((ROWS, D), BF),
            struct((CHIPS, ROWS, FS), BF),
            struct((CHIPS, ROWS, D), BF),
            struct((TOK, BAND), BF),
        ),
        in_specs=[anywhere, pl.BlockSpec(memory_space=pltpu.SMEM)] + [anywhere] * 9,
        out_specs=(anywhere,) * 8,
        scratch_shapes=[pltpu.VMEM(shape, kind) for shape, kind in SCRATCH.values()]
        + [
            pltpu.SemaphoreType.DMA((N_REMOTE,)),
            pltpu.SemaphoreType.DMA((N_REMOTE,)),
            pltpu.SemaphoreType.DMA((N_LOCAL,)),
        ],
        compiler_params=pltpu.CompilerParams(
            collective_id=0, has_side_effects=True, vmem_limit_bytes=VMEM_BYTES
        ),
        cost_estimate=pl.CostEstimate(
            flops=15_000_000_000, bytes_accessed=8_000_000, transcendentals=4_000_000
        ),
        name="aft_layer",
    )(
        tokens.reshape(2, TOK, D), lengths.reshape(2), cotangent.reshape(2, TOK, D), gains,
        w_query, w_key, w_value, w_out, w_up, w_down, pos_bias,
    )
    out, gtok, gq, gv, gwout, gup, gdn, gpb = results
    whole = pl.BlockSpec(memory_space=pltpu.VMEM)
    f32_out = [struct(shape, kind) for shape, kind in FIN_OUT.values()]
    row = struct((1, ROWS), F32)
    out, gtok, grad_gain_a, grad_q, grad_k, grad_v, grad_o, grad_gain_m, grad_up, grad_down, grad_bias = (
        pl.pallas_call(
            finish_kernel,
            out_shape=(struct((2, TOK, D), BF),) * 2 + (row, *f32_out[:4], row, *f32_out[4:]),
            in_specs=[anywhere] * 8 + [whole] * 2 + [anywhere] * 5,
            out_specs=(anywhere, anywhere, whole) + (anywhere,) * 4 + (whole,) + (anywhere,) * 3,
            scratch_shapes=[pltpu.VMEM(shape, kind) for shape, kind in (*FIN_IN.values(), *FIN_OUT.values())]
            + [pltpu.SemaphoreType.DMA((len(FIN_IN),)), pltpu.SemaphoreType.DMA((len(FIN_OUT) + 2,))],
            compiler_params=pltpu.CompilerParams(vmem_limit_bytes=VMEM_BYTES),
            cost_estimate=pl.CostEstimate(flops=4_000_000, bytes_accessed=9_000_000, transcendentals=100_000),
            name="gradients_out",
        )(
            out, gtok, gq, gv, gwout, gup, gdn.reshape(FF // (CHIPS * CORES), D), gpb,
            gain_attn.reshape(1, ROWS), gain_mlp.reshape(1, ROWS),
            w_query, w_key, w_value, w_up, pos_bias,
        )
    )
    return (
        out.reshape(tokens.shape),
        gtok.reshape(tokens.shape),
        grad_gain_a.reshape(ROWS),
        grad_q,
        grad_k,
        grad_v,
        grad_o,
        grad_gain_m.reshape(ROWS),
        grad_up,
        grad_down,
        grad_bias,
    )


def solution(mesh):
    in_specs = (
        P(None, "pipe", "dp", None),
        P(None, "pipe", None),
        P(None, "pipe", "dp", None),
        P("dp"),
        P("dp", None),
        P("dp", None),
        P("dp", None),
        P("dp", None),
        P("dp"),
        P("dp", None),
        P("dp", None),
        P("dp", None),
    )
    out_specs = (
        P(None, "pipe", "dp", None),
        P(None, "pipe", "dp", None),
        P("dp"),
        P("dp", None),
        P("dp", None),
        P("dp", None),
        P("dp", None),
        P("dp"),
        P("dp", None),
        P("dp", None),
        P("dp", None),
    )
    fits = mesh.shape["dp"] == CHIPS * CORES and mesh.shape["pipe"] == DEPTH
    return jax.shard_map(plane_program if fits else local, mesh=mesh, in_specs=in_specs, out_specs=out_specs, check_vma=False)
```

```python
import types

import jax
import jax.numpy as jnp
from jax import lax
from jax.experimental import pallas as pl
from jax.experimental.pallas import tpu as pltpu
from jax.sharding import PartitionSpec as P

D = 768
FF = 3072
SEQ = 1024
WIN = 256


EPSILON = 1e-05
GELU_SCALE = 0.7978845608028654
GELU_CUBE = 0.044715
VMEM_BYTES = 63 * 2**20


def normalize(values, gain):
    centre = values - jnp.mean(values, axis=-1, keepdims=True)
    spread = jnp.mean(centre * centre, axis=-1, keepdims=True)
    return centre * lax.rsqrt(spread + EPSILON) * gain


def gelu_tanh(values):
    return jax.nn.gelu(values, approximate=True)


def band_ones(width):
    row_ids = jnp.arange(width)[:, None]
    col_ids = jnp.arange(3 * width)[None, :]
    return (jnp.abs(col_ids - width - row_ids) < width).astype(jnp.float32)


def band_blocks(bias, width):
    length = bias.shape[0]
    padded = jnp.pad(bias, ((0, 0), (width, width)))
    return jnp.stack(
        [
            padded[block * width : (block + 1) * width, block * width : block * width + 3 * width]
            for block in range(length // width)
        ]
    )


def windows(operand, width):
    blocks = operand.shape[0] // width
    padded = jnp.pad(operand, ((width, width), (0, 0))).reshape(blocks + 2, width, operand.shape[1])
    return jnp.concatenate([padded[:-2], padded[1:-1], padded[2:]], axis=1)


def unwindow(grad_windows, width):
    blocks = grad_windows.shape[0]
    leading = jnp.pad(grad_windows[:, :width], ((0, 2), (0, 0), (0, 0)))
    middle = jnp.pad(grad_windows[:, width : 2 * width], ((1, 1), (0, 0), (0, 0)))
    trailing = jnp.pad(grad_windows[:, 2 * width :], ((2, 0), (0, 0), (0, 0)))
    summed = leading + middle + trailing
    return summed[1:-1].reshape(blocks * width, grad_windows.shape[2])


def to_columns(matrix, seq_count, length):
    channels = matrix.shape[1]
    return (
        matrix.reshape(seq_count, length, channels)
        .transpose(1, 0, 2)
        .reshape(length, seq_count * channels)
    )


def from_columns(matrix, seq_count, length):
    channels = matrix.shape[1] // seq_count
    return (
        matrix.reshape(length, seq_count, channels)
        .transpose(1, 0, 2)
        .reshape(seq_count * length, channels)
    )


def outer_sum(left, right):
    return lax.dot_general(
        left, right, (((0,), (0,)), ((), ())), preferred_element_type=jnp.float32
    )


def times_transpose(left, right):
    return lax.dot_general(
        left, right, (((1,), (1,)), ((), ())), preferred_element_type=jnp.float32
    )


def local(
    tokens,
    lengths,
    cotangent,
    gain_attn,
    w_query,
    w_key,
    w_value,
    w_out,
    gain_mlp,
    w_up,
    w_down,
    pos_bias,
):
    gathered = (
        lax.all_gather(gain_attn, "dp", axis=0, tiled=True),
        lax.all_gather(w_query, "dp", axis=0, tiled=True),
        lax.all_gather(w_key, "dp", axis=0, tiled=True),
        lax.all_gather(w_value, "dp", axis=0, tiled=True),
        lax.all_gather(w_out, "dp", axis=0, tiled=True),
        lax.all_gather(gain_mlp, "dp", axis=0, tiled=True),
        lax.all_gather(w_up, "dp", axis=0, tiled=True),
        lax.all_gather(w_down, "dp", axis=0, tiled=True),
        lax.all_gather(pos_bias, "dp", axis=0, tiled=True),
    )
    gain_a = gathered[0].astype(jnp.float32)
    query_w, key_w, value_w, out_w = (gathered[1], gathered[2], gathered[3], gathered[4])
    gain_m = gathered[5].astype(jnp.float32)
    up_w, down_w = (gathered[6], gathered[7])
    bias_full = gathered[8].astype(jnp.float32)
    group_size = lax.axis_size("dp")
    tok_rows = tokens.shape[2]
    seq_count = group_size * tok_rows // SEQ
    band_mask = band_ones(WIN)
    bias_blocks = jnp.exp(band_blocks(bias_full, WIN))
    exp_band = bias_blocks * band_mask
    kernel = ((bias_blocks - 1.0) * band_mask).astype(jnp.bfloat16)
    positions = jnp.arange(SEQ)
    grad_gain_a = jnp.zeros((D,), jnp.float32)
    grad_gain_m = jnp.zeros((D,), jnp.float32)
    grad_query_w = jnp.zeros((D, D), jnp.float32)
    grad_key_w = jnp.zeros((D, D), jnp.float32)
    grad_value_w = jnp.zeros((D, D), jnp.float32)
    grad_out_w = jnp.zeros((D, D), jnp.float32)
    grad_up_w = jnp.zeros((D, FF), jnp.float32)
    grad_down_w = jnp.zeros((FF, D), jnp.float32)
    grad_kernel = jnp.zeros(exp_band.shape, jnp.float32)
    outputs_list = []
    grads_in_list = []
    for micro in range(tokens.shape[0]):
        inputs_f = tokens[micro, 0].astype(jnp.float32)
        normed_f, norm_back_a = jax.vjp(normalize, inputs_f, gain_a)
        normed = normed_f.astype(jnp.bfloat16)
        query = jnp.dot(normed, query_w, preferred_element_type=jnp.float32)
        keys = jnp.dot(normed, key_w, preferred_element_type=jnp.float32).astype(jnp.bfloat16)
        values = jnp.dot(normed, value_w, preferred_element_type=jnp.float32).astype(jnp.bfloat16)
        key_chan, value_chan = (
            lax.all_to_all(keys, "dp", split_axis=1, concat_axis=0, tiled=True),
            lax.all_to_all(values, "dp", split_axis=1, concat_axis=0, tiled=True),
        )
        seq_lengths = lengths[micro, 0]
        channels = key_chan.shape[1]
        valid_seq = (positions[:, None] < seq_lengths[None, :]).astype(jnp.float32)
        valid_cols = jnp.broadcast_to(valid_seq[:, :, None], (SEQ, seq_count, channels)).reshape(
            SEQ, seq_count * channels
        )
        key_cols = to_columns(key_chan, seq_count, SEQ).astype(jnp.float32)
        value_cols = to_columns(value_chan, seq_count, SEQ).astype(jnp.float32)
        weighted = jnp.exp(key_cols) * valid_cols
        col_count = weighted.shape[1]
        operand = jnp.concatenate(
            [(weighted * value_cols).astype(jnp.bfloat16), weighted.astype(jnp.bfloat16)], axis=1
        )
        windowed = windows(operand, WIN)
        banded = jnp.einsum(
            "nqk,nkc->nqc", kernel, windowed, preferred_element_type=jnp.float32
        ).reshape(SEQ, 2 * col_count)
        result = banded + jnp.sum(operand, axis=0, dtype=jnp.float32)[None, :]
        numerator = result[:, :col_count]
        denominator = result[:, col_count:] + 1.0 - valid_cols
        mixed_cols = numerator / denominator * valid_cols
        mixed_tok = lax.all_to_all(
            from_columns(mixed_cols.astype(jnp.bfloat16), seq_count, SEQ),
            "dp",
            split_axis=0,
            concat_axis=1,
            tiled=True,
        )
        sigmoid_q = jax.nn.sigmoid(query)
        mixed_f = mixed_tok.astype(jnp.float32)
        gated = (sigmoid_q * mixed_f).astype(jnp.bfloat16)
        resid = inputs_f + jnp.dot(gated, out_w, preferred_element_type=jnp.float32)
        normed_two_f, norm_back_m = jax.vjp(normalize, resid, gain_m)
        normed_two = normed_two_f.astype(jnp.bfloat16)
        upper = jnp.dot(normed_two, up_w, preferred_element_type=jnp.float32)
        hidden_f, gelu_back = jax.vjp(gelu_tanh, upper)
        hidden = hidden_f.astype(jnp.bfloat16)
        outputs_list.append(
            (resid + jnp.dot(hidden, down_w, preferred_element_type=jnp.float32)).astype(
                jnp.bfloat16
            )
        )
        grad_out = cotangent[micro, 0]
        grad_down_w = grad_down_w + outer_sum(hidden, grad_out)
        grad_hidden = times_transpose(grad_out, down_w)
        grad_upper = gelu_back(grad_hidden)[0].astype(jnp.bfloat16)
        grad_up_w = grad_up_w + outer_sum(normed_two, grad_upper)
        grad_normed_two = times_transpose(grad_upper, up_w)
        grad_resid_norm, grad_gain_part_m = norm_back_m(grad_normed_two)
        grad_gain_m = grad_gain_m + grad_gain_part_m
        grad_resid = grad_out.astype(jnp.float32) + grad_resid_norm
        grad_attn = grad_resid.astype(jnp.bfloat16)
        grad_out_w = grad_out_w + outer_sum(gated, grad_attn)
        grad_gated = times_transpose(grad_attn, out_w)
        grad_mixed = (grad_gated * sigmoid_q).astype(jnp.bfloat16)
        grad_query = (grad_gated * mixed_f * sigmoid_q * (1.0 - sigmoid_q)).astype(jnp.bfloat16)
        grad_mixed_chan = lax.all_to_all(grad_mixed, "dp", split_axis=1, concat_axis=0, tiled=True)
        grad_mixed_cols = to_columns(grad_mixed_chan, seq_count, SEQ).astype(jnp.float32)
        grad_numerator = grad_mixed_cols * valid_cols / denominator
        grad_denominator = -grad_numerator * (numerator / denominator)
        grad_flat = jnp.concatenate(
            [grad_numerator.astype(jnp.bfloat16), grad_denominator.astype(jnp.bfloat16)], axis=1
        )
        grad_result = grad_flat.reshape(SEQ // WIN, WIN, 2 * col_count)
        grad_windowed = jnp.einsum(
            "nqk,nqc->nkc", kernel, grad_result, preferred_element_type=jnp.float32
        )
        grad_kernel = grad_kernel + jnp.einsum(
            "nqc,nkc->nqk", grad_result, windowed, preferred_element_type=jnp.float32
        )
        grad_operand = (
            unwindow(grad_windowed, WIN) + jnp.sum(grad_flat, axis=0, dtype=jnp.float32)[None, :]
        )
        grad_key_value = grad_operand[:, :col_count]
        grad_key_weight = grad_operand[:, col_count:]
        grad_keys_cols = (grad_key_value * value_cols + grad_key_weight) * weighted
        grad_values_cols = grad_key_value * weighted
        grad_keys, grad_values = (
            lax.all_to_all(
                from_columns(grad_keys_cols.astype(jnp.bfloat16), seq_count, SEQ),
                "dp",
                split_axis=0,
                concat_axis=1,
                tiled=True,
            ),
            lax.all_to_all(
                from_columns(grad_values_cols.astype(jnp.bfloat16), seq_count, SEQ),
                "dp",
                split_axis=0,
                concat_axis=1,
                tiled=True,
            ),
        )
        grad_query_w = grad_query_w + outer_sum(normed, grad_query)
        grad_key_w = grad_key_w + outer_sum(normed, grad_keys)
        grad_value_w = grad_value_w + outer_sum(normed, grad_values)
        grad_normed = (
            times_transpose(grad_query, query_w)
            + times_transpose(grad_keys, key_w)
            + times_transpose(grad_values, value_w)
        )
        grad_input_norm, grad_gain_part_a = norm_back_a(grad_normed)
        grad_gain_a = grad_gain_a + grad_gain_part_a
        grads_in_list.append((grad_resid + grad_input_norm).astype(jnp.bfloat16))
    grad_kernel_bias = grad_kernel * exp_band
    grad_bias_pad = jnp.zeros((SEQ, SEQ + 2 * WIN), jnp.float32)
    for block in range(SEQ // WIN):
        grad_bias_pad = grad_bias_pad.at[
            block * WIN : (block + 1) * WIN, block * WIN : block * WIN + 3 * WIN
        ].add(grad_kernel_bias[block])
    grad_bias = grad_bias_pad[:, WIN : WIN + SEQ]
    shares = (
        lax.psum_scatter(grad_gain_a, "dp", scatter_dimension=0, tiled=True),
        lax.psum_scatter(grad_query_w, "dp", scatter_dimension=0, tiled=True),
        lax.psum_scatter(grad_key_w, "dp", scatter_dimension=0, tiled=True),
        lax.psum_scatter(grad_value_w, "dp", scatter_dimension=0, tiled=True),
        lax.psum_scatter(grad_out_w, "dp", scatter_dimension=0, tiled=True),
        lax.psum_scatter(grad_gain_m, "dp", scatter_dimension=0, tiled=True),
        lax.psum_scatter(grad_up_w, "dp", scatter_dimension=0, tiled=True),
        lax.psum_scatter(grad_down_w, "dp", scatter_dimension=0, tiled=True),
        lax.psum_scatter(grad_bias, "dp", scatter_dimension=0, tiled=True),
    )
    reduced = lax.psum(
        (
            shares[0],
            shares[1],
            shares[2],
            shares[3],
            shares[4],
            shares[5],
            shares[6],
            shares[7],
            shares[8],
        ),
        "pipe",
    )
    final_grads = (
        reduced[0],
        reduced[1],
        reduced[2],
        reduced[3],
        reduced[4],
        reduced[5],
        reduced[6],
        reduced[7],
        reduced[8],
    )
    output = jnp.stack(outputs_list)[:, None]
    grad_tokens = jnp.stack(grads_in_list)[:, None]
    return (
        output,
        grad_tokens,
        final_grads[0],
        final_grads[1],
        final_grads[2],
        final_grads[3],
        final_grads[4],
        final_grads[5],
        final_grads[6],
        final_grads[7],
        final_grads[8],
    )


CHIPS = 4
CORES = 2
DEPTH = 4
LANES = 128
TOK = 128
BLK = CORES * TOK
ROWS = D // (CHIPS * CORES)
SL = D // CHIPS
SLP = -(-SL // LANES) * LANES
FS = FF // CHIPS
BAND = 5 * LANES
HALF = D // 2
PACK = ROWS + ROWS // 2
MESH_ID = pl.DeviceIdType.MESH
F32 = jnp.float32
BF = jnp.bfloat16

SCRATCH = dict(
    tok=((BLK, D), BF),
    cot=((SEQ, D), BF),
    gains=((CHIPS * CORES, 16, LANES), BF),
    gain=((16, D), F32),
    wst=((3, ROWS, D), BF),
    wqs=((CHIPS, ROWS, 3 * SLP), BF),
    wqkv=((D, 3 * SLP), BF),
    wout=((CHIPS * SLP, D), BF),
    wup=((D, FS), BF),
    wdn=((FS, D), BF),
    pbw=((TOK, BAND), BF),
    kern=((CHIPS * CORES, TOK, BAND), BF),
    h1=((SEQ, D), BF),
    h2=((SEQ, D), BF),
    n1=((BLK, D), F32),
    r1=((BLK, LANES), F32),
    n2=((BLK, D), F32),
    r2=((BLK, LANES), F32),
    tmp=((HALF, D), F32),
    tmix=((TOK, 2 * SLP), F32),
    sums=((8, 2 * SLP), F32),
    sig=((SEQ, SLP), F32),
    wgt=((SEQ, SLP), F32),
    val=((SEQ, SLP), BF),
    op=((SEQ, 2 * SLP), BF),
    ratio=((SEQ, SLP), F32),
    rden=((SEQ, SLP), F32),
    mixed=((SEQ, SLP), BF),
    gated=((SEQ, SLP), BF),
    grecv=((CHIPS, BLK, SLP), BF),
    ghs=((CHIPS, TOK, LANES), BF),
    ghr=((CHIPS - 1, TOK, LANES), BF),
    gghs=((CHIPS - 1, TOK, LANES), BF),
    gghr=((CHIPS - 1, TOK, LANES), BF),
    resid=((BLK, D), F32),
    hid=((SEQ, FS), BF),
    dge=((3 * BLK, FS), F32),
    gop=((SEQ, 2 * SLP), F32),
    gupr=((SEQ, FS), BF),
    pout=((CHIPS - 1, BLK, D), BF),
    pgh=((CHIPS - 1, BLK, D), BF),
    own=((BLK, D), F32),
    rbout=((6, TOK, D), BF),
    rbg2=((6, TOK, D), BF),
    rbg1=((6, TOK, D), BF),
    gresid=((BLK, D), F32),
    gattn=((BLK, D), BF),
    ggs=((CHIPS - 1, BLK, LANES), BF),
    ggr=((CHIPS, BLK, SLP), BF),
    gdo=((HALF, D), F32),
    gdx=((HALF, D), F32),
    gds=((CHIPS, ROWS, D), BF),
    gdr=((CHIPS, ROWS, D), BF),
    guo=((D, FS), F32),
    gus=((CHIPS, ROWS, FS), BF),
    gur=((CHIPS, ROWS, FS), BF),
    gqo=((CHIPS, ROWS, SLP), F32),
    gqs=((CHIPS, ROWS, SLP), BF),
    gqr=((CHIPS, ROWS, SLP), BF),
    gvo=((CHIPS, ROWS, 2 * SLP), F32),
    gvs=((CHIPS, ROWS, 2 * SLP), BF),
    gvr=((CHIPS, ROWS, 2 * SLP), BF),
    goo=((CHIPS, ROWS, D), F32),
    gos=((CHIPS, ROWS, D), BF),
    gor=((CHIPS, ROWS, D), BF),
    po=((CHIPS - 1, ROWS, D), BF),
    rbo=((6, ROWS // 2, D), BF),
    gko=((CHIPS, TOK, BAND), F32),
    gks=((CHIPS, TOK, BAND), BF),
    gkr=((CHIPS, TOK, BAND), BF),
    pk=((CHIPS - 1, TOK, BAND), BF),
    rbk=((6, TOK // 2, BAND), BF),
    zdb=((CHIPS, ROWS, D), BF),
    zdr=((CHIPS, ROWS, D), BF),
    zdt=((CHIPS, ROWS, D), BF),
    zub=((CHIPS, ROWS, FS), BF),
    zur=((CHIPS, ROWS, FS), BF),
    zut=((CHIPS, ROWS, FS), BF),
    zqb=((CHIPS, PACK, LANES), BF),
    zqr=((CHIPS, PACK, LANES), BF),
    zqt=((CHIPS, PACK, LANES), BF),
    zvb=((CHIPS, 2 * PACK, LANES), BF),
    zvr=((CHIPS, 2 * PACK, LANES), BF),
    zvt=((CHIPS, 2 * PACK, LANES), BF),
    zob=((ROWS, D), BF),
    zor=((ROWS, D), BF),
    zot=((ROWS, D), BF),
    zkb=((TOK, BAND), BF),
    zkr=((TOK, BAND), BF),
    zkt=((TOK, BAND), BF),
    fout=((BLK, D), BF),
    fgt=((BLK, D), BF),
)
POLLS = {
    1: "d3", 2: "d1", 4: "d2 D3", 6: "d0 D1", 9: "D2", 11: "u3", 13: "D0", 15: "u1", 16: "u2 U3", 23: "u0 U1",
    25: "U2", 27: "U0", 28: "q3 q1 q2 q0 o", 29: "Q3 v3 Q1 v1 Q2 v2 Q0 v0 O V3 V1 V2 V0 k", 31: "K",
}
N_REMOTE = 200
N_LOCAL = 40


def dot(left, right, left_dim, right_dim):
    return lax.dot_general(
        left, right, (((left_dim,), (right_dim,)), ((), ())), preferred_element_type=F32
    )


def rows_loop(count, step, body, unroll=1):
    def one(i, carry):
        body(pl.multiple_of(i * step, step))
        return carry

    lax.fori_loop(0, count // step, one, 0, unroll=unroll)


def plane_kernel(
    tok_in, len_in, cot_in, ga_in, gm_in, wq_in, wk_in, wv_in, wout_in, wup_in, wdn_in, pb_in,
    out_out, gtok_out, gq_out, gv_out, gwout_out, gup_out, gdn_out, gpb_out,
    *scratch,
):
    m = types.SimpleNamespace(**dict(zip(SCRATCH, scratch)))
    send_sem, recv_sem, local_sem = scratch[len(SCRATCH):]
    r = lax.axis_index("dp")
    z = lax.axis_index("pipe")
    c = lax.rem(r, 2)
    x = lax.rem(r // 2, 2)
    y = r // 4
    b = r // 2
    length = len_in[c]

    def chip(k):
        return 2 * (1 - y if k // 2 else y) + (1 - x if k % 2 else x)

    def peer(k, other=0):
        return (2 * chip(k) + (1 - c if other else c), z)

    jx, jy, jd = chip(1), chip(2), chip(3)
    SIB, PX, PY, PD = peer(0, 1), peer(1), peer(2), peer(3)
    z_near = z + 1 - 2 * lax.rem(z, 2)
    z_far = 3 - z
    ZN, ZF = (r, z_near), (r, z_far)
    outer = z * (3 - z) == 0
    inner = z * (3 - z) != 0

    remote, locals_ = {}, []
    waited = set()
    begun = []

    def make(name, src, dst, to):
        assert name not in remote, name
        i = len(remote)
        cp = pltpu.make_async_remote_copy(
            src_ref=src, dst_ref=dst, send_sem=send_sem.at[i], recv_sem=recv_sem.at[i],
            device_id=to, device_id_type=MESH_ID,
        )
        remote[name] = cp
        return cp

    def send(name, src, dst, to):
        make(name, src, dst, to)
        start(name)

    def start(*names):
        for name in names:
            begun.append(name)
            remote[name].start()

    def got(*names):
        for name in names:
            if name not in waited:
                waited.add(name)
                remote[name].wait_recv()

    def sent(*names):
        for name in names:
            if name + "/s" not in waited:
                waited.add(name + "/s")
                remote[name].wait_send()

    def local_copy(src, dst):
        cp = pltpu.make_async_copy(src, dst, local_sem.at[len(locals_)])
        locals_.append(cp)
        cp.start()
        return cp

    def ds(start, size, unit):
        return pl.ds(pl.multiple_of(start, unit), size)

    def band_at(d):
        return pl.multiple_of(jnp.minimum(jnp.maximum(d - 2, 0), 3) * LANES, LANES)

    def gather_open(name, blk):
        make(name + "X0", blk(b, 0), blk(b, 0), PX)
        make(name + "Y1", blk(b, 1), blk(b, 1), PY)
        make(name + "X1", blk(b, 1), blk(b, 1), PX)
        make(name + "Y0", blk(b, 0), blk(b, 0), PY)
        make(name + "F0", blk(jx, 0), blk(jx, 0), PY)
        make(name + "F1", blk(jy, 1), blk(jy, 1), PX)

    def gather_start(name):
        start(name + "X0", name + "Y1", name + "X1", name + "Y0")

    def gather_forward(name):
        got(name + "X0")
        start(name + "F0")
        got(name + "Y1")
        start(name + "F1")

    def gather_wait(name, k):
        got(*{1: (name + "X0", name + "X1"), 2: (name + "Y0", name + "Y1"), 3: (name + "F0", name + "F1")}[k])

    fetch = lax.rem(z, 2) == c
    passed = lax.rem(z, 2) != c
    in_fetch = []

    def relay_open(name, place):
        for k in (1, 2, 3):
            make(f"{name}Z{k}", place(k), place(k), ZN)
            in_fetch.append(f"{name}Z{k}")

    def relay(name, place, arrive):
        for k in (1, 2, 3):

            @pl.when(fetch)
            def _(k=k):
                arrive(k)
                start(f"{name}Z{k}")

            @pl.when(passed)
            def _(k=k):
                remote[f"{name}Z{k}"].wait_recv()

            waited.add(f"{name}Z{k}")
            send(f"{name}S{k}", place(k), place(k), SIB)

    def scatter_diagonal(name, part, buf, half):
        send(name + "0", part.at[2, pl.ds(half, half)], buf.at[0], PX)
        send(name + "1", part.at[2, pl.ds(0, half)], buf.at[1], PY)

    def scatter_direct_x(name, part, buf, half):
        send(name + "2", part.at[0, pl.ds(half, half)], buf.at[2], PX)

    def scatter_direct_y(name, part, buf, half):
        send(name + "3", part.at[1, pl.ds(0, half)], buf.at[3], PY)

    def scatter_combine(name, part, buf, half):
        got(name + "1")
        part[0, pl.ds(0, half), :] = (
            part[0, pl.ds(0, half), :].astype(F32) + buf[1].astype(F32)
        ).astype(BF)
        send(name + "4", part.at[0, pl.ds(0, half)], buf.at[4], PX)
        got(name + "0")
        part[1, pl.ds(half, half), :] = (
            part[1, pl.ds(half, half), :].astype(F32) + buf[0].astype(F32)
        ).astype(BF)
        send(name + "5", part.at[1, pl.ds(half, half)], buf.at[5], PY)

    def scatter_wait(name):
        got(name + "2", name + "3", name + "4", name + "5")

    def scatter_sum(buf, half, h, rows):
        if h == 0:
            return buf[3, rows, :].astype(F32) + buf[4, rows, :].astype(F32)
        return buf[2, rows, :].astype(F32) + buf[5, rows, :].astype(F32)

    zitems = {}

    def z_open(name, base, near, total):
        zitems[name] = (
            base,
            near,
            total,
            make(name + "a", base, near, ZN),
            make(name + "b", base, total, ZF),
            make(name + "c", total, total, ZN),
        )

    def z_start(name):
        item = zitems[name]

        @pl.when(outer)
        def _():
            item[3].start()

    def z_mid(name):
        base, near, total, into, across, back = zitems[name]

        @pl.when(inner)
        def _():
            into.wait_recv()
            base[...] = (base[...].astype(F32) + near[...].astype(F32)).astype(BF)
            across.start()

    def z_end(name):
        base, near, total, into, across, back = zitems[name]

        @pl.when(inner)
        def _():
            across.wait_recv()
            total[...] = (base[...].astype(F32) + total[...].astype(F32)).astype(BF)
            back.start()

        @pl.when(outer)
        def _():
            back.wait_recv()

    def z_close(name):
        base, near, total, into, across, back = zitems[name]

        @pl.when(outer)
        def _():
            into.wait_send()

        @pl.when(inner)
        def _():
            across.wait_send()
            back.wait_send()

    for k in range(CHIPS):
        j = chip(k)
        z_open(f"zd{k}", m.zdb.at[j], m.zdr.at[j], m.zdt.at[j])
        z_open(f"zu{k}", m.zub.at[j], m.zur.at[j], m.zut.at[j])
        z_open(f"zq{k}", m.zqb.at[j], m.zqr.at[j], m.zqt.at[j])
        z_open(f"zv{k}", m.zvb.at[j], m.zvr.at[j], m.zvt.at[j])
    z_open("zo", m.zob, m.zor, m.zot)
    z_open("zk", m.zkb, m.zkr, m.zkt)
    ORDER = (3, 1, 2, 0)

    def spread(name, k, total, landing):
        if k:
            send(f"{name}{k}", total.at[chip(k)], landing.at[b], peer(k))
        else:
            local_copy(total.at[b], landing.at[b])

    def poll(place):
        for step in POLLS.get(place, "").split():
            name = "z" + step.lower()
            if step.islower():
                z_mid(name)
                continue
            z_end(name)
            which, k = step[0], chip(int(step[1:] or 0))
            if which == "D":
                local_copy(m.zdt.at[k], gdn_out.at[k])
            elif which == "U":
                spread("fu", int(step[1]), m.zut, gup_out)
            elif which == "Q":
                spread("fq", int(step[1]), m.zqt, gq_out)
            elif which == "V":
                spread("fv", int(step[1]), m.zvt, gv_out)
            elif which == "O":
                local_copy(m.zot, gwout_out)
            else:
                local_copy(m.zkt, gpb_out)

    own_half = ds(c * TOK, TOK, TOK)
    other_half = ds((1 - c) * TOK, TOK, TOK)
    l_tok = local_copy(tok_in.at[c], m.tok.at[own_half])
    l_w = [local_copy(w, m.wst.at[i]) for i, w in enumerate((wq_in, wk_in, wv_in))]
    l_pb = local_copy(pb_in.at[:, ds(band_at(r), BAND, LANES)], m.pbw)

    def wout_rows(j, core):
        return m.wout.at[ds(j * SLP + core * ROWS, ROWS, 32)]

    l_wout = local_copy(wout_in, wout_rows(b, c))
    up_rows = ds(r * ROWS, ROWS, 32)
    l_wup = local_copy(wup_in.at[:, ds(b * FS, FS, LANES)], m.wup.at[up_rows])
    dn_rows = ds(c * HALF, HALF, LANES)
    l_wdn = local_copy(wdn_in, m.wdn.at[dn_rows])
    cot_half = ds(b * BLK + c * TOK, TOK, TOK)
    l_cot = local_copy(cot_in.at[c], m.cot.at[cot_half])

    line = lax.broadcasted_iota(jnp.int32, (16, LANES), 0)
    fill = jnp.zeros((1, LANES - ROWS), F32)
    both_gains = [
        jnp.broadcast_to(jnp.concatenate([g[...].astype(F32), fill], axis=1), (16, LANES)) for g in (ga_in, gm_in)
    ]
    m.gains[r] = jnp.where(line == 0, both_gains[0], both_gains[1]).astype(BF)

    barrier = pltpu.get_barrier_semaphore()
    everyone = [peer(k, o) for k in range(CHIPS) for o in range(CORES) if (k, o) != (0, 0)] + [ZN, ZF]
    for other in everyone:
        pl.semaphore_signal(barrier, inc=1, device_id=other, device_id_type=MESH_ID)
    l_pb.wait()
    t_ids = r * TOK + lax.broadcasted_iota(jnp.int32, (TOK, BAND), 0)
    u_ids = band_at(r) + lax.broadcasted_iota(jnp.int32, (TOK, BAND), 1)
    in_band = jnp.abs(t_ids - u_ids) < WIN
    m.kern[r] = jnp.where(in_band, jnp.exp(m.pbw[...].astype(F32)) - 1.0, 0.0).astype(BF)

    for cp in l_w:
        cp.wait()
    for i in range(3):
        w_rows = m.wst[i].astype(F32)
        for j in range(CHIPS):
            piece = w_rows[:, j * SL : (j + 1) * SL]
            m.wqs[j, :, i * SLP : (i + 1) * SLP] = jnp.concatenate(
                [piece, jnp.zeros((ROWS, SLP - SL), F32)], axis=1
            ).astype(BF)
    pl.semaphore_wait(barrier, len(everyone))

    send("tokS", tok_in.at[1 - c], m.tok.at[own_half], SIB)
    gain_names = []
    for k in range(CHIPS):
        for o in range(CORES):
            if (k, o) != (0, 0):
                gain_names.append(f"gain{k}{o}")
                send(gain_names[-1], m.gains.at[r], m.gains.at[r], peer(k, o))

    def wout_blk(j, h):
        return m.wout.at[ds(j * SLP + c * ROWS + h * (ROWS // 2), ROWS // 2, 16)]

    gather_open("wo", wout_blk)
    in_fetch.extend("wo" + part for part in ("X0", "X1", "Y0", "Y1", "F0", "F1"))
    l_wout.wait()

    @pl.when(fetch)
    def _():
        gather_start("wo")

    for k, to in ((1, PX), (2, PY), (3, PD)):
        make(f"wq{k}", m.wqs.at[chip(k)], m.wqkv.at[up_rows], to)
        in_fetch.append(f"wq{k}")

    @pl.when(fetch)
    def _():
        start("wq1", "wq2", "wq3")

    def kern_blk(j, h):
        return m.kern.at[2 * j + c, pl.ds(h * (TOK // 2), TOK // 2)]

    gather_open("kn", kern_blk)
    in_fetch.extend("kn" + part for part in ("X0", "X1", "Y0", "Y1", "F0", "F1"))

    @pl.when(fetch)
    def _():
        gather_start("kn")

    send("knS0", m.kern.at[r], m.kern.at[r], SIB)

    send("wqS0", m.wqs.at[b], m.wqkv.at[up_rows], SIB)
    m.wqkv[up_rows, :] = m.wqs[b]

    def norm(src, n_ref, r_ref):
        def body(i):
            rows = pl.ds(i, 32)
            values = src[rows, :].astype(F32)
            centre = values - jnp.mean(values, axis=-1, keepdims=True)
            spread = jnp.mean(centre * centre, axis=-1, keepdims=True)
            rinv = lax.rsqrt(spread + EPSILON)
            n_ref[rows, :] = centre * rinv
            r_ref[rows, :] = jnp.broadcast_to(rinv, (32, LANES))

        rows_loop(BLK, 32, body, unroll=2)

    def scale(n_ref, gain_row, dst, base):
        def body(i):
            dst[pl.ds(pl.multiple_of(base + i, 32), 32), :] = (
                n_ref[pl.ds(i, 32), :] * m.gain[gain_row : gain_row + 1, :]
            ).astype(BF)

        rows_loop(BLK, 32, body, unroll=2)

    l_tok.wait()
    got("tokS")
    norm(m.tok, m.n1, m.r1)
    got(*gain_names)
    m.gain[...] = jnp.concatenate(
        [m.gains[d].astype(F32)[:, :ROWS] for d in range(CHIPS * CORES)], axis=1
    )
    scale(m.n1, 0, m.h1, b * BLK)

    def h1_blk(j, h):
        return m.h1.at[ds(j * BLK + h * TOK, TOK, TOK)]

    gather_open("h1", h1_blk)
    gather_start("h1")

    def w_place(ref):
        return lambda k: ref.at[ds((2 * chip(k) + c) * ROWS, ROWS, 32)]

    wq_place = w_place(m.wqkv)
    relay_open("wq", wq_place)
    relay("wq", wq_place, lambda k: got(f"wq{k}"))

    @pl.when(fetch)
    def _():
        gather_forward("kn")

    gather_forward("h1")
    for j in range(CHIPS):
        m.wout[j * SLP + SL : (j + 1) * SLP, :] = jnp.zeros((SLP - SL, D), BF)

    for k, to in ((1, PX), (2, PY), (3, PD)):
        make(f"wu{k}", wup_in.at[:, ds(chip(k) * FS, FS, LANES)], m.wup.at[up_rows], to)
        in_fetch.append(f"wu{k}")

    @pl.when(fetch)
    def _():
        gather_forward("wo")
        start("wu1", "wu2", "wu3")

    send("woS0", wout_rows(b, c), wout_rows(b, c), SIB)
    l_wup.wait()
    send("wuS0", m.wup.at[up_rows], m.wup.at[up_rows], SIB)
    l_wdn.wait()
    send("wdS", m.wdn.at[dn_rows], m.wdn.at[dn_rows], SIB)
    send("cotS", cot_in.at[1 - c], m.cot.at[cot_half], SIB)
    got("wqS0", "wqS1", "wqS2", "wqS3")

    def blk_rows(j):
        return ds(j * BLK, BLK, BLK)

    def project(j):
        m.tmp[0:BLK, :] = dot(m.h1[blk_rows(j), :], m.wqkv[...], 1, 0)

        def body(i):
            rows = pl.ds(i, 16)
            at = pl.multiple_of(j * BLK + i, 16)
            to = pl.ds(at, 16)
            q = m.tmp[rows, 0:SLP]
            m.sig[to, :] = 1.0 / (1.0 + jnp.exp(-q))
            keys = m.tmp[rows, SLP : 2 * SLP].astype(BF).astype(F32)
            values = m.tmp[rows, 2 * SLP : 3 * SLP].astype(BF)
            pos = at + lax.broadcasted_iota(jnp.int32, (16, SLP), 0)
            weighted = jnp.where(pos < length, jnp.exp(keys), 0.0)
            m.wgt[to, :] = weighted
            m.val[to, :] = values
            m.op[to, 0:SLP] = (weighted * values.astype(F32)).astype(BF)
            m.op[to, SLP : 2 * SLP] = weighted.astype(BF)

        rows_loop(BLK, 16, body, unroll=2)

    project(b)
    kn_place = lambda k: m.kern.at[2 * chip(k) + c]
    relay_open("kn", kn_place)
    relay("kn", kn_place, lambda k: gather_wait("kn", k))
    for k in (1, 2):
        gather_wait("h1", k)
        project(chip(k))
    gather_wait("h1", 3)
    project(jd)
    l_cot.wait()
    got("cotS")

    def cot_blk(j, h):
        return m.cot.at[ds(j * BLK + h * TOK, TOK, TOK)]

    gather_open("ct", cot_blk)
    start("ctX0", "ctY1")

    got("knS0", "knS1", "knS2", "knS3")
    ones = jnp.ones((8, SEQ), BF)
    m.sums[...] = dot(ones, m.op[...], 1, 0)

    def mix(j, half):
        d = 2 * j + half
        m.tmix[...] = dot(m.kern[d], m.op[pl.ds(band_at(d), BAND), :], 1, 0)

        def body(i):
            rows = pl.ds(i, 32)
            at = pl.multiple_of(d * TOK + i, 32)
            to = pl.ds(at, 32)
            pos = at + lax.broadcasted_iota(jnp.int32, (32, SLP), 0)
            valid = jnp.where(pos < length, 1.0, 0.0)
            num = m.tmix[rows, 0:SLP] + m.sums[0:1, 0:SLP]
            den = m.tmix[rows, SLP : 2 * SLP] + m.sums[0:1, SLP : 2 * SLP] + 1.0 - valid
            rden = 1.0 / den
            ratio = num * rden
            mixed = (ratio * valid).astype(BF)
            m.ratio[to, :] = ratio
            m.rden[to, :] = rden * valid
            m.mixed[to, :] = mixed
            gated = m.sig[to, :] * mixed.astype(F32)
            m.gated[to, :] = gated.astype(BF)
            high = gated[:, LANES:]
            m.ghs[j, rows, :] = jnp.where(
                half == 0, high, m.ghs[j, rows, :].astype(F32) + pltpu.roll(high, SL - LANES, 1)
            ).astype(BF)

        rows_loop(TOK, 32, body, unroll=2)

    def mix_block(j):
        def one(i, carry):
            mix(j, i)
            return carry

        lax.fori_loop(0, CORES, one, 0)

    low_lanes = pl.ds(0, LANES)

    def unpack(dst, high):
        lane = lax.broadcasted_iota(jnp.int32, (TOK, LANES), 1)
        both = high[...].astype(F32)
        for h in range(2):
            part = both if h == 0 else pltpu.roll(both, LANES - (SL - LANES), 1)
            dst[h * TOK : (h + 1) * TOK, LANES:] = jnp.where(lane < SL - LANES, part, 0.0).astype(BF)

    for k, to in ((3, PD), (1, PX), (2, PY)):
        j = chip(k)
        mix_block(j)
        send(f"ga{k}", m.gated.at[blk_rows(j), low_lanes], m.grecv.at[k, :, low_lanes], to)
        send(f"gh{k}", m.ghs.at[j], m.ghr.at[k - 1], to)
    mix_block(b)
    m.grecv[0] = m.gated[blk_rows(b), :]

    gather_forward("ct")
    wo_place = lambda k: wout_rows(chip(k), c)
    relay_open("wo", wo_place)
    relay("wo", wo_place, lambda k: gather_wait("wo", k))
    wu_place = w_place(m.wup)
    relay_open("wu", wu_place)
    relay("wu", wu_place, lambda k: got(f"wu{k}"))

    got("woS0", "woS1", "woS2", "woS3")
    m.resid[...] = m.tok[...].astype(F32)
    for k in (0, 1, 2, 3):
        if k:
            got(f"ga{k}", f"gh{k}")
            unpack(m.grecv.at[k], m.ghr.at[k - 1])
        m.resid[...] += dot(m.grecv[k], m.wout[ds(chip(k) * SLP, SLP, SLP), :], 1, 0)
    norm(m.resid, m.n2, m.r2)
    scale(m.n2, 1, m.h2, b * BLK)

    def h2_blk(j, h):
        return m.h2.at[ds(j * BLK + h * TOK, TOK, TOK)]

    gather_open("h2", h2_blk)
    gather_start("h2")

    got("wuS0", "wuS1", "wuS2", "wuS3", "wdS")

    def ff_forward(k):
        j = chip(k)
        keep = (k % 3) * BLK
        m.tmp[0:BLK, :] = dot(m.h2[blk_rows(j), :], m.wup[...], 1, 0)

        def gelu(i):
            v = m.tmp[pl.ds(i, 16), :]
            square = v * v
            t = jnp.tanh(GELU_SCALE * v * (1.0 + GELU_CUBE * square))
            half = 0.5 * (1.0 + t)
            m.hid[pl.ds(pl.multiple_of(j * BLK + i, 16), 16), :] = (v * half).astype(BF)
            m.dge[pl.ds(pl.multiple_of(keep + i, 16), 16), :] = half + 0.5 * v * (1.0 - t * t) * (
                GELU_SCALE * (1.0 + 3.0 * GELU_CUBE * square)
            )

        rows_loop(BLK, 16, gelu, unroll=2)

    def ff_out(k):
        part = dot(m.hid[blk_rows(chip(k)), :], m.wdn[...], 1, 0)
        if k == 0:
            m.resid[...] += part
        else:
            m.pout[k - 1] = part.astype(BF)

    def ff_backward(k):
        j = chip(k)
        keep = (k % 3) * BLK
        m.tmp[0:BLK, :] = dot(m.cot[blk_rows(j), :], m.wdn[...], 1, 1)

        def back(i):
            m.gupr[pl.ds(pl.multiple_of(j * BLK + i, 16), 16), :] = (
                m.tmp[pl.ds(i, 16), :] * m.dge[pl.ds(pl.multiple_of(keep + i, 16), 16), :]
            ).astype(BF)

        rows_loop(BLK, 16, back, unroll=2)
        part = dot(m.gupr[blk_rows(j), :], m.wup[...], 1, 1)
        if k == 0:
            m.own[...] = part
        else:
            m.pgh[k - 1] = part.astype(BF)

    other_cols = ds((1 - c) * HALF, HALF, LANES)
    own_cols = ds(c * HALF, HALF, LANES)

    def ff_grads(k):
        rows = blk_rows(chip(k))
        for dst, at, left, cols, right in (
            (m.gdx, 0, m.hid, other_cols, m.cot),
            (m.gdo, 0, m.hid, own_cols, m.cot),
            (m.guo, 0, m.h2, pl.ds(0, HALF), m.gupr),
            (m.guo, HALF, m.h2, pl.ds(HALF, HALF), m.gupr),
        ):
            part = dot(left[rows, cols], right[rows, :], 0, 0)
            to = pl.ds(at, HALF)
            if k == 0:
                dst[to, :] = part
            else:
                dst[to, :] += part

    ff_forward(0)
    ff_backward(0)
    gather_forward("h2")
    start("ctX1", "ctY0")
    ff_out(0)
    ff_grads(0)
    for k in (1, 2):
        gather_wait("h2", k)
        ff_forward(k)
    gather_wait("h2", 3)
    ff_forward(3)
    gather_wait("ct", 3)
    ff_backward(3)
    scatter_diagonal("g2", m.pgh, m.rbg2, TOK)
    gather_wait("ct", 1)
    ff_backward(1)
    scatter_direct_x("g2", m.pgh, m.rbg2, TOK)
    gather_wait("ct", 2)
    ff_backward(2)
    scatter_direct_y("g2", m.pgh, m.rbg2, TOK)
    ff_grads(3)
    ff_grads(1)
    scatter_combine("g2", m.pgh, m.rbg2, TOK)
    ff_grads(2)

    for j in range(CHIPS):
        m.gds[j] = m.gdx[j * ROWS : (j + 1) * ROWS, :].astype(BF)
    send("gdS", m.gds, m.gdr, SIB)
    for j in range(CHIPS):
        m.gus[j] = m.guo[ds((2 * j + 1 - c) * ROWS, ROWS, 32), :].astype(BF)
    send("guS", m.gus, m.gur, SIB)

    def split_rows(left, right, kept, leaving):
        width = right.shape[1]
        for i in range(2):
            m.tmp[:, 0:width] = dot(left[:, i * HALF : (i + 1) * HALF], right[...], 0, 0)
            for q in range(2):
                kept[2 * i + q] = m.tmp[ds((2 * q + c) * ROWS, ROWS, 32), 0:width]
                leaving[2 * i + q] = m.tmp[ds((2 * q + 1 - c) * ROWS, ROWS, 32), 0:width].astype(BF)

    def pair_sum(name, kept, came, base):
        for k in ORDER:
            j = chip(k)
            base[j] = (kept(j) + came[j].astype(F32)).astype(BF)
            z_start(f"{name}{k}")

    def pack(dst, at, rows):
        n = rows.shape[0]
        dst[at : at + n, :] = rows[:, :LANES].astype(BF)
        dst[at + n : at + n + n // 2, :] = jnp.concatenate(
            [rows[: n // 2, LANES:SL], rows[n // 2 :, LANES:SL]], axis=1
        ).astype(BF)

    def pair_sum_packed(name, kept, came, base):
        for k in ORDER:
            j = chip(k)
            total = kept[j] + came[j].astype(F32)
            for i in range(total.shape[1] // SLP):
                pack(base.at[j], i * PACK, total[:, i * SLP : (i + 1) * SLP])
            z_start(f"{name}{k}")

    got("gdS")
    pair_sum("zd", lambda j: m.gdo[ds(j * ROWS, ROWS, 32), :], m.gdr, m.zdb)
    got("guS")
    pair_sum("zu", lambda j: m.guo[ds((2 * j + c) * ROWS, ROWS, 32), :], m.gur, m.zub)
    for k in (3, 1, 2):
        ff_out(k)
    scatter_diagonal("ou", m.pout, m.rbout, TOK)
    poll(1)

    scatter_wait("g2")

    def norm_back(total, gain_row, n_ref, r_ref, i, base):
        rows = pl.ds(i, 32)
        e = total * m.gain[gain_row : gain_row + 1, :]
        n = n_ref[rows, :]
        mean_e = jnp.mean(e, axis=-1, keepdims=True)
        mean_en = jnp.mean(e * n, axis=-1, keepdims=True)
        return base + r_ref[rows, 0:1] * (e - mean_e - n * mean_en)

    for h in range(2):

        def back_two(i, h=h):
            at = pl.multiple_of(h * TOK + i, 32)
            rows = pl.ds(at, 32)
            total = m.own[rows, :] + scatter_sum(m.rbg2, TOK, h, pl.ds(i, 32))
            base = m.cot[pl.ds(pl.multiple_of(b * BLK + at, 32), 32), :].astype(F32)
            g = norm_back(total, 1, m.n2, m.r2, at, base)
            m.gresid[rows, :] = g
            m.gattn[rows, :] = g.astype(BF)

        rows_loop(TOK, 32, back_two, unroll=2)
    poll(2)

    for k, to in ((3, PD), (1, PX), (2, PY)):
        part = dot(m.gattn[...], m.wout[ds(chip(k) * SLP, SLP, SLP), :], 1, 1)
        m.ggs[k - 1] = part[:, :LANES].astype(BF)
        send(f"gg{k}", m.ggs.at[k - 1], m.ggr.at[k, :, low_lanes], to)
        high = part[:, LANES:]
        m.gghs[k - 1] = (high[:TOK] + pltpu.roll(high[TOK:], SL - LANES, 1)).astype(BF)
        send(f"gi{k}", m.gghs.at[k - 1], m.gghr.at[k - 1], to)
    m.ggr[0] = dot(m.gattn[...], m.wout[ds(b * SLP, SLP, SLP), :], 1, 1).astype(BF)
    poll(3)
    for k in range(CHIPS):
        m.tmp[0:SLP, :] = dot(m.grecv[k], m.gattn[...], 0, 0)
        m.goo[k] = m.tmp[ds(c * ROWS, ROWS, 32), :]
        m.gos[k] = m.tmp[ds((1 - c) * ROWS, ROWS, 32), :].astype(BF)
    send("goS", m.gos, m.gor, SIB)
    poll(4)

    gqkv = m.hid
    gres = m.h2
    sent("h2X0", "h2X1", "h2Y0", "h2Y1", "h2F0", "h2F1")

    def mix_back(k):
        j = chip(k)

        def body(i):
            at = pl.multiple_of(j * BLK + i, 16)
            rows = pl.ds(at, 16)
            gg = m.ggr[k, pl.ds(i, 16), :].astype(F32)
            sig = m.sig[rows, :]
            gm = (gg * sig).astype(BF).astype(F32)
            gqkv[rows, 0:SLP] = (
                gg * m.mixed[rows, :].astype(F32) * sig * (1.0 - sig)
            ).astype(BF)
            gnum = gm * m.rden[rows, :]
            gres[rows, 0:SLP] = gnum.astype(BF)
            gres[rows, SLP : 2 * SLP] = (-gnum * m.ratio[rows, :]).astype(BF)

        rows_loop(BLK, 16, body, unroll=2)

    mix_back(0)
    poll(5)
    got("goS")
    for k in (1, 2, 3):
        m.po[k - 1] = (m.goo[k] + m.gor[k].astype(F32)).astype(BF)
    scatter_diagonal("wg", m.po, m.rbo, ROWS // 2)
    scatter_direct_x("wg", m.po, m.rbo, ROWS // 2)
    scatter_direct_y("wg", m.po, m.rbo, ROWS // 2)
    scatter_direct_x("ou", m.pout, m.rbout, TOK)
    scatter_direct_y("ou", m.pout, m.rbout, TOK)
    poll(6)
    for k in (1, 2, 3):
        got(f"gg{k}", f"gi{k}")
        unpack(m.ggr.at[k], m.gghr.at[k - 1])
        mix_back(k)
        poll(6 + k)
    scatter_combine("wg", m.po, m.rbo, ROWS // 2)
    m.sums[...] = dot(ones, gres[:, 0 : 2 * SLP], 1, 0)
    m.gop[...] = jnp.broadcast_to(m.sums[0:1, :], (SEQ, 2 * SLP))
    poll(10)

    def kernel_grad(d):
        return dot(
            gres[ds(d * TOK, TOK, TOK), 0 : 2 * SLP], m.op[pl.ds(band_at(d), BAND), :], 1, 1
        )

    for k in range(CHIPS):
        m.gks[k] = kernel_grad(2 * chip(k) + 1 - c).astype(BF)
    send("gkS", m.gks, m.gkr, SIB)
    poll(11)
    split_rows(m.h1, gqkv.at[:, 0:SLP], m.gqo, m.gqs)
    send("gqS", m.gqs, m.gqr, SIB)
    poll(12)
    for k in range(CHIPS):
        m.gko[k] = kernel_grad(2 * chip(k) + c)
    poll(13)
    got("gkS")
    for k in (1, 2, 3):
        m.pk[k - 1] = (m.gko[k] + m.gkr[k].astype(F32)).astype(BF)
    scatter_diagonal("kg", m.pk, m.rbk, TOK // 2)
    scatter_direct_x("kg", m.pk, m.rbk, TOK // 2)
    scatter_direct_y("kg", m.pk, m.rbk, TOK // 2)
    poll(14)

    def mix_t(d, carry):
        at = pl.ds(band_at(d), BAND)
        m.gop[at, :] += dot(m.kern[d], gres[ds(d * TOK, TOK, TOK), 0 : 2 * SLP], 0, 0)
        return carry

    lax.fori_loop(0, CHIPS * CORES, mix_t, 0)
    poll(15)

    def keys_back(i):
        rows = pl.ds(i, 16)
        gkv = m.gop[rows, 0:SLP]
        w = m.wgt[rows, :]
        gqkv[rows, SLP : 2 * SLP] = (
            (gkv * m.val[rows, :].astype(F32) + m.gop[rows, SLP : 2 * SLP]) * w
        ).astype(BF)
        gqkv[rows, 2 * SLP : 3 * SLP] = (gkv * w).astype(BF)

    rows_loop(SEQ, 16, keys_back, unroll=2)
    poll(16)

    sent("g20", "g21", "g22", "g23", "g24", "g25")
    for k in ORDER:
        part = dot(gqkv[blk_rows(chip(k)), :], m.wqkv[...], 1, 1)
        if k == 0:
            m.own[...] = part
        else:
            m.pgh[k - 1] = part.astype(BF)
        if k == 3:
            scatter_diagonal("g1", m.pgh, m.rbg1, TOK)
        if k == 1:
            scatter_direct_x("g1", m.pgh, m.rbg1, TOK)
        if k == 2:
            scatter_direct_y("g1", m.pgh, m.rbg1, TOK)
        poll(17 + k)
    got("gqS")
    pair_sum_packed("zq", m.gqo, m.gqr, m.zqb)
    poll(21)

    def scattered(dst, mine, came, buf, half):
        for h in range(2):
            rows = pl.ds(h * half, half)
            dst[rows, :] = (
                mine[0, rows, :] + came[0, rows, :].astype(F32)
                + scatter_sum(buf, half, h, pl.ds(0, half))
            ).astype(BF)

    scatter_wait("wg")
    scattered(m.zob, m.goo, m.gor, m.rbo, ROWS // 2)
    z_start("zo")
    poll(22)
    split_rows(m.h1, gqkv.at[:, SLP : 3 * SLP], m.gvo, m.gvs)
    send("gvS", m.gvs, m.gvr, SIB)
    poll(23)
    scatter_combine("kg", m.pk, m.rbk, TOK // 2)
    poll(24)
    scatter_combine("g1", m.pgh, m.rbg1, TOK)
    poll(25)
    got("gvS")
    pair_sum_packed("zv", m.gvo, m.gvr, m.zvb)
    poll(26)
    scatter_combine("ou", m.pout, m.rbout, TOK)
    poll(27)
    poll(28)
    scatter_wait("kg")
    scattered(m.zkb, m.gko, m.gkr, m.rbk, TOK // 2)
    z_start("zk")

    poll(29)

    poll(30)
    scatter_wait("ou")
    for h in range(2):

        def out_rows(i, h=h):
            rows = pl.ds(pl.multiple_of(h * TOK + i, 32), 32)
            m.fout[rows, :] = (
                m.resid[rows, :] + scatter_sum(m.rbout, TOK, h, pl.ds(i, 32))
            ).astype(BF)

        rows_loop(TOK, 32, out_rows)
    send("outS", m.fout.at[other_half], out_out.at[c], SIB)
    local_copy(m.fout.at[own_half], out_out.at[c])

    scatter_wait("g1")
    for h in range(2):

        def back_one(i, h=h):
            at = pl.multiple_of(h * TOK + i, 32)
            rows = pl.ds(at, 32)
            total = m.own[rows, :] + scatter_sum(m.rbg1, TOK, h, pl.ds(i, 32))
            m.fgt[rows, :] = norm_back(total, 0, m.n1, m.r1, at, m.gresid[rows, :]).astype(BF)

        rows_loop(TOK, 32, back_one, unroll=2)
    send("gtS", m.fgt.at[other_half], gtok_out.at[c], SIB)
    local_copy(m.fgt.at[own_half], gtok_out.at[c])
    poll(31)

    for cp in locals_:
        if all(cp is not done for done in (l_tok, l_pb, l_wout, l_wup, l_wdn, l_cot, *l_w)):
            cp.wait()
    for name in begun:
        if name not in in_fetch:
            got(name)
            sent(name)

    @pl.when(fetch)
    def _():
        for name in in_fetch:
            sent(name)

    for name in zitems:
        z_close(name)


FIN_IN = dict(
    gq=((CHIPS, PACK, LANES), BF),
    gv=((CHIPS, 2 * PACK, LANES), BF),
    gup=((CHIPS, ROWS, FS), BF),
    gdn=((FF // (CHIPS * CORES), D), BF),
    gwout=((ROWS, D), BF),
    gpb=((TOK, BAND), BF),
    wq=((ROWS, D), BF),
    wk=((ROWS, D), BF),
    wv=((ROWS, D), BF),
    wup=((ROWS, FF), BF),
    pb=((TOK, BAND), BF),
    out=((2, TOK, D), BF),
    gtok=((2, TOK, D), BF),
)
FIN_OUT = dict(
    q=((ROWS, D), F32),
    k=((ROWS, D), F32),
    v=((ROWS, D), F32),
    o=((ROWS, D), F32),
    up=((ROWS, FF), F32),
    dn=((FF // (CHIPS * CORES), D), F32),
    bias=((TOK, SEQ), F32),
)


def finish_kernel(
    out_in, gtok_in, gq_in, gv_in, gwout_in, gup_in, gdn_in, gpb_in, ga_in, gm_in,
    wq_in, wk_in, wv_in, wup_in, pb_in,
    out_out, gtok_out, ga_out, q_out, k_out, v_out, o_out, gm_out, up_out, dn_out, bias_out,
    *scratch,
):
    m = types.SimpleNamespace(**dict(zip((*FIN_IN, *FIN_OUT), scratch)))
    in_sem, out_sem = scratch[len(FIN_IN) + len(FIN_OUT):]
    start = pl.multiple_of(
        jnp.minimum(jnp.maximum(lax.axis_index("dp") - 2, 0), 3) * LANES, LANES
    )
    stores = []

    def store(src, dst):
        stores.append(pltpu.make_async_copy(src, dst, out_sem.at[len(stores)]))
        stores[-1].start()

    sources = dict(
        gdn=gdn_in, gup=gup_in, wup=wup_in, gq=gq_in, wq=wq_in, gv=gv_in, wk=wk_in, wv=wv_in, gwout=gwout_in,
        gpb=gpb_in, pb=pb_in.at[:, pl.ds(start, BAND)], out=out_in, gtok=gtok_in,
    )
    loads = types.SimpleNamespace(
        **{
            name: pltpu.make_async_copy(src, vars(m)[name], in_sem.at[i])
            for i, (name, src) in enumerate(sources.items())
        }
    )
    for cp in vars(loads).values():
        cp.start()

    loads.gdn.wait()
    m.dn[...] = m.gdn[...].astype(F32)
    store(m.dn, dn_out)

    def as_row(column, gain):
        square = jnp.broadcast_to(column, (ROWS, LANES))
        return jnp.transpose(square)[0:1, :] / gain[...].astype(F32)

    loads.gup.wait()
    loads.wup.wait()
    column = jnp.zeros((ROWS, 1), F32)
    for j in range(CHIPS):
        cols = slice(j * FS, (j + 1) * FS)
        g = m.gup[j].astype(F32)
        m.up[:, cols] = g
        column += jnp.sum(g * m.wup[:, cols].astype(F32), axis=1, keepdims=True)
    store(m.up, up_out)
    gm_out[...] = as_row(column, gm_in)

    def unpack(ref, j, at):
        low = ref[j, at : at + ROWS, :].astype(F32)
        high = ref[j, at + ROWS : at + PACK, :].astype(F32)
        rest = SL - LANES
        return jnp.concatenate(
            [low, jnp.concatenate([high[:, :rest], high[:, rest:]], axis=0)], axis=1
        )

    column = jnp.zeros((ROWS, 1), F32)
    for needs, ref, at, w, mine, dst in (
        ((loads.gq, loads.wq), m.gq, 0, m.wq, m.q, q_out),
        ((loads.gv, loads.wk), m.gv, 0, m.wk, m.k, k_out),
        ((loads.wv,), m.gv, PACK, m.wv, m.v, v_out),
    ):
        for cp in needs:
            cp.wait()
        g = jnp.concatenate([unpack(ref, j, at) for j in range(CHIPS)], axis=1)
        mine[...] = g
        store(mine, dst)
        column += jnp.sum(g * w[...].astype(F32), axis=1, keepdims=True)
    ga_out[...] = as_row(column, ga_in)

    loads.gwout.wait()
    m.o[...] = m.gwout[...].astype(F32)
    store(m.o, o_out)
    loads.gpb.wait()
    loads.pb.wait()
    t_ids = lax.axis_index("dp") * TOK + lax.broadcasted_iota(jnp.int32, (TOK, BAND), 0)
    u_ids = start + lax.broadcasted_iota(jnp.int32, (TOK, BAND), 1)
    m.bias[...] = jnp.zeros((TOK, SEQ), F32)
    m.bias[:, pl.ds(start, BAND)] = jnp.where(
        jnp.abs(t_ids - u_ids) < WIN, m.gpb[...].astype(F32) * jnp.exp(m.pb[...].astype(F32)), 0.0
    )
    store(m.bias, bias_out)
    loads.out.wait()
    store(m.out, out_out)
    loads.gtok.wait()
    store(m.gtok, gtok_out)
    for cp in stores:
        cp.wait()


def plane_program(
    tokens, lengths, cotangent, gain_attn, w_query, w_key, w_value, w_out, gain_mlp, w_up, w_down, pos_bias
):
    anywhere = pl.BlockSpec(memory_space=pl.ANY)
    whole = pl.BlockSpec(memory_space=pltpu.VMEM)
    struct = jax.ShapeDtypeStruct
    results = pl.pallas_call(
        plane_kernel,
        out_shape=(
            struct((2, TOK, D), BF),
            struct((2, TOK, D), BF),
            struct((CHIPS, PACK, LANES), BF),
            struct((CHIPS, 2 * PACK, LANES), BF),
            struct((ROWS, D), BF),
            struct((CHIPS, ROWS, FS), BF),
            struct((CHIPS, ROWS, D), BF),
            struct((TOK, BAND), BF),
        ),
        in_specs=[anywhere, pl.BlockSpec(memory_space=pltpu.SMEM), anywhere, whole, whole] + [anywhere] * 7,
        out_specs=(anywhere,) * 8,
        scratch_shapes=[pltpu.VMEM(shape, kind) for shape, kind in SCRATCH.values()]
        + [
            pltpu.SemaphoreType.DMA((N_REMOTE,)),
            pltpu.SemaphoreType.DMA((N_REMOTE,)),
            pltpu.SemaphoreType.DMA((N_LOCAL,)),
        ],
        compiler_params=pltpu.CompilerParams(
            collective_id=0, has_side_effects=True, vmem_limit_bytes=VMEM_BYTES
        ),
        cost_estimate=pl.CostEstimate(
            flops=15_000_000_000, bytes_accessed=8_000_000, transcendentals=4_000_000
        ),
        name="aft_layer",
    )(
        tokens.reshape(2, TOK, D), lengths.reshape(2), cotangent.reshape(2, TOK, D),
        gain_attn.reshape(1, ROWS), gain_mlp.reshape(1, ROWS),
        w_query, w_key, w_value, w_out, w_up, w_down, pos_bias,
    )
    out, gtok, gq, gv, gwout, gup, gdn, gpb = results
    f32_out = [struct(shape, kind) for shape, kind in FIN_OUT.values()]
    row = struct((1, ROWS), F32)
    out, gtok, grad_gain_a, grad_q, grad_k, grad_v, grad_o, grad_gain_m, grad_up, grad_down, grad_bias = (
        pl.pallas_call(
            finish_kernel,
            out_shape=(struct((2, TOK, D), BF),) * 2 + (row, *f32_out[:4], row, *f32_out[4:]),
            in_specs=[anywhere] * 8 + [whole] * 2 + [anywhere] * 5,
            out_specs=(anywhere, anywhere, whole) + (anywhere,) * 4 + (whole,) + (anywhere,) * 3,
            scratch_shapes=[pltpu.VMEM(shape, kind) for shape, kind in (*FIN_IN.values(), *FIN_OUT.values())]
            + [pltpu.SemaphoreType.DMA((len(FIN_IN),)), pltpu.SemaphoreType.DMA((len(FIN_OUT) + 2,))],
            compiler_params=pltpu.CompilerParams(vmem_limit_bytes=VMEM_BYTES),
            cost_estimate=pl.CostEstimate(flops=4_000_000, bytes_accessed=9_000_000, transcendentals=100_000),
            name="gradients_out",
        )(
            out, gtok, gq, gv, gwout, gup, gdn.reshape(FF // (CHIPS * CORES), D), gpb,
            gain_attn.reshape(1, ROWS), gain_mlp.reshape(1, ROWS),
            w_query, w_key, w_value, w_up, pos_bias,
        )
    )
    return (
        out.reshape(tokens.shape),
        gtok.reshape(tokens.shape),
        grad_gain_a.reshape(ROWS),
        grad_q,
        grad_k,
        grad_v,
        grad_o,
        grad_gain_m.reshape(ROWS),
        grad_up,
        grad_down,
        grad_bias,
    )


def solution(mesh):
    in_specs = (
        P(None, "pipe", "dp", None),
        P(None, "pipe", None),
        P(None, "pipe", "dp", None),
        P("dp"),
        P("dp", None),
        P("dp", None),
        P("dp", None),
        P("dp", None),
        P("dp"),
        P("dp", None),
        P("dp", None),
        P("dp", None),
    )
    out_specs = (
        P(None, "pipe", "dp", None),
        P(None, "pipe", "dp", None),
        P("dp"),
        P("dp", None),
        P("dp", None),
        P("dp", None),
        P("dp", None),
        P("dp"),
        P("dp", None),
        P("dp", None),
        P("dp", None),
    )
    fits = mesh.shape["dp"] == CHIPS * CORES and mesh.shape["pipe"] == DEPTH
    return jax.shard_map(plane_program if fits else local, mesh=mesh, in_specs=in_specs, out_specs=out_specs, check_vma=False)
```

```python
import types

import jax
import jax.numpy as jnp
from jax import lax
from jax.experimental import pallas as pl
from jax.experimental.pallas import tpu as pltpu
from jax.sharding import PartitionSpec as P

D = 768
FF = 3072
SEQ = 1024
WIN = 256


EPSILON = 1e-05
GELU_SCALE = 0.7978845608028654
GELU_CUBE = 0.044715
VMEM_BYTES = 63 * 2**20


def normalize(values, gain):
    centre = values - jnp.mean(values, axis=-1, keepdims=True)
    spread = jnp.mean(centre * centre, axis=-1, keepdims=True)
    return centre * lax.rsqrt(spread + EPSILON) * gain


def gelu_tanh(values):
    return jax.nn.gelu(values, approximate=True)


def band_ones(width):
    row_ids = jnp.arange(width)[:, None]
    col_ids = jnp.arange(3 * width)[None, :]
    return (jnp.abs(col_ids - width - row_ids) < width).astype(jnp.float32)


def band_blocks(bias, width):
    length = bias.shape[0]
    padded = jnp.pad(bias, ((0, 0), (width, width)))
    return jnp.stack(
        [
            padded[block * width : (block + 1) * width, block * width : block * width + 3 * width]
            for block in range(length // width)
        ]
    )


def windows(operand, width):
    blocks = operand.shape[0] // width
    padded = jnp.pad(operand, ((width, width), (0, 0))).reshape(blocks + 2, width, operand.shape[1])
    return jnp.concatenate([padded[:-2], padded[1:-1], padded[2:]], axis=1)


def unwindow(grad_windows, width):
    blocks = grad_windows.shape[0]
    leading = jnp.pad(grad_windows[:, :width], ((0, 2), (0, 0), (0, 0)))
    middle = jnp.pad(grad_windows[:, width : 2 * width], ((1, 1), (0, 0), (0, 0)))
    trailing = jnp.pad(grad_windows[:, 2 * width :], ((2, 0), (0, 0), (0, 0)))
    summed = leading + middle + trailing
    return summed[1:-1].reshape(blocks * width, grad_windows.shape[2])


def to_columns(matrix, seq_count, length):
    channels = matrix.shape[1]
    return (
        matrix.reshape(seq_count, length, channels)
        .transpose(1, 0, 2)
        .reshape(length, seq_count * channels)
    )


def from_columns(matrix, seq_count, length):
    channels = matrix.shape[1] // seq_count
    return (
        matrix.reshape(length, seq_count, channels)
        .transpose(1, 0, 2)
        .reshape(seq_count * length, channels)
    )


def outer_sum(left, right):
    return lax.dot_general(
        left, right, (((0,), (0,)), ((), ())), preferred_element_type=jnp.float32
    )


def times_transpose(left, right):
    return lax.dot_general(
        left, right, (((1,), (1,)), ((), ())), preferred_element_type=jnp.float32
    )


def local(
    tokens,
    lengths,
    cotangent,
    gain_attn,
    w_query,
    w_key,
    w_value,
    w_out,
    gain_mlp,
    w_up,
    w_down,
    pos_bias,
):
    gathered = (
        lax.all_gather(gain_attn, "dp", axis=0, tiled=True),
        lax.all_gather(w_query, "dp", axis=0, tiled=True),
        lax.all_gather(w_key, "dp", axis=0, tiled=True),
        lax.all_gather(w_value, "dp", axis=0, tiled=True),
        lax.all_gather(w_out, "dp", axis=0, tiled=True),
        lax.all_gather(gain_mlp, "dp", axis=0, tiled=True),
        lax.all_gather(w_up, "dp", axis=0, tiled=True),
        lax.all_gather(w_down, "dp", axis=0, tiled=True),
        lax.all_gather(pos_bias, "dp", axis=0, tiled=True),
    )
    gain_a = gathered[0].astype(jnp.float32)
    query_w, key_w, value_w, out_w = (gathered[1], gathered[2], gathered[3], gathered[4])
    gain_m = gathered[5].astype(jnp.float32)
    up_w, down_w = (gathered[6], gathered[7])
    bias_full = gathered[8].astype(jnp.float32)
    group_size = lax.axis_size("dp")
    tok_rows = tokens.shape[2]
    seq_count = group_size * tok_rows // SEQ
    band_mask = band_ones(WIN)
    bias_blocks = jnp.exp(band_blocks(bias_full, WIN))
    exp_band = bias_blocks * band_mask
    kernel = ((bias_blocks - 1.0) * band_mask).astype(jnp.bfloat16)
    positions = jnp.arange(SEQ)
    grad_gain_a = jnp.zeros((D,), jnp.float32)
    grad_gain_m = jnp.zeros((D,), jnp.float32)
    grad_query_w = jnp.zeros((D, D), jnp.float32)
    grad_key_w = jnp.zeros((D, D), jnp.float32)
    grad_value_w = jnp.zeros((D, D), jnp.float32)
    grad_out_w = jnp.zeros((D, D), jnp.float32)
    grad_up_w = jnp.zeros((D, FF), jnp.float32)
    grad_down_w = jnp.zeros((FF, D), jnp.float32)
    grad_kernel = jnp.zeros(exp_band.shape, jnp.float32)
    outputs_list = []
    grads_in_list = []
    for micro in range(tokens.shape[0]):
        inputs_f = tokens[micro, 0].astype(jnp.float32)
        normed_f, norm_back_a = jax.vjp(normalize, inputs_f, gain_a)
        normed = normed_f.astype(jnp.bfloat16)
        query = jnp.dot(normed, query_w, preferred_element_type=jnp.float32)
        keys = jnp.dot(normed, key_w, preferred_element_type=jnp.float32).astype(jnp.bfloat16)
        values = jnp.dot(normed, value_w, preferred_element_type=jnp.float32).astype(jnp.bfloat16)
        key_chan, value_chan = (
            lax.all_to_all(keys, "dp", split_axis=1, concat_axis=0, tiled=True),
            lax.all_to_all(values, "dp", split_axis=1, concat_axis=0, tiled=True),
        )
        seq_lengths = lengths[micro, 0]
        channels = key_chan.shape[1]
        valid_seq = (positions[:, None] < seq_lengths[None, :]).astype(jnp.float32)
        valid_cols = jnp.broadcast_to(valid_seq[:, :, None], (SEQ, seq_count, channels)).reshape(
            SEQ, seq_count * channels
        )
        key_cols = to_columns(key_chan, seq_count, SEQ).astype(jnp.float32)
        value_cols = to_columns(value_chan, seq_count, SEQ).astype(jnp.float32)
        weighted = jnp.exp(key_cols) * valid_cols
        col_count = weighted.shape[1]
        operand = jnp.concatenate(
            [(weighted * value_cols).astype(jnp.bfloat16), weighted.astype(jnp.bfloat16)], axis=1
        )
        windowed = windows(operand, WIN)
        banded = jnp.einsum(
            "nqk,nkc->nqc", kernel, windowed, preferred_element_type=jnp.float32
        ).reshape(SEQ, 2 * col_count)
        result = banded + jnp.sum(operand, axis=0, dtype=jnp.float32)[None, :]
        numerator = result[:, :col_count]
        denominator = result[:, col_count:] + 1.0 - valid_cols
        mixed_cols = numerator / denominator * valid_cols
        mixed_tok = lax.all_to_all(
            from_columns(mixed_cols.astype(jnp.bfloat16), seq_count, SEQ),
            "dp",
            split_axis=0,
            concat_axis=1,
            tiled=True,
        )
        sigmoid_q = jax.nn.sigmoid(query)
        mixed_f = mixed_tok.astype(jnp.float32)
        gated = (sigmoid_q * mixed_f).astype(jnp.bfloat16)
        resid = inputs_f + jnp.dot(gated, out_w, preferred_element_type=jnp.float32)
        normed_two_f, norm_back_m = jax.vjp(normalize, resid, gain_m)
        normed_two = normed_two_f.astype(jnp.bfloat16)
        upper = jnp.dot(normed_two, up_w, preferred_element_type=jnp.float32)
        hidden_f, gelu_back = jax.vjp(gelu_tanh, upper)
        hidden = hidden_f.astype(jnp.bfloat16)
        outputs_list.append(
            (resid + jnp.dot(hidden, down_w, preferred_element_type=jnp.float32)).astype(
                jnp.bfloat16
            )
        )
        grad_out = cotangent[micro, 0]
        grad_down_w = grad_down_w + outer_sum(hidden, grad_out)
        grad_hidden = times_transpose(grad_out, down_w)
        grad_upper = gelu_back(grad_hidden)[0].astype(jnp.bfloat16)
        grad_up_w = grad_up_w + outer_sum(normed_two, grad_upper)
        grad_normed_two = times_transpose(grad_upper, up_w)
        grad_resid_norm, grad_gain_part_m = norm_back_m(grad_normed_two)
        grad_gain_m = grad_gain_m + grad_gain_part_m
        grad_resid = grad_out.astype(jnp.float32) + grad_resid_norm
        grad_attn = grad_resid.astype(jnp.bfloat16)
        grad_out_w = grad_out_w + outer_sum(gated, grad_attn)
        grad_gated = times_transpose(grad_attn, out_w)
        grad_mixed = (grad_gated * sigmoid_q).astype(jnp.bfloat16)
        grad_query = (grad_gated * mixed_f * sigmoid_q * (1.0 - sigmoid_q)).astype(jnp.bfloat16)
        grad_mixed_chan = lax.all_to_all(grad_mixed, "dp", split_axis=1, concat_axis=0, tiled=True)
        grad_mixed_cols = to_columns(grad_mixed_chan, seq_count, SEQ).astype(jnp.float32)
        grad_numerator = grad_mixed_cols * valid_cols / denominator
        grad_denominator = -grad_numerator * (numerator / denominator)
        grad_flat = jnp.concatenate(
            [grad_numerator.astype(jnp.bfloat16), grad_denominator.astype(jnp.bfloat16)], axis=1
        )
        grad_result = grad_flat.reshape(SEQ // WIN, WIN, 2 * col_count)
        grad_windowed = jnp.einsum(
            "nqk,nqc->nkc", kernel, grad_result, preferred_element_type=jnp.float32
        )
        grad_kernel = grad_kernel + jnp.einsum(
            "nqc,nkc->nqk", grad_result, windowed, preferred_element_type=jnp.float32
        )
        grad_operand = (
            unwindow(grad_windowed, WIN) + jnp.sum(grad_flat, axis=0, dtype=jnp.float32)[None, :]
        )
        grad_key_value = grad_operand[:, :col_count]
        grad_key_weight = grad_operand[:, col_count:]
        grad_keys_cols = (grad_key_value * value_cols + grad_key_weight) * weighted
        grad_values_cols = grad_key_value * weighted
        grad_keys, grad_values = (
            lax.all_to_all(
                from_columns(grad_keys_cols.astype(jnp.bfloat16), seq_count, SEQ),
                "dp",
                split_axis=0,
                concat_axis=1,
                tiled=True,
            ),
            lax.all_to_all(
                from_columns(grad_values_cols.astype(jnp.bfloat16), seq_count, SEQ),
                "dp",
                split_axis=0,
                concat_axis=1,
                tiled=True,
            ),
        )
        grad_query_w = grad_query_w + outer_sum(normed, grad_query)
        grad_key_w = grad_key_w + outer_sum(normed, grad_keys)
        grad_value_w = grad_value_w + outer_sum(normed, grad_values)
        grad_normed = (
            times_transpose(grad_query, query_w)
            + times_transpose(grad_keys, key_w)
            + times_transpose(grad_values, value_w)
        )
        grad_input_norm, grad_gain_part_a = norm_back_a(grad_normed)
        grad_gain_a = grad_gain_a + grad_gain_part_a
        grads_in_list.append((grad_resid + grad_input_norm).astype(jnp.bfloat16))
    grad_kernel_bias = grad_kernel * exp_band
    grad_bias_pad = jnp.zeros((SEQ, SEQ + 2 * WIN), jnp.float32)
    for block in range(SEQ // WIN):
        grad_bias_pad = grad_bias_pad.at[
            block * WIN : (block + 1) * WIN, block * WIN : block * WIN + 3 * WIN
        ].add(grad_kernel_bias[block])
    grad_bias = grad_bias_pad[:, WIN : WIN + SEQ]
    shares = (
        lax.psum_scatter(grad_gain_a, "dp", scatter_dimension=0, tiled=True),
        lax.psum_scatter(grad_query_w, "dp", scatter_dimension=0, tiled=True),
        lax.psum_scatter(grad_key_w, "dp", scatter_dimension=0, tiled=True),
        lax.psum_scatter(grad_value_w, "dp", scatter_dimension=0, tiled=True),
        lax.psum_scatter(grad_out_w, "dp", scatter_dimension=0, tiled=True),
        lax.psum_scatter(grad_gain_m, "dp", scatter_dimension=0, tiled=True),
        lax.psum_scatter(grad_up_w, "dp", scatter_dimension=0, tiled=True),
        lax.psum_scatter(grad_down_w, "dp", scatter_dimension=0, tiled=True),
        lax.psum_scatter(grad_bias, "dp", scatter_dimension=0, tiled=True),
    )
    reduced = lax.psum(
        (
            shares[0],
            shares[1],
            shares[2],
            shares[3],
            shares[4],
            shares[5],
            shares[6],
            shares[7],
            shares[8],
        ),
        "pipe",
    )
    final_grads = (
        reduced[0],
        reduced[1],
        reduced[2],
        reduced[3],
        reduced[4],
        reduced[5],
        reduced[6],
        reduced[7],
        reduced[8],
    )
    output = jnp.stack(outputs_list)[:, None]
    grad_tokens = jnp.stack(grads_in_list)[:, None]
    return (
        output,
        grad_tokens,
        final_grads[0],
        final_grads[1],
        final_grads[2],
        final_grads[3],
        final_grads[4],
        final_grads[5],
        final_grads[6],
        final_grads[7],
        final_grads[8],
    )


CHIPS = 4
CORES = 2
DEPTH = 4
LANES = 128
TOK = 128
BLK = CORES * TOK
ROWS = D // (CHIPS * CORES)
SL = D // CHIPS
SLP = -(-SL // LANES) * LANES
FS = FF // CHIPS
BAND = 5 * LANES
HALF = D // 2
PACK = ROWS + ROWS // 2
MESH_ID = pl.DeviceIdType.MESH
F32 = jnp.float32
BF = jnp.bfloat16

SCRATCH = dict(
    tok=((BLK, D), BF),
    cot=((SEQ, D), BF),
    gains=((CHIPS * CORES, 16, LANES), BF),
    gain=((16, D), F32),
    wst=((3, ROWS, D), BF),
    wqs=((CHIPS, ROWS, 3 * SLP), BF),
    wqkv=((D, 3 * SLP), BF),
    wout=((CHIPS * SLP, D), BF),
    wup=((D, FS), BF),
    wdn=((FS, D), BF),
    pbw=((TOK, BAND), BF),
    kern=((CHIPS * CORES, TOK, BAND), BF),
    h1=((SEQ, D), BF),
    h2=((SEQ, D), BF),
    n1=((BLK, D), F32),
    r1=((BLK, LANES), F32),
    n2=((BLK, D), F32),
    r2=((BLK, LANES), F32),
    tmp=((HALF, D), F32),
    tmix=((TOK, 2 * SLP), F32),
    sums=((8, 2 * SLP), F32),
    sig=((SEQ, SLP), F32),
    wgt=((SEQ, SLP), F32),
    val=((SEQ, SLP), BF),
    op=((SEQ, 2 * SLP), BF),
    ratio=((SEQ, SLP), F32),
    rden=((SEQ, SLP), F32),
    mixed=((SEQ, SLP), BF),
    gated=((SEQ, SLP), BF),
    grecv=((CHIPS, BLK, SLP), BF),
    ghs=((CHIPS, TOK, LANES), BF),
    ghr=((CHIPS - 1, TOK, LANES), BF),
    gghs=((CHIPS - 1, TOK, LANES), BF),
    gghr=((CHIPS - 1, TOK, LANES), BF),
    resid=((BLK, D), F32),
    hid=((SEQ, FS), BF),
    dge=((3 * BLK, FS), F32),
    gop=((SEQ, 2 * SLP), F32),
    gupr=((SEQ, FS), BF),
    pout=((CHIPS - 1, BLK, D), BF),
    pgh=((CHIPS - 1, BLK, D), BF),
    own=((BLK, D), F32),
    rbout=((6, TOK, D), BF),
    rbg2=((6, TOK, D), BF),
    rbg1=((6, TOK, D), BF),
    gresid=((BLK, D), F32),
    gattn=((BLK, D), BF),
    ggs=((CHIPS - 1, BLK, LANES), BF),
    ggr=((CHIPS, BLK, SLP), BF),
    gdo=((HALF, D), F32),
    gdx=((HALF, D), F32),
    gds=((CHIPS, ROWS, D), BF),
    gdr=((CHIPS, ROWS, D), BF),
    guo=((D, FS), F32),
    gus=((CHIPS, ROWS, FS), BF),
    gur=((CHIPS, ROWS, FS), BF),
    gqo=((CHIPS, ROWS, SLP), F32),
    gqs=((CHIPS, ROWS, SLP), BF),
    gqr=((CHIPS, ROWS, SLP), BF),
    gvo=((CHIPS, ROWS, 2 * SLP), F32),
    gvs=((CHIPS, ROWS, 2 * SLP), BF),
    gvr=((CHIPS, ROWS, 2 * SLP), BF),
    goo=((CHIPS, ROWS, D), F32),
    gos=((CHIPS, ROWS, D), BF),
    gor=((CHIPS, ROWS, D), BF),
    po=((CHIPS - 1, ROWS, D), BF),
    rbo=((6, ROWS // 2, D), BF),
    gko=((CHIPS, TOK, BAND), F32),
    gks=((CHIPS, TOK, BAND), BF),
    gkr=((CHIPS, TOK, BAND), BF),
    pk=((CHIPS - 1, TOK, BAND), BF),
    rbk=((6, TOK // 2, BAND), BF),
    zdb=((CHIPS, ROWS, D), BF),
    zdr=((CHIPS, ROWS, D), BF),
    zdt=((CHIPS, ROWS, D), BF),
    zub=((CHIPS, ROWS, FS), BF),
    zur=((CHIPS, ROWS, FS), BF),
    zut=((CHIPS, ROWS, FS), BF),
    zqb=((CHIPS, PACK, LANES), BF),
    zqr=((CHIPS, PACK, LANES), BF),
    zqt=((CHIPS, PACK, LANES), BF),
    zvb=((CHIPS, 2 * PACK, LANES), BF),
    zvr=((CHIPS, 2 * PACK, LANES), BF),
    zvt=((CHIPS, 2 * PACK, LANES), BF),
    zob=((ROWS, D), BF),
    zor=((ROWS, D), BF),
    zot=((ROWS, D), BF),
    zkb=((TOK, BAND), BF),
    zkr=((TOK, BAND), BF),
    zkt=((TOK, BAND), BF),
    fout=((BLK, D), BF),
    fgt=((BLK, D), BF),
)
POLLS = {
    1: ("d3",),
    2: ("d1",),
    4: ("d2", "D3",),
    6: ("d0", "D1",),
    9: ("D2",),
    11: ("u3",),
    13: ("D0",),
    15: ("u1",),
    16: ("u2",),
    23: ("u0", "U3",),
    25: ("U1",),
    27: ("U2", "U0",),
    28: ("q3", "q1", "q2", "q0", "o", "+U3", "+U1",),
    29: ("Q3", "v3", "Q1", "v1", "Q2", "v2", "Q0", "v0", "O", "V3", "V1", "V2", "V0", "k", "+U2", "+U0",),
    30: ("+Q3", "+Q1", "+Q2", "+Q0",),
    31: ("K", "+V3", "+V1", "+V2", "+V0", "+O", "+D3", "+D1", "+D2", "+D0", "+K",),
}
N_REMOTE = 200
N_LOCAL = 40


def dot(left, right, left_dim, right_dim):
    return lax.dot_general(
        left, right, (((left_dim,), (right_dim,)), ((), ())), preferred_element_type=F32
    )


def rows_loop(count, step, body, unroll=1):
    def one(i, carry):
        body(pl.multiple_of(i * step, step))
        return carry

    lax.fori_loop(0, count // step, one, 0, unroll=unroll)


def plane_kernel(
    tok_in, len_in, cot_in, ga_in, gm_in, wq_in, wk_in, wv_in, wout_in, wup_in, wdn_in, pb_in,
    out_out, gtok_out, gq_out, gv_out, gwout_out, gup_out, gdn_out, gpb_out,
    *scratch,
):
    m = types.SimpleNamespace(**dict(zip(SCRATCH, scratch)))
    send_sem, recv_sem, local_sem = scratch[len(SCRATCH):]
    r = lax.axis_index("dp")
    z = lax.axis_index("pipe")
    c = lax.rem(r, 2)
    x = lax.rem(r // 2, 2)
    y = r // 4
    b = r // 2
    length = len_in[c]

    def chip(k):
        return 2 * (1 - y if k // 2 else y) + (1 - x if k % 2 else x)

    def peer(k, other=0):
        return (2 * chip(k) + (1 - c if other else c), z)

    jx, jy, jd = chip(1), chip(2), chip(3)
    SIB, PX, PY, PD = peer(0, 1), peer(1), peer(2), peer(3)
    z_near = z + 1 - 2 * lax.rem(z, 2)
    z_far = 3 - z
    ZN, ZF = (r, z_near), (r, z_far)
    outer = z * (3 - z) == 0
    inner = z * (3 - z) != 0

    remote, locals_ = {}, []
    waited = set()
    begun = []

    def make(name, src, dst, to):
        assert name not in remote, name
        i = len(remote)
        cp = pltpu.make_async_remote_copy(
            src_ref=src, dst_ref=dst, send_sem=send_sem.at[i], recv_sem=recv_sem.at[i],
            device_id=to, device_id_type=MESH_ID,
        )
        remote[name] = cp
        return cp

    def send(name, src, dst, to):
        make(name, src, dst, to)
        start(name)

    def start(*names):
        for name in names:
            begun.append(name)
            remote[name].start()

    def got(*names):
        for name in names:
            if name not in waited:
                waited.add(name)
                remote[name].wait_recv()

    def sent(*names):
        for name in names:
            if name + "/s" not in waited:
                waited.add(name + "/s")
                remote[name].wait_send()

    def local_copy(src, dst):
        cp = pltpu.make_async_copy(src, dst, local_sem.at[len(locals_)])
        locals_.append(cp)
        cp.start()
        return cp

    def ds(start, size, unit):
        return pl.ds(pl.multiple_of(start, unit), size)

    def band_at(d):
        return pl.multiple_of(jnp.minimum(jnp.maximum(d - 2, 0), 3) * LANES, LANES)

    def gather_open(name, blk):
        make(name + "X0", blk(b, 0), blk(b, 0), PX)
        make(name + "Y1", blk(b, 1), blk(b, 1), PY)
        make(name + "X1", blk(b, 1), blk(b, 1), PX)
        make(name + "Y0", blk(b, 0), blk(b, 0), PY)
        make(name + "F0", blk(jx, 0), blk(jx, 0), PY)
        make(name + "F1", blk(jy, 1), blk(jy, 1), PX)

    def gather_start(name):
        start(name + "X0", name + "Y1", name + "X1", name + "Y0")

    def gather_forward(name):
        got(name + "X0")
        start(name + "F0")
        got(name + "Y1")
        start(name + "F1")

    def gather_wait(name, k):
        got(*{1: (name + "X0", name + "X1"), 2: (name + "Y0", name + "Y1"), 3: (name + "F0", name + "F1")}[k])

    fetch = lax.rem(z, 2) == c
    passed = lax.rem(z, 2) != c
    in_fetch = []

    def relay_open(name, place):
        for k in (1, 2, 3):
            make(f"{name}Z{k}", place(k), place(k), ZN)
            in_fetch.append(f"{name}Z{k}")

    def relay(name, place, arrive):
        for k in (1, 2, 3):

            @pl.when(fetch)
            def _(k=k):
                arrive(k)
                start(f"{name}Z{k}")

            @pl.when(passed)
            def _(k=k):
                remote[f"{name}Z{k}"].wait_recv()

            waited.add(f"{name}Z{k}")
            send(f"{name}S{k}", place(k), place(k), SIB)

    def scatter_diagonal(name, part, buf, half):
        send(name + "0", part.at[2, pl.ds(half, half)], buf.at[0], PX)
        send(name + "1", part.at[2, pl.ds(0, half)], buf.at[1], PY)

    def scatter_direct_x(name, part, buf, half):
        send(name + "2", part.at[0, pl.ds(half, half)], buf.at[2], PX)

    def scatter_direct_y(name, part, buf, half):
        send(name + "3", part.at[1, pl.ds(0, half)], buf.at[3], PY)

    def scatter_combine(name, part, buf, half):
        got(name + "1")
        part[0, pl.ds(0, half), :] = (
            part[0, pl.ds(0, half), :].astype(F32) + buf[1].astype(F32)
        ).astype(BF)
        send(name + "4", part.at[0, pl.ds(0, half)], buf.at[4], PX)
        got(name + "0")
        part[1, pl.ds(half, half), :] = (
            part[1, pl.ds(half, half), :].astype(F32) + buf[0].astype(F32)
        ).astype(BF)
        send(name + "5", part.at[1, pl.ds(half, half)], buf.at[5], PY)

    def scatter_wait(name):
        got(name + "2", name + "3", name + "4", name + "5")

    def scatter_sum(buf, half, h, rows):
        if h == 0:
            return buf[3, rows, :].astype(F32) + buf[4, rows, :].astype(F32)
        return buf[2, rows, :].astype(F32) + buf[5, rows, :].astype(F32)

    zitems = {}

    def z_open(name, base, near, total):
        zitems[name] = (
            base,
            near,
            total,
            make(name + "a", base, near, ZN),
            make(name + "b", base, total, ZF),
            make(name + "c", total, total, ZN),
        )

    def z_start(name):
        item = zitems[name]

        @pl.when(outer)
        def _():
            item[3].start()

    def z_mid(name):
        base, near, total, into, across, back = zitems[name]

        @pl.when(inner)
        def _():
            into.wait_recv()
            base[...] = (base[...].astype(F32) + near[...].astype(F32)).astype(BF)
            across.start()

    def z_end(name):
        base, near, total, into, across, back = zitems[name]

        @pl.when(inner)
        def _():
            across.wait_recv()
            total[...] = (base[...].astype(F32) + total[...].astype(F32)).astype(BF)
            back.start()

    def z_take(name):
        back = zitems[name][5]

        @pl.when(outer)
        def _():
            back.wait_recv()

    def z_close(name):
        base, near, total, into, across, back = zitems[name]

        @pl.when(outer)
        def _():
            into.wait_send()

        @pl.when(inner)
        def _():
            across.wait_send()
            back.wait_send()

    for k in range(CHIPS):
        j = chip(k)
        z_open(f"zd{k}", m.zdb.at[j], m.zdr.at[j], m.zdt.at[j])
        z_open(f"zu{k}", m.zub.at[j], m.zur.at[j], m.zut.at[j])
        z_open(f"zq{k}", m.zqb.at[j], m.zqr.at[j], m.zqt.at[j])
        z_open(f"zv{k}", m.zvb.at[j], m.zvr.at[j], m.zvt.at[j])
    z_open("zo", m.zob, m.zor, m.zot)
    z_open("zk", m.zkb, m.zkr, m.zkt)
    ORDER = (3, 1, 2, 0)

    onward = {}

    def prepare(which, k):
        j = chip(k)
        whole = dict(D=m.zdt, U=m.zut, Q=m.zqt, V=m.zvt, O=m.zot, K=m.zkt)[which]
        out = dict(D=gdn_out, U=gup_out, Q=gq_out, V=gv_out, O=gwout_out, K=gpb_out)[which]
        if which in "UQV" and k:
            name = f"f{which}{k}"
            begun.append(name)
            return make(name, whole.at[j], out.at[b], peer(k))
        src, dst = (whole, out) if which in "OK" else (whole.at[j], out.at[j])
        locals_.append(pltpu.make_async_copy(src, dst, local_sem.at[len(locals_)]))
        return locals_[-1]

    def poll(place):
        for step in POLLS.get(place, ()):
            code = step.strip("+")
            name = "z" + code.lower()
            if code.islower():
                z_mid(name)
                continue
            if name not in onward:
                onward[name] = prepare(code[0], int(code[1:] or 0))
            if step == code:
                z_end(name)
                pl.when(inner)(onward[name].start)
            else:
                z_take(name)
                pl.when(outer)(onward[name].start)

    own_half = ds(c * TOK, TOK, TOK)
    other_half = ds((1 - c) * TOK, TOK, TOK)
    l_tok = local_copy(tok_in.at[c], m.tok.at[own_half])
    l_w = [local_copy(w, m.wst.at[i]) for i, w in enumerate((wq_in, wk_in, wv_in))]
    l_pb = local_copy(pb_in.at[:, ds(band_at(r), BAND, LANES)], m.pbw)

    def wout_rows(j, core):
        return m.wout.at[ds(j * SLP + core * ROWS, ROWS, 32)]

    l_wout = local_copy(wout_in, wout_rows(b, c))
    up_rows = ds(r * ROWS, ROWS, 32)
    l_wup = local_copy(wup_in.at[:, ds(b * FS, FS, LANES)], m.wup.at[up_rows])
    dn_rows = ds(c * HALF, HALF, LANES)
    l_wdn = local_copy(wdn_in, m.wdn.at[dn_rows])
    cot_half = ds(b * BLK + c * TOK, TOK, TOK)
    l_cot = local_copy(cot_in.at[c], m.cot.at[cot_half])

    line = lax.broadcasted_iota(jnp.int32, (16, LANES), 0)
    fill = jnp.zeros((1, LANES - ROWS), F32)
    both_gains = [
        jnp.broadcast_to(jnp.concatenate([g[...].astype(F32), fill], axis=1), (16, LANES)) for g in (ga_in, gm_in)
    ]
    m.gains[r] = jnp.where(line == 0, both_gains[0], both_gains[1]).astype(BF)

    barrier = pltpu.get_barrier_semaphore()
    everyone = [peer(k, o) for k in range(CHIPS) for o in range(CORES) if (k, o) != (0, 0)] + [ZN, ZF]
    for other in everyone:
        pl.semaphore_signal(barrier, inc=1, device_id=other, device_id_type=MESH_ID)
    l_pb.wait()
    t_ids = r * TOK + lax.broadcasted_iota(jnp.int32, (TOK, BAND), 0)
    u_ids = band_at(r) + lax.broadcasted_iota(jnp.int32, (TOK, BAND), 1)
    in_band = jnp.abs(t_ids - u_ids) < WIN
    m.kern[r] = jnp.where(in_band, jnp.exp(m.pbw[...].astype(F32)) - 1.0, 0.0).astype(BF)

    for cp in l_w:
        cp.wait()
    for i in range(3):
        w_rows = m.wst[i].astype(F32)
        for j in range(CHIPS):
            piece = w_rows[:, j * SL : (j + 1) * SL]
            m.wqs[j, :, i * SLP : (i + 1) * SLP] = jnp.concatenate(
                [piece, jnp.zeros((ROWS, SLP - SL), F32)], axis=1
            ).astype(BF)
    pl.semaphore_wait(barrier, len(everyone))

    send("tokS", tok_in.at[1 - c], m.tok.at[own_half], SIB)
    gain_names = []
    for k in range(CHIPS):
        for o in range(CORES):
            if (k, o) != (0, 0):
                gain_names.append(f"gain{k}{o}")
                send(gain_names[-1], m.gains.at[r], m.gains.at[r], peer(k, o))

    def wout_blk(j, h):
        return m.wout.at[ds(j * SLP + c * ROWS + h * (ROWS // 2), ROWS // 2, 16)]

    gather_open("wo", wout_blk)
    in_fetch.extend("wo" + part for part in ("X0", "X1", "Y0", "Y1", "F0", "F1"))
    l_wout.wait()

    @pl.when(fetch)
    def _():
        gather_start("wo")

    for k, to in ((1, PX), (2, PY), (3, PD)):
        make(f"wq{k}", m.wqs.at[chip(k)], m.wqkv.at[up_rows], to)
        in_fetch.append(f"wq{k}")

    @pl.when(fetch)
    def _():
        start("wq1", "wq2", "wq3")

    def kern_blk(j, h):
        return m.kern.at[2 * j + c, pl.ds(h * (TOK // 2), TOK // 2)]

    gather_open("kn", kern_blk)
    in_fetch.extend("kn" + part for part in ("X0", "X1", "Y0", "Y1", "F0", "F1"))

    @pl.when(fetch)
    def _():
        gather_start("kn")

    send("knS0", m.kern.at[r], m.kern.at[r], SIB)

    send("wqS0", m.wqs.at[b], m.wqkv.at[up_rows], SIB)
    m.wqkv[up_rows, :] = m.wqs[b]

    def norm(src, n_ref, r_ref):
        def body(i):
            rows = pl.ds(i, 32)
            values = src[rows, :].astype(F32)
            centre = values - jnp.mean(values, axis=-1, keepdims=True)
            spread = jnp.mean(centre * centre, axis=-1, keepdims=True)
            rinv = lax.rsqrt(spread + EPSILON)
            n_ref[rows, :] = centre * rinv
            r_ref[rows, :] = jnp.broadcast_to(rinv, (32, LANES))

        rows_loop(BLK, 32, body, unroll=2)

    def scale(n_ref, gain_row, dst, base):
        def body(i):
            dst[pl.ds(pl.multiple_of(base + i, 32), 32), :] = (
                n_ref[pl.ds(i, 32), :] * m.gain[gain_row : gain_row + 1, :]
            ).astype(BF)

        rows_loop(BLK, 32, body, unroll=2)

    l_tok.wait()
    got("tokS")
    norm(m.tok, m.n1, m.r1)
    got(*gain_names)
    m.gain[...] = jnp.concatenate(
        [m.gains[d].astype(F32)[:, :ROWS] for d in range(CHIPS * CORES)], axis=1
    )
    scale(m.n1, 0, m.h1, b * BLK)

    def h1_blk(j, h):
        return m.h1.at[ds(j * BLK + h * TOK, TOK, TOK)]

    gather_open("h1", h1_blk)
    gather_start("h1")

    def w_place(ref):
        return lambda k: ref.at[ds((2 * chip(k) + c) * ROWS, ROWS, 32)]

    wq_place = w_place(m.wqkv)
    relay_open("wq", wq_place)
    relay("wq", wq_place, lambda k: got(f"wq{k}"))

    @pl.when(fetch)
    def _():
        gather_forward("kn")

    gather_forward("h1")
    for j in range(CHIPS):
        m.wout[j * SLP + SL : (j + 1) * SLP, :] = jnp.zeros((SLP - SL, D), BF)

    for k, to in ((1, PX), (2, PY), (3, PD)):
        make(f"wu{k}", wup_in.at[:, ds(chip(k) * FS, FS, LANES)], m.wup.at[up_rows], to)
        in_fetch.append(f"wu{k}")

    @pl.when(fetch)
    def _():
        gather_forward("wo")
        start("wu1", "wu2", "wu3")

    send("woS0", wout_rows(b, c), wout_rows(b, c), SIB)
    l_wup.wait()
    send("wuS0", m.wup.at[up_rows], m.wup.at[up_rows], SIB)
    l_wdn.wait()
    send("wdS", m.wdn.at[dn_rows], m.wdn.at[dn_rows], SIB)
    send("cotS", cot_in.at[1 - c], m.cot.at[cot_half], SIB)
    got("wqS0", "wqS1", "wqS2", "wqS3")

    def blk_rows(j):
        return ds(j * BLK, BLK, BLK)

    def project(j):
        m.tmp[0:BLK, :] = dot(m.h1[blk_rows(j), :], m.wqkv[...], 1, 0)

        def body(i):
            rows = pl.ds(i, 16)
            at = pl.multiple_of(j * BLK + i, 16)
            to = pl.ds(at, 16)
            q = m.tmp[rows, 0:SLP]
            m.sig[to, :] = 1.0 / (1.0 + jnp.exp(-q))
            keys = m.tmp[rows, SLP : 2 * SLP].astype(BF).astype(F32)
            values = m.tmp[rows, 2 * SLP : 3 * SLP].astype(BF)
            pos = at + lax.broadcasted_iota(jnp.int32, (16, SLP), 0)
            weighted = jnp.where(pos < length, jnp.exp(keys), 0.0)
            m.wgt[to, :] = weighted
            m.val[to, :] = values
            m.op[to, 0:SLP] = (weighted * values.astype(F32)).astype(BF)
            m.op[to, SLP : 2 * SLP] = weighted.astype(BF)

        rows_loop(BLK, 16, body, unroll=2)

    project(b)
    kn_place = lambda k: m.kern.at[2 * chip(k) + c]
    relay_open("kn", kn_place)
    relay("kn", kn_place, lambda k: gather_wait("kn", k))
    for k in (1, 2):
        gather_wait("h1", k)
        project(chip(k))
    gather_wait("h1", 3)
    project(jd)
    l_cot.wait()
    got("cotS")

    def cot_blk(j, h):
        return m.cot.at[ds(j * BLK + h * TOK, TOK, TOK)]

    gather_open("ct", cot_blk)
    start("ctX0", "ctY1")

    got("knS0", "knS1", "knS2", "knS3")
    ones = jnp.ones((8, SEQ), BF)
    m.sums[...] = dot(ones, m.op[...], 1, 0)

    def mix(j, half):
        d = 2 * j + half
        m.tmix[...] = dot(m.kern[d], m.op[pl.ds(band_at(d), BAND), :], 1, 0)

        def body(i):
            rows = pl.ds(i, 32)
            at = pl.multiple_of(d * TOK + i, 32)
            to = pl.ds(at, 32)
            pos = at + lax.broadcasted_iota(jnp.int32, (32, SLP), 0)
            valid = jnp.where(pos < length, 1.0, 0.0)
            num = m.tmix[rows, 0:SLP] + m.sums[0:1, 0:SLP]
            den = m.tmix[rows, SLP : 2 * SLP] + m.sums[0:1, SLP : 2 * SLP] + 1.0 - valid
            rden = 1.0 / den
            ratio = num * rden
            mixed = (ratio * valid).astype(BF)
            m.ratio[to, :] = ratio
            m.rden[to, :] = rden * valid
            m.mixed[to, :] = mixed
            gated = m.sig[to, :] * mixed.astype(F32)
            m.gated[to, :] = gated.astype(BF)
            high = gated[:, LANES:]
            m.ghs[j, rows, :] = jnp.where(
                half == 0, high, m.ghs[j, rows, :].astype(F32) + pltpu.roll(high, SL - LANES, 1)
            ).astype(BF)

        rows_loop(TOK, 32, body, unroll=2)

    def mix_block(j):
        def one(i, carry):
            mix(j, i)
            return carry

        lax.fori_loop(0, CORES, one, 0)

    low_lanes = pl.ds(0, LANES)

    def unpack(dst, high):
        lane = lax.broadcasted_iota(jnp.int32, (TOK, LANES), 1)
        both = high[...].astype(F32)
        for h in range(2):
            part = both if h == 0 else pltpu.roll(both, LANES - (SL - LANES), 1)
            dst[h * TOK : (h + 1) * TOK, LANES:] = jnp.where(lane < SL - LANES, part, 0.0).astype(BF)

    for k, to in ((3, PD), (1, PX), (2, PY)):
        j = chip(k)
        mix_block(j)
        send(f"ga{k}", m.gated.at[blk_rows(j), low_lanes], m.grecv.at[k, :, low_lanes], to)
        send(f"gh{k}", m.ghs.at[j], m.ghr.at[k - 1], to)
    mix_block(b)
    m.grecv[0] = m.gated[blk_rows(b), :]

    gather_forward("ct")
    wo_place = lambda k: wout_rows(chip(k), c)
    relay_open("wo", wo_place)
    relay("wo", wo_place, lambda k: gather_wait("wo", k))
    wu_place = w_place(m.wup)
    relay_open("wu", wu_place)
    relay("wu", wu_place, lambda k: got(f"wu{k}"))

    got("woS0", "woS1", "woS2", "woS3")
    m.resid[...] = m.tok[...].astype(F32)
    for k in (0, 1, 2, 3):
        if k:
            got(f"ga{k}", f"gh{k}")
            unpack(m.grecv.at[k], m.ghr.at[k - 1])
        m.resid[...] += dot(m.grecv[k], m.wout[ds(chip(k) * SLP, SLP, SLP), :], 1, 0)
    norm(m.resid, m.n2, m.r2)
    scale(m.n2, 1, m.h2, b * BLK)

    def h2_blk(j, h):
        return m.h2.at[ds(j * BLK + h * TOK, TOK, TOK)]

    gather_open("h2", h2_blk)
    gather_start("h2")

    got("wuS0", "wuS1", "wuS2", "wuS3", "wdS")

    def ff_forward(k):
        j = chip(k)
        keep = (k % 3) * BLK
        m.tmp[0:BLK, :] = dot(m.h2[blk_rows(j), :], m.wup[...], 1, 0)

        def gelu(i):
            v = m.tmp[pl.ds(i, 16), :]
            square = v * v
            t = jnp.tanh(GELU_SCALE * v * (1.0 + GELU_CUBE * square))
            half = 0.5 * (1.0 + t)
            m.hid[pl.ds(pl.multiple_of(j * BLK + i, 16), 16), :] = (v * half).astype(BF)
            m.dge[pl.ds(pl.multiple_of(keep + i, 16), 16), :] = half + 0.5 * v * (1.0 - t * t) * (
                GELU_SCALE * (1.0 + 3.0 * GELU_CUBE * square)
            )

        rows_loop(BLK, 16, gelu, unroll=2)

    def ff_out(k):
        part = dot(m.hid[blk_rows(chip(k)), :], m.wdn[...], 1, 0)
        if k == 0:
            m.resid[...] += part
        else:
            m.pout[k - 1] = part.astype(BF)

    def ff_backward(k):
        j = chip(k)
        keep = (k % 3) * BLK
        m.tmp[0:BLK, :] = dot(m.cot[blk_rows(j), :], m.wdn[...], 1, 1)

        def back(i):
            m.gupr[pl.ds(pl.multiple_of(j * BLK + i, 16), 16), :] = (
                m.tmp[pl.ds(i, 16), :] * m.dge[pl.ds(pl.multiple_of(keep + i, 16), 16), :]
            ).astype(BF)

        rows_loop(BLK, 16, back, unroll=2)
        part = dot(m.gupr[blk_rows(j), :], m.wup[...], 1, 1)
        if k == 0:
            m.own[...] = part
        else:
            m.pgh[k - 1] = part.astype(BF)

    other_cols = ds((1 - c) * HALF, HALF, LANES)
    own_cols = ds(c * HALF, HALF, LANES)

    def ff_grads(k):
        rows = blk_rows(chip(k))
        for dst, at, left, cols, right in (
            (m.gdx, 0, m.hid, other_cols, m.cot),
            (m.gdo, 0, m.hid, own_cols, m.cot),
            (m.guo, 0, m.h2, pl.ds(0, HALF), m.gupr),
            (m.guo, HALF, m.h2, pl.ds(HALF, HALF), m.gupr),
        ):
            part = dot(left[rows, cols], right[rows, :], 0, 0)
            to = pl.ds(at, HALF)
            if k == 0:
                dst[to, :] = part
            else:
                dst[to, :] += part

    ff_forward(0)
    ff_backward(0)
    gather_forward("h2")
    start("ctX1", "ctY0")
    ff_out(0)
    ff_grads(0)
    for k in (1, 2):
        gather_wait("h2", k)
        ff_forward(k)
    gather_wait("h2", 3)
    ff_forward(3)
    gather_wait("ct", 3)
    ff_backward(3)
    scatter_diagonal("g2", m.pgh, m.rbg2, TOK)
    gather_wait("ct", 1)
    ff_backward(1)
    scatter_direct_x("g2", m.pgh, m.rbg2, TOK)
    gather_wait("ct", 2)
    ff_backward(2)
    scatter_direct_y("g2", m.pgh, m.rbg2, TOK)
    ff_grads(3)
    ff_grads(1)
    scatter_combine("g2", m.pgh, m.rbg2, TOK)
    ff_grads(2)

    for j in range(CHIPS):
        m.gds[j] = m.gdx[j * ROWS : (j + 1) * ROWS, :].astype(BF)
    send("gdS", m.gds, m.gdr, SIB)
    for j in range(CHIPS):
        m.gus[j] = m.guo[ds((2 * j + 1 - c) * ROWS, ROWS, 32), :].astype(BF)
    send("guS", m.gus, m.gur, SIB)

    def split_rows(left, right, kept, leaving):
        width = right.shape[1]
        for i in range(2):
            m.tmp[:, 0:width] = dot(left[:, i * HALF : (i + 1) * HALF], right[...], 0, 0)
            for q in range(2):
                kept[2 * i + q] = m.tmp[ds((2 * q + c) * ROWS, ROWS, 32), 0:width]
                leaving[2 * i + q] = m.tmp[ds((2 * q + 1 - c) * ROWS, ROWS, 32), 0:width].astype(BF)

    def pair_sum(name, kept, came, base):
        for k in ORDER:
            j = chip(k)
            base[j] = (kept(j) + came[j].astype(F32)).astype(BF)
            z_start(f"{name}{k}")

    def pack(dst, at, rows):
        n = rows.shape[0]
        dst[at : at + n, :] = rows[:, :LANES].astype(BF)
        dst[at + n : at + n + n // 2, :] = jnp.concatenate(
            [rows[: n // 2, LANES:SL], rows[n // 2 :, LANES:SL]], axis=1
        ).astype(BF)

    def pair_sum_packed(name, kept, came, base):
        for k in ORDER:
            j = chip(k)
            total = kept[j] + came[j].astype(F32)
            for i in range(total.shape[1] // SLP):
                pack(base.at[j], i * PACK, total[:, i * SLP : (i + 1) * SLP])
            z_start(f"{name}{k}")

    got("gdS")
    pair_sum("zd", lambda j: m.gdo[ds(j * ROWS, ROWS, 32), :], m.gdr, m.zdb)
    got("guS")
    pair_sum("zu", lambda j: m.guo[ds((2 * j + c) * ROWS, ROWS, 32), :], m.gur, m.zub)
    for k in (3, 1, 2):
        ff_out(k)
    scatter_diagonal("ou", m.pout, m.rbout, TOK)
    poll(1)

    scatter_wait("g2")

    def norm_back(total, gain_row, n_ref, r_ref, i, base):
        rows = pl.ds(i, 32)
        e = total * m.gain[gain_row : gain_row + 1, :]
        n = n_ref[rows, :]
        mean_e = jnp.mean(e, axis=-1, keepdims=True)
        mean_en = jnp.mean(e * n, axis=-1, keepdims=True)
        return base + r_ref[rows, 0:1] * (e - mean_e - n * mean_en)

    for h in range(2):

        def back_two(i, h=h):
            at = pl.multiple_of(h * TOK + i, 32)
            rows = pl.ds(at, 32)
            total = m.own[rows, :] + scatter_sum(m.rbg2, TOK, h, pl.ds(i, 32))
            base = m.cot[pl.ds(pl.multiple_of(b * BLK + at, 32), 32), :].astype(F32)
            g = norm_back(total, 1, m.n2, m.r2, at, base)
            m.gresid[rows, :] = g
            m.gattn[rows, :] = g.astype(BF)

        rows_loop(TOK, 32, back_two, unroll=2)
    poll(2)

    for k, to in ((3, PD), (1, PX), (2, PY)):
        part = dot(m.gattn[...], m.wout[ds(chip(k) * SLP, SLP, SLP), :], 1, 1)
        m.ggs[k - 1] = part[:, :LANES].astype(BF)
        send(f"gg{k}", m.ggs.at[k - 1], m.ggr.at[k, :, low_lanes], to)
        high = part[:, LANES:]
        m.gghs[k - 1] = (high[:TOK] + pltpu.roll(high[TOK:], SL - LANES, 1)).astype(BF)
        send(f"gi{k}", m.gghs.at[k - 1], m.gghr.at[k - 1], to)
    m.ggr[0] = dot(m.gattn[...], m.wout[ds(b * SLP, SLP, SLP), :], 1, 1).astype(BF)
    poll(3)
    for k in range(CHIPS):
        m.tmp[0:SLP, :] = dot(m.grecv[k], m.gattn[...], 0, 0)
        m.goo[k] = m.tmp[ds(c * ROWS, ROWS, 32), :]
        m.gos[k] = m.tmp[ds((1 - c) * ROWS, ROWS, 32), :].astype(BF)
    send("goS", m.gos, m.gor, SIB)
    poll(4)

    gqkv = m.hid
    gres = m.h2
    sent("h2X0", "h2X1", "h2Y0", "h2Y1", "h2F0", "h2F1")

    def mix_back(k):
        j = chip(k)

        def body(i):
            at = pl.multiple_of(j * BLK + i, 16)
            rows = pl.ds(at, 16)
            gg = m.ggr[k, pl.ds(i, 16), :].astype(F32)
            sig = m.sig[rows, :]
            gm = (gg * sig).astype(BF).astype(F32)
            gqkv[rows, 0:SLP] = (
                gg * m.mixed[rows, :].astype(F32) * sig * (1.0 - sig)
            ).astype(BF)
            gnum = gm * m.rden[rows, :]
            gres[rows, 0:SLP] = gnum.astype(BF)
            gres[rows, SLP : 2 * SLP] = (-gnum * m.ratio[rows, :]).astype(BF)

        rows_loop(BLK, 16, body, unroll=2)

    mix_back(0)
    poll(5)
    got("goS")
    for k in (1, 2, 3):
        m.po[k - 1] = (m.goo[k] + m.gor[k].astype(F32)).astype(BF)
    scatter_diagonal("wg", m.po, m.rbo, ROWS // 2)
    scatter_direct_x("wg", m.po, m.rbo, ROWS // 2)
    scatter_direct_y("wg", m.po, m.rbo, ROWS // 2)
    scatter_direct_x("ou", m.pout, m.rbout, TOK)
    scatter_direct_y("ou", m.pout, m.rbout, TOK)
    poll(6)
    for k in (1, 2, 3):
        got(f"gg{k}", f"gi{k}")
        unpack(m.ggr.at[k], m.gghr.at[k - 1])
        mix_back(k)
        poll(6 + k)
    scatter_combine("wg", m.po, m.rbo, ROWS // 2)
    m.sums[...] = dot(ones, gres[:, 0 : 2 * SLP], 1, 0)
    m.gop[...] = jnp.broadcast_to(m.sums[0:1, :], (SEQ, 2 * SLP))
    poll(10)

    def kernel_grad(d):
        return dot(
            gres[ds(d * TOK, TOK, TOK), 0 : 2 * SLP], m.op[pl.ds(band_at(d), BAND), :], 1, 1
        )

    for k in range(CHIPS):
        m.gks[k] = kernel_grad(2 * chip(k) + 1 - c).astype(BF)
    send("gkS", m.gks, m.gkr, SIB)
    poll(11)
    split_rows(m.h1, gqkv.at[:, 0:SLP], m.gqo, m.gqs)
    send("gqS", m.gqs, m.gqr, SIB)
    poll(12)
    for k in range(CHIPS):
        m.gko[k] = kernel_grad(2 * chip(k) + c)
    poll(13)
    got("gkS")
    for k in (1, 2, 3):
        m.pk[k - 1] = (m.gko[k] + m.gkr[k].astype(F32)).astype(BF)
    scatter_diagonal("kg", m.pk, m.rbk, TOK // 2)
    scatter_direct_x("kg", m.pk, m.rbk, TOK // 2)
    scatter_direct_y("kg", m.pk, m.rbk, TOK // 2)
    poll(14)

    def mix_t(d, carry):
        at = pl.ds(band_at(d), BAND)
        m.gop[at, :] += dot(m.kern[d], gres[ds(d * TOK, TOK, TOK), 0 : 2 * SLP], 0, 0)
        return carry

    lax.fori_loop(0, CHIPS * CORES, mix_t, 0)
    poll(15)

    def keys_back(i):
        rows = pl.ds(i, 16)
        gkv = m.gop[rows, 0:SLP]
        w = m.wgt[rows, :]
        gqkv[rows, SLP : 2 * SLP] = (
            (gkv * m.val[rows, :].astype(F32) + m.gop[rows, SLP : 2 * SLP]) * w
        ).astype(BF)
        gqkv[rows, 2 * SLP : 3 * SLP] = (gkv * w).astype(BF)

    rows_loop(SEQ, 16, keys_back, unroll=2)
    poll(16)

    sent("g20", "g21", "g22", "g23", "g24", "g25")
    for k in ORDER:
        part = dot(gqkv[blk_rows(chip(k)), :], m.wqkv[...], 1, 1)
        if k == 0:
            m.own[...] = part
        else:
            m.pgh[k - 1] = part.astype(BF)
        if k == 3:
            scatter_diagonal("g1", m.pgh, m.rbg1, TOK)
        if k == 1:
            scatter_direct_x("g1", m.pgh, m.rbg1, TOK)
        if k == 2:
            scatter_direct_y("g1", m.pgh, m.rbg1, TOK)
        poll(17 + k)
    got("gqS")
    pair_sum_packed("zq", m.gqo, m.gqr, m.zqb)
    poll(21)

    def scattered(dst, mine, came, buf, half):
        for h in range(2):
            rows = pl.ds(h * half, half)
            dst[rows, :] = (
                mine[0, rows, :] + came[0, rows, :].astype(F32)
                + scatter_sum(buf, half, h, pl.ds(0, half))
            ).astype(BF)

    scatter_wait("wg")
    scattered(m.zob, m.goo, m.gor, m.rbo, ROWS // 2)
    z_start("zo")
    poll(22)
    split_rows(m.h1, gqkv.at[:, SLP : 3 * SLP], m.gvo, m.gvs)
    send("gvS", m.gvs, m.gvr, SIB)
    poll(23)
    scatter_combine("kg", m.pk, m.rbk, TOK // 2)
    poll(24)
    scatter_combine("g1", m.pgh, m.rbg1, TOK)
    poll(25)
    got("gvS")
    pair_sum_packed("zv", m.gvo, m.gvr, m.zvb)
    poll(26)
    scatter_combine("ou", m.pout, m.rbout, TOK)
    poll(27)
    poll(28)
    scatter_wait("kg")
    scattered(m.zkb, m.gko, m.gkr, m.rbk, TOK // 2)
    z_start("zk")

    poll(29)

    poll(30)
    scatter_wait("ou")
    for h in range(2):

        def out_rows(i, h=h):
            rows = pl.ds(pl.multiple_of(h * TOK + i, 32), 32)
            m.fout[rows, :] = (
                m.resid[rows, :] + scatter_sum(m.rbout, TOK, h, pl.ds(i, 32))
            ).astype(BF)

        rows_loop(TOK, 32, out_rows)
    send("outS", m.fout.at[other_half], out_out.at[c], SIB)
    local_copy(m.fout.at[own_half], out_out.at[c])

    scatter_wait("g1")
    for h in range(2):

        def back_one(i, h=h):
            at = pl.multiple_of(h * TOK + i, 32)
            rows = pl.ds(at, 32)
            total = m.own[rows, :] + scatter_sum(m.rbg1, TOK, h, pl.ds(i, 32))
            m.fgt[rows, :] = norm_back(total, 0, m.n1, m.r1, at, m.gresid[rows, :]).astype(BF)

        rows_loop(TOK, 32, back_one, unroll=2)
    send("gtS", m.fgt.at[other_half], gtok_out.at[c], SIB)
    local_copy(m.fgt.at[own_half], gtok_out.at[c])
    poll(31)

    for cp in locals_:
        if all(cp is not done for done in (l_tok, l_pb, l_wout, l_wup, l_wdn, l_cot, *l_w)):
            cp.wait()
    for name in begun:
        if name not in in_fetch:
            got(name)
            sent(name)

    @pl.when(fetch)
    def _():
        for name in in_fetch:
            sent(name)

    for name in zitems:
        z_close(name)


FIN_IN = dict(
    gq=((CHIPS, PACK, LANES), BF),
    gv=((CHIPS, 2 * PACK, LANES), BF),
    gup=((CHIPS, ROWS, FS), BF),
    gdn=((FF // (CHIPS * CORES), D), BF),
    gwout=((ROWS, D), BF),
    gpb=((TOK, BAND), BF),
    wq=((ROWS, D), BF),
    wk=((ROWS, D), BF),
    wv=((ROWS, D), BF),
    wup=((ROWS, FF), BF),
    pb=((TOK, BAND), BF),
    out=((2, TOK, D), BF),
    gtok=((2, TOK, D), BF),
)
FIN_OUT = dict(
    q=((ROWS, D), F32),
    k=((ROWS, D), F32),
    v=((ROWS, D), F32),
    o=((ROWS, D), F32),
    up=((ROWS, FF), F32),
    dn=((FF // (CHIPS * CORES), D), F32),
    bias=((TOK, SEQ), F32),
)


def finish_kernel(
    out_in, gtok_in, gq_in, gv_in, gwout_in, gup_in, gdn_in, gpb_in, ga_in, gm_in,
    wq_in, wk_in, wv_in, wup_in, pb_in,
    out_out, gtok_out, ga_out, q_out, k_out, v_out, o_out, gm_out, up_out, dn_out, bias_out,
    *scratch,
):
    m = types.SimpleNamespace(**dict(zip((*FIN_IN, *FIN_OUT), scratch)))
    in_sem, out_sem = scratch[len(FIN_IN) + len(FIN_OUT):]
    start = pl.multiple_of(
        jnp.minimum(jnp.maximum(lax.axis_index("dp") - 2, 0), 3) * LANES, LANES
    )
    stores = []

    def store(src, dst):
        stores.append(pltpu.make_async_copy(src, dst, out_sem.at[len(stores)]))
        stores[-1].start()

    sources = dict(
        gdn=gdn_in, gup=gup_in, wup=wup_in, out=out_in, gtok=gtok_in, gq=gq_in, wq=wq_in, gv=gv_in, wk=wk_in,
        wv=wv_in, gwout=gwout_in, gpb=gpb_in, pb=pb_in.at[:, pl.ds(start, BAND)],
    )
    loads = types.SimpleNamespace(
        **{
            name: pltpu.make_async_copy(src, vars(m)[name], in_sem.at[i])
            for i, (name, src) in enumerate(sources.items())
        }
    )
    for cp in vars(loads).values():
        cp.start()

    loads.gdn.wait()
    m.dn[...] = m.gdn[...].astype(F32)
    store(m.dn, dn_out)

    def as_row(column, gain):
        square = jnp.broadcast_to(column, (ROWS, LANES))
        return jnp.transpose(square)[0:1, :] / gain[...].astype(F32)

    loads.gup.wait()
    loads.wup.wait()
    column = jnp.zeros((ROWS, 1), F32)
    for j in range(CHIPS):
        cols = slice(j * FS, (j + 1) * FS)
        g = m.gup[j].astype(F32)
        m.up[:, cols] = g
        store(m.up.at[:, cols], up_out.at[:, cols])
        column += jnp.sum(g * m.wup[:, cols].astype(F32), axis=1, keepdims=True)
    loads.out.wait()
    store(m.out, out_out)
    loads.gtok.wait()
    store(m.gtok, gtok_out)
    gm_out[...] = as_row(column, gm_in)

    def unpack(ref, j, at):
        low = ref[j, at : at + ROWS, :].astype(F32)
        high = ref[j, at + ROWS : at + PACK, :].astype(F32)
        rest = SL - LANES
        return jnp.concatenate(
            [low, jnp.concatenate([high[:, :rest], high[:, rest:]], axis=0)], axis=1
        )

    column = jnp.zeros((ROWS, 1), F32)
    for needs, ref, at, w, mine, dst in (
        ((loads.gq, loads.wq), m.gq, 0, m.wq, m.q, q_out),
        ((loads.gv, loads.wk), m.gv, 0, m.wk, m.k, k_out),
        ((loads.wv,), m.gv, PACK, m.wv, m.v, v_out),
    ):
        for cp in needs:
            cp.wait()
        g = jnp.concatenate([unpack(ref, j, at) for j in range(CHIPS)], axis=1)
        mine[...] = g
        store(mine, dst)
        column += jnp.sum(g * w[...].astype(F32), axis=1, keepdims=True)
    ga_out[...] = as_row(column, ga_in)

    loads.gwout.wait()
    m.o[...] = m.gwout[...].astype(F32)
    store(m.o, o_out)
    loads.gpb.wait()
    loads.pb.wait()
    t_ids = lax.axis_index("dp") * TOK + lax.broadcasted_iota(jnp.int32, (TOK, BAND), 0)
    u_ids = start + lax.broadcasted_iota(jnp.int32, (TOK, BAND), 1)
    m.bias[...] = jnp.zeros((TOK, SEQ), F32)
    m.bias[:, pl.ds(start, BAND)] = jnp.where(
        jnp.abs(t_ids - u_ids) < WIN, m.gpb[...].astype(F32) * jnp.exp(m.pb[...].astype(F32)), 0.0
    )
    store(m.bias, bias_out)
    for cp in stores:
        cp.wait()


def plane_program(
    tokens, lengths, cotangent, gain_attn, w_query, w_key, w_value, w_out, gain_mlp, w_up, w_down, pos_bias
):
    anywhere = pl.BlockSpec(memory_space=pl.ANY)
    whole = pl.BlockSpec(memory_space=pltpu.VMEM)
    struct = jax.ShapeDtypeStruct
    results = pl.pallas_call(
        plane_kernel,
        out_shape=(
            struct((2, TOK, D), BF),
            struct((2, TOK, D), BF),
            struct((CHIPS, PACK, LANES), BF),
            struct((CHIPS, 2 * PACK, LANES), BF),
            struct((ROWS, D), BF),
            struct((CHIPS, ROWS, FS), BF),
            struct((CHIPS, ROWS, D), BF),
            struct((TOK, BAND), BF),
        ),
        in_specs=[anywhere, pl.BlockSpec(memory_space=pltpu.SMEM), anywhere, whole, whole] + [anywhere] * 7,
        out_specs=(anywhere,) * 8,
        scratch_shapes=[pltpu.VMEM(shape, kind) for shape, kind in SCRATCH.values()]
        + [
            pltpu.SemaphoreType.DMA((N_REMOTE,)),
            pltpu.SemaphoreType.DMA((N_REMOTE,)),
            pltpu.SemaphoreType.DMA((N_LOCAL,)),
        ],
        compiler_params=pltpu.CompilerParams(
            collective_id=0, has_side_effects=True, vmem_limit_bytes=VMEM_BYTES
        ),
        cost_estimate=pl.CostEstimate(
            flops=15_000_000_000, bytes_accessed=8_000_000, transcendentals=4_000_000
        ),
        name="aft_layer",
    )(
        tokens.reshape(2, TOK, D), lengths.reshape(2), cotangent.reshape(2, TOK, D),
        gain_attn.reshape(1, ROWS), gain_mlp.reshape(1, ROWS),
        w_query, w_key, w_value, w_out, w_up, w_down, pos_bias,
    )
    out, gtok, gq, gv, gwout, gup, gdn, gpb = results
    f32_out = [struct(shape, kind) for shape, kind in FIN_OUT.values()]
    row = struct((1, ROWS), F32)
    out, gtok, grad_gain_a, grad_q, grad_k, grad_v, grad_o, grad_gain_m, grad_up, grad_down, grad_bias = (
        pl.pallas_call(
            finish_kernel,
            out_shape=(struct((2, TOK, D), BF),) * 2 + (row, *f32_out[:4], row, *f32_out[4:]),
            in_specs=[anywhere] * 8 + [whole] * 2 + [anywhere] * 5,
            out_specs=(anywhere, anywhere, whole) + (anywhere,) * 4 + (whole,) + (anywhere,) * 3,
            scratch_shapes=[pltpu.VMEM(shape, kind) for shape, kind in (*FIN_IN.values(), *FIN_OUT.values())]
            + [pltpu.SemaphoreType.DMA((len(FIN_IN),)), pltpu.SemaphoreType.DMA((len(FIN_OUT) + 1 + CHIPS,))],
            compiler_params=pltpu.CompilerParams(vmem_limit_bytes=VMEM_BYTES),
            cost_estimate=pl.CostEstimate(flops=4_000_000, bytes_accessed=9_000_000, transcendentals=100_000),
            name="gradients_out",
        )(
            out, gtok, gq, gv, gwout, gup, gdn.reshape(FF // (CHIPS * CORES), D), gpb,
            gain_attn.reshape(1, ROWS), gain_mlp.reshape(1, ROWS),
            w_query, w_key, w_value, w_up, pos_bias,
        )
    )
    return (
        out.reshape(tokens.shape),
        gtok.reshape(tokens.shape),
        grad_gain_a.reshape(ROWS),
        grad_q,
        grad_k,
        grad_v,
        grad_o,
        grad_gain_m.reshape(ROWS),
        grad_up,
        grad_down,
        grad_bias,
    )


def solution(mesh):
    in_specs = (
        P(None, "pipe", "dp", None),
        P(None, "pipe", None),
        P(None, "pipe", "dp", None),
        P("dp"),
        P("dp", None),
        P("dp", None),
        P("dp", None),
        P("dp", None),
        P("dp"),
        P("dp", None),
        P("dp", None),
        P("dp", None),
    )
    out_specs = (
        P(None, "pipe", "dp", None),
        P(None, "pipe", "dp", None),
        P("dp"),
        P("dp", None),
        P("dp", None),
        P("dp", None),
        P("dp", None),
        P("dp"),
        P("dp", None),
        P("dp", None),
        P("dp", None),
    )
    fits = mesh.shape["dp"] == CHIPS * CORES and mesh.shape["pipe"] == DEPTH
    return jax.shard_map(plane_program if fits else local, mesh=mesh, in_specs=in_specs, out_specs=out_specs, check_vma=False)
```

```python
import types

import jax
import jax.numpy as jnp
from jax import lax
from jax.experimental import pallas as pl
from jax.experimental.pallas import tpu as pltpu
from jax.sharding import PartitionSpec as P

D = 768
FF = 3072
SEQ = 1024
WIN = 256


EPSILON = 1e-05
GELU_SCALE = 0.7978845608028654
GELU_CUBE = 0.044715
VMEM_BYTES = 63 * 2**20


def normalize(values, gain):
    centre = values - jnp.mean(values, axis=-1, keepdims=True)
    spread = jnp.mean(centre * centre, axis=-1, keepdims=True)
    return centre * lax.rsqrt(spread + EPSILON) * gain


def gelu_tanh(values):
    return jax.nn.gelu(values, approximate=True)


def band_ones(width):
    row_ids = jnp.arange(width)[:, None]
    col_ids = jnp.arange(3 * width)[None, :]
    return (jnp.abs(col_ids - width - row_ids) < width).astype(jnp.float32)


def band_blocks(bias, width):
    length = bias.shape[0]
    padded = jnp.pad(bias, ((0, 0), (width, width)))
    return jnp.stack(
        [
            padded[block * width : (block + 1) * width, block * width : block * width + 3 * width]
            for block in range(length // width)
        ]
    )


def windows(operand, width):
    blocks = operand.shape[0] // width
    padded = jnp.pad(operand, ((width, width), (0, 0))).reshape(blocks + 2, width, operand.shape[1])
    return jnp.concatenate([padded[:-2], padded[1:-1], padded[2:]], axis=1)


def unwindow(grad_windows, width):
    blocks = grad_windows.shape[0]
    leading = jnp.pad(grad_windows[:, :width], ((0, 2), (0, 0), (0, 0)))
    middle = jnp.pad(grad_windows[:, width : 2 * width], ((1, 1), (0, 0), (0, 0)))
    trailing = jnp.pad(grad_windows[:, 2 * width :], ((2, 0), (0, 0), (0, 0)))
    summed = leading + middle + trailing
    return summed[1:-1].reshape(blocks * width, grad_windows.shape[2])


def to_columns(matrix, seq_count, length):
    channels = matrix.shape[1]
    return (
        matrix.reshape(seq_count, length, channels)
        .transpose(1, 0, 2)
        .reshape(length, seq_count * channels)
    )


def from_columns(matrix, seq_count, length):
    channels = matrix.shape[1] // seq_count
    return (
        matrix.reshape(length, seq_count, channels)
        .transpose(1, 0, 2)
        .reshape(seq_count * length, channels)
    )


def outer_sum(left, right):
    return lax.dot_general(
        left, right, (((0,), (0,)), ((), ())), preferred_element_type=jnp.float32
    )


def times_transpose(left, right):
    return lax.dot_general(
        left, right, (((1,), (1,)), ((), ())), preferred_element_type=jnp.float32
    )


def local(
    tokens,
    lengths,
    cotangent,
    gain_attn,
    w_query,
    w_key,
    w_value,
    w_out,
    gain_mlp,
    w_up,
    w_down,
    pos_bias,
):
    gathered = (
        lax.all_gather(gain_attn, "dp", axis=0, tiled=True),
        lax.all_gather(w_query, "dp", axis=0, tiled=True),
        lax.all_gather(w_key, "dp", axis=0, tiled=True),
        lax.all_gather(w_value, "dp", axis=0, tiled=True),
        lax.all_gather(w_out, "dp", axis=0, tiled=True),
        lax.all_gather(gain_mlp, "dp", axis=0, tiled=True),
        lax.all_gather(w_up, "dp", axis=0, tiled=True),
        lax.all_gather(w_down, "dp", axis=0, tiled=True),
        lax.all_gather(pos_bias, "dp", axis=0, tiled=True),
    )
    gain_a = gathered[0].astype(jnp.float32)
    query_w, key_w, value_w, out_w = (gathered[1], gathered[2], gathered[3], gathered[4])
    gain_m = gathered[5].astype(jnp.float32)
    up_w, down_w = (gathered[6], gathered[7])
    bias_full = gathered[8].astype(jnp.float32)
    group_size = lax.axis_size("dp")
    tok_rows = tokens.shape[2]
    seq_count = group_size * tok_rows // SEQ
    band_mask = band_ones(WIN)
    bias_blocks = jnp.exp(band_blocks(bias_full, WIN))
    exp_band = bias_blocks * band_mask
    kernel = ((bias_blocks - 1.0) * band_mask).astype(jnp.bfloat16)
    positions = jnp.arange(SEQ)
    grad_gain_a = jnp.zeros((D,), jnp.float32)
    grad_gain_m = jnp.zeros((D,), jnp.float32)
    grad_query_w = jnp.zeros((D, D), jnp.float32)
    grad_key_w = jnp.zeros((D, D), jnp.float32)
    grad_value_w = jnp.zeros((D, D), jnp.float32)
    grad_out_w = jnp.zeros((D, D), jnp.float32)
    grad_up_w = jnp.zeros((D, FF), jnp.float32)
    grad_down_w = jnp.zeros((FF, D), jnp.float32)
    grad_kernel = jnp.zeros(exp_band.shape, jnp.float32)
    outputs_list = []
    grads_in_list = []
    for micro in range(tokens.shape[0]):
        inputs_f = tokens[micro, 0].astype(jnp.float32)
        normed_f, norm_back_a = jax.vjp(normalize, inputs_f, gain_a)
        normed = normed_f.astype(jnp.bfloat16)
        query = jnp.dot(normed, query_w, preferred_element_type=jnp.float32)
        keys = jnp.dot(normed, key_w, preferred_element_type=jnp.float32).astype(jnp.bfloat16)
        values = jnp.dot(normed, value_w, preferred_element_type=jnp.float32).astype(jnp.bfloat16)
        key_chan, value_chan = (
            lax.all_to_all(keys, "dp", split_axis=1, concat_axis=0, tiled=True),
            lax.all_to_all(values, "dp", split_axis=1, concat_axis=0, tiled=True),
        )
        seq_lengths = lengths[micro, 0]
        channels = key_chan.shape[1]
        valid_seq = (positions[:, None] < seq_lengths[None, :]).astype(jnp.float32)
        valid_cols = jnp.broadcast_to(valid_seq[:, :, None], (SEQ, seq_count, channels)).reshape(
            SEQ, seq_count * channels
        )
        key_cols = to_columns(key_chan, seq_count, SEQ).astype(jnp.float32)
        value_cols = to_columns(value_chan, seq_count, SEQ).astype(jnp.float32)
        weighted = jnp.exp(key_cols) * valid_cols
        col_count = weighted.shape[1]
        operand = jnp.concatenate(
            [(weighted * value_cols).astype(jnp.bfloat16), weighted.astype(jnp.bfloat16)], axis=1
        )
        windowed = windows(operand, WIN)
        banded = jnp.einsum(
            "nqk,nkc->nqc", kernel, windowed, preferred_element_type=jnp.float32
        ).reshape(SEQ, 2 * col_count)
        result = banded + jnp.sum(operand, axis=0, dtype=jnp.float32)[None, :]
        numerator = result[:, :col_count]
        denominator = result[:, col_count:] + 1.0 - valid_cols
        mixed_cols = numerator / denominator * valid_cols
        mixed_tok = lax.all_to_all(
            from_columns(mixed_cols.astype(jnp.bfloat16), seq_count, SEQ),
            "dp",
            split_axis=0,
            concat_axis=1,
            tiled=True,
        )
        sigmoid_q = jax.nn.sigmoid(query)
        mixed_f = mixed_tok.astype(jnp.float32)
        gated = (sigmoid_q * mixed_f).astype(jnp.bfloat16)
        resid = inputs_f + jnp.dot(gated, out_w, preferred_element_type=jnp.float32)
        normed_two_f, norm_back_m = jax.vjp(normalize, resid, gain_m)
        normed_two = normed_two_f.astype(jnp.bfloat16)
        upper = jnp.dot(normed_two, up_w, preferred_element_type=jnp.float32)
        hidden_f, gelu_back = jax.vjp(gelu_tanh, upper)
        hidden = hidden_f.astype(jnp.bfloat16)
        outputs_list.append(
            (resid + jnp.dot(hidden, down_w, preferred_element_type=jnp.float32)).astype(
                jnp.bfloat16
            )
        )
        grad_out = cotangent[micro, 0]
        grad_down_w = grad_down_w + outer_sum(hidden, grad_out)
        grad_hidden = times_transpose(grad_out, down_w)
        grad_upper = gelu_back(grad_hidden)[0].astype(jnp.bfloat16)
        grad_up_w = grad_up_w + outer_sum(normed_two, grad_upper)
        grad_normed_two = times_transpose(grad_upper, up_w)
        grad_resid_norm, grad_gain_part_m = norm_back_m(grad_normed_two)
        grad_gain_m = grad_gain_m + grad_gain_part_m
        grad_resid = grad_out.astype(jnp.float32) + grad_resid_norm
        grad_attn = grad_resid.astype(jnp.bfloat16)
        grad_out_w = grad_out_w + outer_sum(gated, grad_attn)
        grad_gated = times_transpose(grad_attn, out_w)
        grad_mixed = (grad_gated * sigmoid_q).astype(jnp.bfloat16)
        grad_query = (grad_gated * mixed_f * sigmoid_q * (1.0 - sigmoid_q)).astype(jnp.bfloat16)
        grad_mixed_chan = lax.all_to_all(grad_mixed, "dp", split_axis=1, concat_axis=0, tiled=True)
        grad_mixed_cols = to_columns(grad_mixed_chan, seq_count, SEQ).astype(jnp.float32)
        grad_numerator = grad_mixed_cols * valid_cols / denominator
        grad_denominator = -grad_numerator * (numerator / denominator)
        grad_flat = jnp.concatenate(
            [grad_numerator.astype(jnp.bfloat16), grad_denominator.astype(jnp.bfloat16)], axis=1
        )
        grad_result = grad_flat.reshape(SEQ // WIN, WIN, 2 * col_count)
        grad_windowed = jnp.einsum(
            "nqk,nqc->nkc", kernel, grad_result, preferred_element_type=jnp.float32
        )
        grad_kernel = grad_kernel + jnp.einsum(
            "nqc,nkc->nqk", grad_result, windowed, preferred_element_type=jnp.float32
        )
        grad_operand = (
            unwindow(grad_windowed, WIN) + jnp.sum(grad_flat, axis=0, dtype=jnp.float32)[None, :]
        )
        grad_key_value = grad_operand[:, :col_count]
        grad_key_weight = grad_operand[:, col_count:]
        grad_keys_cols = (grad_key_value * value_cols + grad_key_weight) * weighted
        grad_values_cols = grad_key_value * weighted
        grad_keys, grad_values = (
            lax.all_to_all(
                from_columns(grad_keys_cols.astype(jnp.bfloat16), seq_count, SEQ),
                "dp",
                split_axis=0,
                concat_axis=1,
                tiled=True,
            ),
            lax.all_to_all(
                from_columns(grad_values_cols.astype(jnp.bfloat16), seq_count, SEQ),
                "dp",
                split_axis=0,
                concat_axis=1,
                tiled=True,
            ),
        )
        grad_query_w = grad_query_w + outer_sum(normed, grad_query)
        grad_key_w = grad_key_w + outer_sum(normed, grad_keys)
        grad_value_w = grad_value_w + outer_sum(normed, grad_values)
        grad_normed = (
            times_transpose(grad_query, query_w)
            + times_transpose(grad_keys, key_w)
            + times_transpose(grad_values, value_w)
        )
        grad_input_norm, grad_gain_part_a = norm_back_a(grad_normed)
        grad_gain_a = grad_gain_a + grad_gain_part_a
        grads_in_list.append((grad_resid + grad_input_norm).astype(jnp.bfloat16))
    grad_kernel_bias = grad_kernel * exp_band
    grad_bias_pad = jnp.zeros((SEQ, SEQ + 2 * WIN), jnp.float32)
    for block in range(SEQ // WIN):
        grad_bias_pad = grad_bias_pad.at[
            block * WIN : (block + 1) * WIN, block * WIN : block * WIN + 3 * WIN
        ].add(grad_kernel_bias[block])
    grad_bias = grad_bias_pad[:, WIN : WIN + SEQ]
    shares = (
        lax.psum_scatter(grad_gain_a, "dp", scatter_dimension=0, tiled=True),
        lax.psum_scatter(grad_query_w, "dp", scatter_dimension=0, tiled=True),
        lax.psum_scatter(grad_key_w, "dp", scatter_dimension=0, tiled=True),
        lax.psum_scatter(grad_value_w, "dp", scatter_dimension=0, tiled=True),
        lax.psum_scatter(grad_out_w, "dp", scatter_dimension=0, tiled=True),
        lax.psum_scatter(grad_gain_m, "dp", scatter_dimension=0, tiled=True),
        lax.psum_scatter(grad_up_w, "dp", scatter_dimension=0, tiled=True),
        lax.psum_scatter(grad_down_w, "dp", scatter_dimension=0, tiled=True),
        lax.psum_scatter(grad_bias, "dp", scatter_dimension=0, tiled=True),
    )
    reduced = lax.psum(
        (
            shares[0],
            shares[1],
            shares[2],
            shares[3],
            shares[4],
            shares[5],
            shares[6],
            shares[7],
            shares[8],
        ),
        "pipe",
    )
    final_grads = (
        reduced[0],
        reduced[1],
        reduced[2],
        reduced[3],
        reduced[4],
        reduced[5],
        reduced[6],
        reduced[7],
        reduced[8],
    )
    output = jnp.stack(outputs_list)[:, None]
    grad_tokens = jnp.stack(grads_in_list)[:, None]
    return (
        output,
        grad_tokens,
        final_grads[0],
        final_grads[1],
        final_grads[2],
        final_grads[3],
        final_grads[4],
        final_grads[5],
        final_grads[6],
        final_grads[7],
        final_grads[8],
    )


CHIPS = 4
CORES = 2
DEPTH = 4
LANES = 128
TOK = 128
BLK = CORES * TOK
ROWS = D // (CHIPS * CORES)
SL = D // CHIPS
SLP = -(-SL // LANES) * LANES
FS = FF // CHIPS
BAND = 5 * LANES
HALF = D // 2
PACK = ROWS + ROWS // 2
MESH_ID = pl.DeviceIdType.MESH
F32 = jnp.float32
BF = jnp.bfloat16

SCRATCH = dict(
    tok=((BLK, D), BF),
    cot=((SEQ, D), BF),
    gains=((CHIPS * CORES, 16, LANES), BF),
    gain=((16, D), F32),
    wst=((3, ROWS, D), BF),
    wqs=((CHIPS, ROWS, 3 * SLP), BF),
    wqkv=((D, 3 * SLP), BF),
    wout=((CHIPS * SLP, D), BF),
    wup=((D, FS), BF),
    wdn=((FS, D), BF),
    pbw=((TOK, BAND), BF),
    kern=((CHIPS * CORES, TOK, BAND), BF),
    h1=((SEQ, D), BF),
    h2=((SEQ, D), BF),
    n1=((BLK, D), F32),
    r1=((BLK, LANES), F32),
    n2=((BLK, D), F32),
    r2=((BLK, LANES), F32),
    tmp=((HALF, D), F32),
    tmix=((TOK, 2 * SLP), F32),
    sums=((8, 2 * SLP), F32),
    sig=((SEQ, SLP), F32),
    wgt=((SEQ, SLP), F32),
    val=((SEQ, SLP), BF),
    op=((SEQ, 2 * SLP), BF),
    ratio=((SEQ, SLP), F32),
    rden=((SEQ, SLP), F32),
    mixed=((SEQ, SLP), BF),
    gated=((SEQ, SLP), BF),
    grecv=((CHIPS, BLK, SLP), BF),
    ghs=((CHIPS, TOK, LANES), BF),
    ghr=((CHIPS - 1, TOK, LANES), BF),
    gghs=((CHIPS - 1, TOK, LANES), BF),
    gghr=((CHIPS - 1, TOK, LANES), BF),
    resid=((BLK, D), F32),
    hid=((SEQ, FS), BF),
    dge=((3 * BLK, FS), F32),
    gop=((SEQ, 2 * SLP), F32),
    gupr=((SEQ, FS), BF),
    pout=((CHIPS - 1, BLK, D), BF),
    pgh=((CHIPS - 1, BLK, D), BF),
    own=((BLK, D), F32),
    rbout=((6, TOK, D), BF),
    rbg2=((6, TOK, D), BF),
    rbg1=((6, TOK, D), BF),
    gresid=((BLK, D), F32),
    gattn=((BLK, D), BF),
    ggs=((CHIPS - 1, BLK, LANES), BF),
    ggr=((CHIPS, BLK, SLP), BF),
    gdo=((HALF, D), F32),
    gdx=((HALF, D), F32),
    gds=((CHIPS, ROWS, D), BF),
    gdr=((CHIPS, ROWS, D), BF),
    guo=((D, FS), F32),
    gus=((CHIPS, ROWS, FS), BF),
    gur=((CHIPS, ROWS, FS), BF),
    gqo=((CHIPS, ROWS, SLP), F32),
    gqs=((CHIPS, ROWS, SLP), BF),
    gqr=((CHIPS, ROWS, SLP), BF),
    gvo=((CHIPS, ROWS, 2 * SLP), F32),
    gvs=((CHIPS, ROWS, 2 * SLP), BF),
    gvr=((CHIPS, ROWS, 2 * SLP), BF),
    goo=((CHIPS, ROWS, D), F32),
    gos=((CHIPS, ROWS, D), BF),
    gor=((CHIPS, ROWS, D), BF),
    po=((CHIPS - 1, ROWS, D), BF),
    rbo=((6, ROWS // 2, D), BF),
    gko=((CHIPS, TOK, BAND), F32),
    gks=((CHIPS, TOK, BAND), BF),
    gkr=((CHIPS, TOK, BAND), BF),
    pk=((CHIPS - 1, TOK, BAND), BF),
    rbk=((6, TOK // 2, BAND), BF),
    zdb=((CHIPS, ROWS, D), BF),
    zdr=((CHIPS, ROWS, D), BF),
    zdt=((CHIPS, ROWS, D), BF),
    zub=((CHIPS, ROWS, FS), BF),
    zur=((CHIPS, ROWS, FS), BF),
    zut=((CHIPS, ROWS, FS), BF),
    zqb=((CHIPS, PACK, LANES), BF),
    zqr=((CHIPS, PACK, LANES), BF),
    zqt=((CHIPS, PACK, LANES), BF),
    zvb=((CHIPS, 2 * PACK, LANES), BF),
    zvr=((CHIPS, 2 * PACK, LANES), BF),
    zvt=((CHIPS, 2 * PACK, LANES), BF),
    zob=((ROWS, D), BF),
    zor=((ROWS, D), BF),
    zot=((ROWS, D), BF),
    zkb=((TOK, BAND), BF),
    zkr=((TOK, BAND), BF),
    zkt=((TOK, BAND), BF),
    fout=((BLK, D), BF),
    fgt=((BLK, D), BF),
)
POLLS = {
    1: ("d3",),
    2: ("d1",),
    4: ("d2", "D3",),
    6: ("d0", "D1",),
    9: ("D2",),
    11: ("u3",),
    13: ("D0",),
    15: ("u1",),
    16: ("u2",),
    23: ("u0", "U3",),
    25: ("U1",),
    27: ("U2", "U0",),
    28: ("q3", "q1", "q2", "q0", "o0", "o1", "+U3", "+U1",),
    29: ("Q3", "v3", "Q1", "v1", "Q2", "v2", "Q0", "v0", "O0", "O1", "V3", "V1", "V2", "V0", "k0", "k1", "+U2", "+U0",),
    30: ("+Q3", "+Q1", "+Q2", "+Q0",),
    31: ("K0", "K1", "+V3", "+V1", "+V2", "+V0", "+O0", "+O1", "+D3", "+D1", "+D2", "+D0", "+K0", "+K1",),
}
N_REMOTE = 200
N_LOCAL = 40


def dot(left, right, left_dim, right_dim):
    return lax.dot_general(
        left, right, (((left_dim,), (right_dim,)), ((), ())), preferred_element_type=F32
    )


def rows_loop(count, step, body, unroll=1):
    def one(i, carry):
        body(pl.multiple_of(i * step, step))
        return carry

    lax.fori_loop(0, count // step, one, 0, unroll=unroll)


def plane_kernel(
    tok_in, len_in, cot_in, ga_in, gm_in, wq_in, wk_in, wv_in, wout_in, wup_in, wdn_in, pb_in,
    out_out, gtok_out, gq_out, gv_out, gwout_out, gup_out, gdn_out, gpb_out,
    *scratch,
):
    m = types.SimpleNamespace(**dict(zip(SCRATCH, scratch)))
    send_sem, recv_sem, local_sem = scratch[len(SCRATCH):]
    r = lax.axis_index("dp")
    z = lax.axis_index("pipe")
    c = lax.rem(r, 2)
    x = lax.rem(r // 2, 2)
    y = r // 4
    b = r // 2
    length = len_in[c]

    def chip(k):
        return 2 * (1 - y if k // 2 else y) + (1 - x if k % 2 else x)

    def peer(k, other=0):
        return (2 * chip(k) + (1 - c if other else c), z)

    jx, jy, jd = chip(1), chip(2), chip(3)
    SIB, PX, PY, PD = peer(0, 1), peer(1), peer(2), peer(3)
    z_near = z + 1 - 2 * lax.rem(z, 2)
    z_far = 3 - z
    ZN, ZF = (r, z_near), (r, z_far)
    outer = z * (3 - z) == 0
    inner = z * (3 - z) != 0

    remote, locals_ = {}, []
    waited = set()
    begun = []

    def make(name, src, dst, to):
        assert name not in remote, name
        i = len(remote)
        cp = pltpu.make_async_remote_copy(
            src_ref=src, dst_ref=dst, send_sem=send_sem.at[i], recv_sem=recv_sem.at[i],
            device_id=to, device_id_type=MESH_ID,
        )
        remote[name] = cp
        return cp

    def send(name, src, dst, to):
        make(name, src, dst, to)
        start(name)

    def start(*names):
        for name in names:
            begun.append(name)
            remote[name].start()

    def got(*names):
        for name in names:
            if name not in waited:
                waited.add(name)
                remote[name].wait_recv()

    def sent(*names):
        for name in names:
            if name + "/s" not in waited:
                waited.add(name + "/s")
                remote[name].wait_send()

    def local_copy(src, dst):
        cp = pltpu.make_async_copy(src, dst, local_sem.at[len(locals_)])
        locals_.append(cp)
        cp.start()
        return cp

    def ds(start, size, unit):
        return pl.ds(pl.multiple_of(start, unit), size)

    def band_at(d):
        return pl.multiple_of(jnp.minimum(jnp.maximum(d - 2, 0), 3) * LANES, LANES)

    def gather_open(name, blk):
        make(name + "X0", blk(b, 0), blk(b, 0), PX)
        make(name + "Y1", blk(b, 1), blk(b, 1), PY)
        make(name + "X1", blk(b, 1), blk(b, 1), PX)
        make(name + "Y0", blk(b, 0), blk(b, 0), PY)
        make(name + "F0", blk(jx, 0), blk(jx, 0), PY)
        make(name + "F1", blk(jy, 1), blk(jy, 1), PX)

    def gather_start(name):
        start(name + "X0", name + "Y1", name + "X1", name + "Y0")

    def gather_forward(name):
        got(name + "X0")
        start(name + "F0")
        got(name + "Y1")
        start(name + "F1")

    def gather_wait(name, k):
        got(*{1: (name + "X0", name + "X1"), 2: (name + "Y0", name + "Y1"), 3: (name + "F0", name + "F1")}[k])

    fetch = lax.rem(z, 2) == c
    passed = lax.rem(z, 2) != c
    in_fetch = []

    def relay_open(name, place):
        for k in (1, 2, 3):
            make(f"{name}Z{k}", place(k), place(k), ZN)
            in_fetch.append(f"{name}Z{k}")

    def relay(name, place, arrive):
        for k in (1, 2, 3):

            @pl.when(fetch)
            def _(k=k):
                arrive(k)
                start(f"{name}Z{k}")

            @pl.when(passed)
            def _(k=k):
                remote[f"{name}Z{k}"].wait_recv()

            waited.add(f"{name}Z{k}")
            send(f"{name}S{k}", place(k), place(k), SIB)

    def scatter_diagonal(name, part, buf, half):
        send(name + "0", part.at[2, pl.ds(half, half)], buf.at[0], PX)
        send(name + "1", part.at[2, pl.ds(0, half)], buf.at[1], PY)

    def scatter_direct_x(name, part, buf, half):
        send(name + "2", part.at[0, pl.ds(half, half)], buf.at[2], PX)

    def scatter_direct_y(name, part, buf, half):
        send(name + "3", part.at[1, pl.ds(0, half)], buf.at[3], PY)

    def scatter_combine(name, part, buf, half):
        got(name + "1")
        part[0, pl.ds(0, half), :] = (
            part[0, pl.ds(0, half), :].astype(F32) + buf[1].astype(F32)
        ).astype(BF)
        send(name + "4", part.at[0, pl.ds(0, half)], buf.at[4], PX)
        got(name + "0")
        part[1, pl.ds(half, half), :] = (
            part[1, pl.ds(half, half), :].astype(F32) + buf[0].astype(F32)
        ).astype(BF)
        send(name + "5", part.at[1, pl.ds(half, half)], buf.at[5], PY)

    def scatter_wait(name):
        got(name + "2", name + "3", name + "4", name + "5")

    def scatter_sum(buf, half, h, rows):
        if h == 0:
            return buf[3, rows, :].astype(F32) + buf[4, rows, :].astype(F32)
        return buf[2, rows, :].astype(F32) + buf[5, rows, :].astype(F32)

    zitems = {}

    def half_rows(which, h):
        size = (ROWS if which == "O" else TOK) // 2
        return pl.ds(h * size, size)


    def z_open(name, base, near, total):
        zitems[name] = (
            base,
            near,
            total,
            make(name + "a", base, near, ZN),
            make(name + "b", base, total, ZF),
            make(name + "c", total, total, ZN),
        )

    def z_start(name):
        item = zitems[name]

        @pl.when(outer)
        def _():
            item[3].start()

    def z_mid(name):
        base, near, total, into, across, back = zitems[name]

        @pl.when(inner)
        def _():
            into.wait_recv()
            base[...] = (base[...].astype(F32) + near[...].astype(F32)).astype(BF)
            across.start()

    def z_end(name):
        base, near, total, into, across, back = zitems[name]

        @pl.when(inner)
        def _():
            across.wait_recv()
            total[...] = (base[...].astype(F32) + total[...].astype(F32)).astype(BF)
            back.start()

    def z_take(name):
        back = zitems[name][5]

        @pl.when(outer)
        def _():
            back.wait_recv()

    def z_close(name):
        base, near, total, into, across, back = zitems[name]

        @pl.when(outer)
        def _():
            into.wait_send()

        @pl.when(inner)
        def _():
            across.wait_send()
            back.wait_send()

    for k in range(CHIPS):
        j = chip(k)
        z_open(f"zd{k}", m.zdb.at[j], m.zdr.at[j], m.zdt.at[j])
        z_open(f"zu{k}", m.zub.at[j], m.zur.at[j], m.zut.at[j])
        z_open(f"zq{k}", m.zqb.at[j], m.zqr.at[j], m.zqt.at[j])
        z_open(f"zv{k}", m.zvb.at[j], m.zvr.at[j], m.zvt.at[j])
    for h in range(2):
        half = half_rows("O", h)
        z_open(f"zo{h}", m.zob.at[half], m.zor.at[half], m.zot.at[half])
        half = half_rows("K", h)
        z_open(f"zk{h}", m.zkb.at[half], m.zkr.at[half], m.zkt.at[half])
    ORDER = (3, 1, 2, 0)

    onward = {}

    def prepare(which, k):
        j = chip(k)
        whole = dict(D=m.zdt, U=m.zut, Q=m.zqt, V=m.zvt, O=m.zot, K=m.zkt)[which]
        out = dict(D=gdn_out, U=gup_out, Q=gq_out, V=gv_out, O=gwout_out, K=gpb_out)[which]
        if which in "UQV" and k:
            name = f"f{which}{k}"
            begun.append(name)
            return make(name, whole.at[j], out.at[b], peer(k))
        part = half_rows(which, k) if which in "OK" else j
        src, dst = whole.at[part], out.at[part]
        locals_.append(pltpu.make_async_copy(src, dst, local_sem.at[len(locals_)]))
        return locals_[-1]

    def poll(place):
        for step in POLLS.get(place, ()):
            code = step.strip("+")
            name = "z" + code.lower()
            if code.islower():
                z_mid(name)
                continue
            if name not in onward:
                onward[name] = prepare(code[0], int(code[1]))
            if step == code:
                z_end(name)
                pl.when(inner)(onward[name].start)
            else:
                z_take(name)
                pl.when(outer)(onward[name].start)

    own_half = ds(c * TOK, TOK, TOK)
    other_half = ds((1 - c) * TOK, TOK, TOK)
    l_tok = local_copy(tok_in.at[c], m.tok.at[own_half])
    l_w = [local_copy(w, m.wst.at[i]) for i, w in enumerate((wq_in, wk_in, wv_in))]
    l_pb = local_copy(pb_in.at[:, ds(band_at(r), BAND, LANES)], m.pbw)

    def wout_rows(j, core):
        return m.wout.at[ds(j * SLP + core * ROWS, ROWS, 32)]

    l_wout = local_copy(wout_in, wout_rows(b, c))
    up_rows = ds(r * ROWS, ROWS, 32)
    l_wup = local_copy(wup_in.at[:, ds(b * FS, FS, LANES)], m.wup.at[up_rows])
    dn_rows = ds(c * HALF, HALF, LANES)
    l_wdn = local_copy(wdn_in, m.wdn.at[dn_rows])
    cot_half = ds(b * BLK + c * TOK, TOK, TOK)
    l_cot = local_copy(cot_in.at[c], m.cot.at[cot_half])

    line = lax.broadcasted_iota(jnp.int32, (16, LANES), 0)
    fill = jnp.zeros((1, LANES - ROWS), F32)
    both_gains = [
        jnp.broadcast_to(jnp.concatenate([g[...].astype(F32), fill], axis=1), (16, LANES)) for g in (ga_in, gm_in)
    ]
    m.gains[r] = jnp.where(line == 0, both_gains[0], both_gains[1]).astype(BF)

    barrier = pltpu.get_barrier_semaphore()
    everyone = [peer(k, o) for k in range(CHIPS) for o in range(CORES) if (k, o) != (0, 0)] + [ZN, ZF]
    for other in everyone:
        pl.semaphore_signal(barrier, inc=1, device_id=other, device_id_type=MESH_ID)
    l_pb.wait()
    t_ids = r * TOK + lax.broadcasted_iota(jnp.int32, (TOK, BAND), 0)
    u_ids = band_at(r) + lax.broadcasted_iota(jnp.int32, (TOK, BAND), 1)
    in_band = jnp.abs(t_ids - u_ids) < WIN
    m.kern[r] = jnp.where(in_band, jnp.exp(m.pbw[...].astype(F32)) - 1.0, 0.0).astype(BF)

    for cp in l_w:
        cp.wait()
    for i in range(3):
        w_rows = m.wst[i].astype(F32)
        for j in range(CHIPS):
            piece = w_rows[:, j * SL : (j + 1) * SL]
            m.wqs[j, :, i * SLP : (i + 1) * SLP] = jnp.concatenate(
                [piece, jnp.zeros((ROWS, SLP - SL), F32)], axis=1
            ).astype(BF)
    pl.semaphore_wait(barrier, len(everyone))

    send("tokS", tok_in.at[1 - c], m.tok.at[own_half], SIB)
    gain_names = []
    for k in range(CHIPS):
        for o in range(CORES):
            if (k, o) != (0, 0):
                gain_names.append(f"gain{k}{o}")
                send(gain_names[-1], m.gains.at[r], m.gains.at[r], peer(k, o))

    def wout_blk(j, h):
        return m.wout.at[ds(j * SLP + c * ROWS + h * (ROWS // 2), ROWS // 2, 16)]

    gather_open("wo", wout_blk)
    in_fetch.extend("wo" + part for part in ("X0", "X1", "Y0", "Y1", "F0", "F1"))
    l_wout.wait()

    @pl.when(fetch)
    def _():
        gather_start("wo")

    for k, to in ((1, PX), (2, PY), (3, PD)):
        make(f"wq{k}", m.wqs.at[chip(k)], m.wqkv.at[up_rows], to)
        in_fetch.append(f"wq{k}")

    @pl.when(fetch)
    def _():
        start("wq1", "wq2", "wq3")

    def kern_blk(j, h):
        return m.kern.at[2 * j + c, pl.ds(h * (TOK // 2), TOK // 2)]

    gather_open("kn", kern_blk)
    in_fetch.extend("kn" + part for part in ("X0", "X1", "Y0", "Y1", "F0", "F1"))

    @pl.when(fetch)
    def _():
        gather_start("kn")

    send("knS0", m.kern.at[r], m.kern.at[r], SIB)

    send("wqS0", m.wqs.at[b], m.wqkv.at[up_rows], SIB)
    m.wqkv[up_rows, :] = m.wqs[b]

    def norm(src, n_ref, r_ref):
        def body(i):
            rows = pl.ds(i, 32)
            values = src[rows, :].astype(F32)
            centre = values - jnp.mean(values, axis=-1, keepdims=True)
            spread = jnp.mean(centre * centre, axis=-1, keepdims=True)
            rinv = lax.rsqrt(spread + EPSILON)
            n_ref[rows, :] = centre * rinv
            r_ref[rows, :] = jnp.broadcast_to(rinv, (32, LANES))

        rows_loop(BLK, 32, body, unroll=2)

    def scale(n_ref, gain_row, dst, base):
        def body(i):
            dst[pl.ds(pl.multiple_of(base + i, 32), 32), :] = (
                n_ref[pl.ds(i, 32), :] * m.gain[gain_row : gain_row + 1, :]
            ).astype(BF)

        rows_loop(BLK, 32, body, unroll=2)

    l_tok.wait()
    got("tokS")
    norm(m.tok, m.n1, m.r1)
    got(*gain_names)
    m.gain[...] = jnp.concatenate(
        [m.gains[d].astype(F32)[:, :ROWS] for d in range(CHIPS * CORES)], axis=1
    )
    scale(m.n1, 0, m.h1, b * BLK)

    def h1_blk(j, h):
        return m.h1.at[ds(j * BLK + h * TOK, TOK, TOK)]

    gather_open("h1", h1_blk)
    gather_start("h1")

    def w_place(ref):
        return lambda k: ref.at[ds((2 * chip(k) + c) * ROWS, ROWS, 32)]

    wq_place = w_place(m.wqkv)
    relay_open("wq", wq_place)
    relay("wq", wq_place, lambda k: got(f"wq{k}"))

    @pl.when(fetch)
    def _():
        gather_forward("kn")

    gather_forward("h1")
    for j in range(CHIPS):
        m.wout[j * SLP + SL : (j + 1) * SLP, :] = jnp.zeros((SLP - SL, D), BF)

    for k, to in ((1, PX), (2, PY), (3, PD)):
        make(f"wu{k}", wup_in.at[:, ds(chip(k) * FS, FS, LANES)], m.wup.at[up_rows], to)
        in_fetch.append(f"wu{k}")

    @pl.when(fetch)
    def _():
        gather_forward("wo")
        start("wu1", "wu2", "wu3")

    send("woS0", wout_rows(b, c), wout_rows(b, c), SIB)
    l_wup.wait()
    send("wuS0", m.wup.at[up_rows], m.wup.at[up_rows], SIB)
    l_wdn.wait()
    send("wdS", m.wdn.at[dn_rows], m.wdn.at[dn_rows], SIB)
    send("cotS", cot_in.at[1 - c], m.cot.at[cot_half], SIB)
    got("wqS0", "wqS1", "wqS2", "wqS3")

    def blk_rows(j):
        return ds(j * BLK, BLK, BLK)

    def project(j):
        m.tmp[0:BLK, :] = dot(m.h1[blk_rows(j), :], m.wqkv[...], 1, 0)

        def body(i):
            rows = pl.ds(i, 16)
            at = pl.multiple_of(j * BLK + i, 16)
            to = pl.ds(at, 16)
            q = m.tmp[rows, 0:SLP]
            m.sig[to, :] = 1.0 / (1.0 + jnp.exp(-q))
            keys = m.tmp[rows, SLP : 2 * SLP].astype(BF).astype(F32)
            values = m.tmp[rows, 2 * SLP : 3 * SLP].astype(BF)
            pos = at + lax.broadcasted_iota(jnp.int32, (16, SLP), 0)
            weighted = jnp.where(pos < length, jnp.exp(keys), 0.0)
            m.wgt[to, :] = weighted
            m.val[to, :] = values
            m.op[to, 0:SLP] = (weighted * values.astype(F32)).astype(BF)
            m.op[to, SLP : 2 * SLP] = weighted.astype(BF)

        rows_loop(BLK, 16, body, unroll=2)

    project(b)
    kn_place = lambda k: m.kern.at[2 * chip(k) + c]
    relay_open("kn", kn_place)
    relay("kn", kn_place, lambda k: gather_wait("kn", k))
    for k in (1, 2):
        gather_wait("h1", k)
        project(chip(k))
    gather_wait("h1", 3)
    project(jd)
    l_cot.wait()
    got("cotS")

    def cot_blk(j, h):
        return m.cot.at[ds(j * BLK + h * TOK, TOK, TOK)]

    gather_open("ct", cot_blk)
    start("ctX0", "ctY1")

    got("knS0", "knS1", "knS2", "knS3")
    ones = jnp.ones((8, SEQ), BF)
    m.sums[...] = dot(ones, m.op[...], 1, 0)

    def mix(j, half):
        d = 2 * j + half
        m.tmix[...] = dot(m.kern[d], m.op[pl.ds(band_at(d), BAND), :], 1, 0)

        def body(i):
            rows = pl.ds(i, 32)
            at = pl.multiple_of(d * TOK + i, 32)
            to = pl.ds(at, 32)
            pos = at + lax.broadcasted_iota(jnp.int32, (32, SLP), 0)
            valid = jnp.where(pos < length, 1.0, 0.0)
            num = m.tmix[rows, 0:SLP] + m.sums[0:1, 0:SLP]
            den = m.tmix[rows, SLP : 2 * SLP] + m.sums[0:1, SLP : 2 * SLP] + 1.0 - valid
            rden = 1.0 / den
            ratio = num * rden
            mixed = (ratio * valid).astype(BF)
            m.ratio[to, :] = ratio
            m.rden[to, :] = rden * valid
            m.mixed[to, :] = mixed
            gated = m.sig[to, :] * mixed.astype(F32)
            m.gated[to, :] = gated.astype(BF)
            high = gated[:, LANES:]
            m.ghs[j, rows, :] = jnp.where(
                half == 0, high, m.ghs[j, rows, :].astype(F32) + pltpu.roll(high, SL - LANES, 1)
            ).astype(BF)

        rows_loop(TOK, 32, body, unroll=2)

    def mix_block(j):
        def one(i, carry):
            mix(j, i)
            return carry

        lax.fori_loop(0, CORES, one, 0)

    low_lanes = pl.ds(0, LANES)

    def unpack(dst, high):
        lane = lax.broadcasted_iota(jnp.int32, (TOK, LANES), 1)
        both = high[...].astype(F32)
        for h in range(2):
            part = both if h == 0 else pltpu.roll(both, LANES - (SL - LANES), 1)
            dst[h * TOK : (h + 1) * TOK, LANES:] = jnp.where(lane < SL - LANES, part, 0.0).astype(BF)

    for k, to in ((3, PD), (1, PX), (2, PY)):
        j = chip(k)
        mix_block(j)
        send(f"ga{k}", m.gated.at[blk_rows(j), low_lanes], m.grecv.at[k, :, low_lanes], to)
        send(f"gh{k}", m.ghs.at[j], m.ghr.at[k - 1], to)
    mix_block(b)
    m.grecv[0] = m.gated[blk_rows(b), :]

    gather_forward("ct")
    wo_place = lambda k: wout_rows(chip(k), c)
    relay_open("wo", wo_place)
    relay("wo", wo_place, lambda k: gather_wait("wo", k))
    wu_place = w_place(m.wup)
    relay_open("wu", wu_place)
    relay("wu", wu_place, lambda k: got(f"wu{k}"))

    got("woS0", "woS1", "woS2", "woS3")
    m.resid[...] = m.tok[...].astype(F32)
    for k in (0, 1, 2, 3):
        if k:
            got(f"ga{k}", f"gh{k}")
            unpack(m.grecv.at[k], m.ghr.at[k - 1])
        m.resid[...] += dot(m.grecv[k], m.wout[ds(chip(k) * SLP, SLP, SLP), :], 1, 0)
    norm(m.resid, m.n2, m.r2)
    scale(m.n2, 1, m.h2, b * BLK)

    def h2_blk(j, h):
        return m.h2.at[ds(j * BLK + h * TOK, TOK, TOK)]

    gather_open("h2", h2_blk)
    gather_start("h2")

    got("wuS0", "wuS1", "wuS2", "wuS3", "wdS")

    def ff_forward(k):
        j = chip(k)
        keep = (k % 3) * BLK
        m.tmp[0:BLK, :] = dot(m.h2[blk_rows(j), :], m.wup[...], 1, 0)

        def gelu(i):
            v = m.tmp[pl.ds(i, 16), :]
            square = v * v
            t = jnp.tanh(GELU_SCALE * v * (1.0 + GELU_CUBE * square))
            half = 0.5 * (1.0 + t)
            m.hid[pl.ds(pl.multiple_of(j * BLK + i, 16), 16), :] = (v * half).astype(BF)
            m.dge[pl.ds(pl.multiple_of(keep + i, 16), 16), :] = half + 0.5 * v * (1.0 - t * t) * (
                GELU_SCALE * (1.0 + 3.0 * GELU_CUBE * square)
            )

        rows_loop(BLK, 16, gelu, unroll=2)

    def ff_out(k):
        part = dot(m.hid[blk_rows(chip(k)), :], m.wdn[...], 1, 0)
        if k == 0:
            m.resid[...] += part
        else:
            m.pout[k - 1] = part.astype(BF)

    def ff_backward(k):
        j = chip(k)
        keep = (k % 3) * BLK
        m.tmp[0:BLK, :] = dot(m.cot[blk_rows(j), :], m.wdn[...], 1, 1)

        def back(i):
            m.gupr[pl.ds(pl.multiple_of(j * BLK + i, 16), 16), :] = (
                m.tmp[pl.ds(i, 16), :] * m.dge[pl.ds(pl.multiple_of(keep + i, 16), 16), :]
            ).astype(BF)

        rows_loop(BLK, 16, back, unroll=2)
        part = dot(m.gupr[blk_rows(j), :], m.wup[...], 1, 1)
        if k == 0:
            m.own[...] = part
        else:
            m.pgh[k - 1] = part.astype(BF)

    other_cols = ds((1 - c) * HALF, HALF, LANES)
    own_cols = ds(c * HALF, HALF, LANES)

    def add_product(first, dst, left, right):
        part = dot(left, right, 0, 0)
        if first:
            dst[...] = part
        else:
            dst[...] += part

    def down_grads(k):
        rows = blk_rows(chip(k))
        add_product(k == 0, m.gdx, m.hid[rows, other_cols], m.cot[rows, :])
        add_product(k == 0, m.gdo, m.hid[rows, own_cols], m.cot[rows, :])

    def up_grads(k):
        rows = blk_rows(chip(k))
        for at in (0, HALF):
            add_product(
                k == 0, m.guo.at[pl.ds(at, HALF)], m.h2[rows, at : at + HALF], m.gupr[rows, :]
            )

    ff_forward(0)
    ff_backward(0)
    gather_forward("h2")
    start("ctX1", "ctY0")
    ff_out(0)
    down_grads(0)
    up_grads(0)
    for k in (1, 2):
        gather_wait("h2", k)
        ff_forward(k)
    gather_wait("h2", 3)
    ff_forward(3)
    gather_wait("ct", 3)
    ff_backward(3)
    scatter_diagonal("g2", m.pgh, m.rbg2, TOK)
    gather_wait("ct", 1)
    ff_backward(1)
    scatter_direct_x("g2", m.pgh, m.rbg2, TOK)
    gather_wait("ct", 2)
    ff_backward(2)
    scatter_direct_y("g2", m.pgh, m.rbg2, TOK)
    for k in (3, 1, 2):
        down_grads(k)

    for j in range(CHIPS):
        m.gds[j] = m.gdx[j * ROWS : (j + 1) * ROWS, :].astype(BF)
    send("gdS", m.gds, m.gdr, SIB)

    def split_rows(left, right, kept, leaving):
        width = right.shape[1]
        for i in range(2):
            m.tmp[:, 0:width] = dot(left[:, i * HALF : (i + 1) * HALF], right[...], 0, 0)
            for q in range(2):
                kept[2 * i + q] = m.tmp[ds((2 * q + c) * ROWS, ROWS, 32), 0:width]
                leaving[2 * i + q] = m.tmp[ds((2 * q + 1 - c) * ROWS, ROWS, 32), 0:width].astype(BF)

    def pair_sum(name, kept, came, base):
        for k in ORDER:
            j = chip(k)
            base[j] = (kept(j) + came[j].astype(F32)).astype(BF)
            z_start(f"{name}{k}")

    def pack(dst, at, rows):
        n = rows.shape[0]
        dst[at : at + n, :] = rows[:, :LANES].astype(BF)
        dst[at + n : at + n + n // 2, :] = jnp.concatenate(
            [rows[: n // 2, LANES:SL], rows[n // 2 :, LANES:SL]], axis=1
        ).astype(BF)

    def pair_sum_packed(name, kept, came, base):
        for k in ORDER:
            j = chip(k)
            total = kept[j] + came[j].astype(F32)
            for i in range(total.shape[1] // SLP):
                pack(base.at[j], i * PACK, total[:, i * SLP : (i + 1) * SLP])
            z_start(f"{name}{k}")

    scatter_combine("g2", m.pgh, m.rbg2, TOK)
    up_grads(3)
    got("gdS")
    pair_sum("zd", lambda j: m.gdo[ds(j * ROWS, ROWS, 32), :], m.gdr, m.zdb)
    up_grads(1)
    up_grads(2)
    for j in range(CHIPS):
        m.gus[j] = m.guo[ds((2 * j + 1 - c) * ROWS, ROWS, 32), :].astype(BF)
    send("guS", m.gus, m.gur, SIB)
    ff_out(3)
    scatter_diagonal("ou", m.pout, m.rbout, TOK)
    got("guS")
    pair_sum("zu", lambda j: m.guo[ds((2 * j + c) * ROWS, ROWS, 32), :], m.gur, m.zub)
    for k in (1, 2):
        ff_out(k)
    poll(1)

    scatter_wait("g2")

    def norm_back(total, gain_row, n_ref, r_ref, i, base):
        rows = pl.ds(i, 32)
        e = total * m.gain[gain_row : gain_row + 1, :]
        n = n_ref[rows, :]
        mean_e = jnp.mean(e, axis=-1, keepdims=True)
        mean_en = jnp.mean(e * n, axis=-1, keepdims=True)
        return base + r_ref[rows, 0:1] * (e - mean_e - n * mean_en)

    for h in range(2):

        def back_two(i, h=h):
            at = pl.multiple_of(h * TOK + i, 32)
            rows = pl.ds(at, 32)
            total = m.own[rows, :] + scatter_sum(m.rbg2, TOK, h, pl.ds(i, 32))
            base = m.cot[pl.ds(pl.multiple_of(b * BLK + at, 32), 32), :].astype(F32)
            g = norm_back(total, 1, m.n2, m.r2, at, base)
            m.gresid[rows, :] = g
            m.gattn[rows, :] = g.astype(BF)

        rows_loop(TOK, 32, back_two, unroll=2)
    poll(2)

    for k, to in ((3, PD), (1, PX), (2, PY)):
        part = dot(m.gattn[...], m.wout[ds(chip(k) * SLP, SLP, SLP), :], 1, 1)
        m.ggs[k - 1] = part[:, :LANES].astype(BF)
        send(f"gg{k}", m.ggs.at[k - 1], m.ggr.at[k, :, low_lanes], to)
        high = part[:, LANES:]
        m.gghs[k - 1] = (high[:TOK] + pltpu.roll(high[TOK:], SL - LANES, 1)).astype(BF)
        send(f"gi{k}", m.gghs.at[k - 1], m.gghr.at[k - 1], to)
    m.ggr[0] = dot(m.gattn[...], m.wout[ds(b * SLP, SLP, SLP), :], 1, 1).astype(BF)
    poll(3)
    for k in range(CHIPS):
        m.tmp[0:SLP, :] = dot(m.grecv[k], m.gattn[...], 0, 0)
        m.goo[k] = m.tmp[ds(c * ROWS, ROWS, 32), :]
        m.gos[k] = m.tmp[ds((1 - c) * ROWS, ROWS, 32), :].astype(BF)
    send("goS", m.gos, m.gor, SIB)
    poll(4)

    gqkv = m.hid
    gres = m.h2
    sent("h2X0", "h2X1", "h2Y0", "h2Y1", "h2F0", "h2F1")

    def mix_back(k):
        j = chip(k)

        def body(i):
            at = pl.multiple_of(j * BLK + i, 16)
            rows = pl.ds(at, 16)
            gg = m.ggr[k, pl.ds(i, 16), :].astype(F32)
            sig = m.sig[rows, :]
            gm = (gg * sig).astype(BF).astype(F32)
            gqkv[rows, 0:SLP] = (
                gg * m.mixed[rows, :].astype(F32) * sig * (1.0 - sig)
            ).astype(BF)
            gnum = gm * m.rden[rows, :]
            gres[rows, 0:SLP] = gnum.astype(BF)
            gres[rows, SLP : 2 * SLP] = (-gnum * m.ratio[rows, :]).astype(BF)

        rows_loop(BLK, 16, body, unroll=2)

    mix_back(0)
    poll(5)
    got("goS")
    for k in (1, 2, 3):
        m.po[k - 1] = (m.goo[k] + m.gor[k].astype(F32)).astype(BF)
    scatter_diagonal("wg", m.po, m.rbo, ROWS // 2)
    scatter_direct_x("wg", m.po, m.rbo, ROWS // 2)
    scatter_direct_y("wg", m.po, m.rbo, ROWS // 2)
    scatter_direct_x("ou", m.pout, m.rbout, TOK)
    scatter_direct_y("ou", m.pout, m.rbout, TOK)
    poll(6)
    for k in (1, 2, 3):
        got(f"gg{k}", f"gi{k}")
        unpack(m.ggr.at[k], m.gghr.at[k - 1])
        mix_back(k)
        poll(6 + k)
    scatter_combine("wg", m.po, m.rbo, ROWS // 2)
    m.sums[...] = dot(ones, gres[:, 0 : 2 * SLP], 1, 0)
    m.gop[...] = jnp.broadcast_to(m.sums[0:1, :], (SEQ, 2 * SLP))
    poll(10)

    def kernel_grad(d):
        return dot(
            gres[ds(d * TOK, TOK, TOK), 0 : 2 * SLP], m.op[pl.ds(band_at(d), BAND), :], 1, 1
        )

    for k in range(CHIPS):
        m.gks[k] = kernel_grad(2 * chip(k) + 1 - c).astype(BF)
    send("gkS", m.gks, m.gkr, SIB)
    poll(11)
    split_rows(m.h1, gqkv.at[:, 0:SLP], m.gqo, m.gqs)
    send("gqS", m.gqs, m.gqr, SIB)
    poll(12)
    for k in range(CHIPS):
        m.gko[k] = kernel_grad(2 * chip(k) + c)
    poll(13)
    got("gkS")
    for k in (1, 2, 3):
        m.pk[k - 1] = (m.gko[k] + m.gkr[k].astype(F32)).astype(BF)
    scatter_diagonal("kg", m.pk, m.rbk, TOK // 2)
    scatter_direct_x("kg", m.pk, m.rbk, TOK // 2)
    scatter_direct_y("kg", m.pk, m.rbk, TOK // 2)
    poll(14)

    def mix_t(d, carry):
        at = pl.ds(band_at(d), BAND)
        m.gop[at, :] += dot(m.kern[d], gres[ds(d * TOK, TOK, TOK), 0 : 2 * SLP], 0, 0)
        return carry

    lax.fori_loop(0, CHIPS * CORES, mix_t, 0)
    poll(15)

    def keys_back(i):
        rows = pl.ds(i, 16)
        gkv = m.gop[rows, 0:SLP]
        w = m.wgt[rows, :]
        gqkv[rows, SLP : 2 * SLP] = (
            (gkv * m.val[rows, :].astype(F32) + m.gop[rows, SLP : 2 * SLP]) * w
        ).astype(BF)
        gqkv[rows, 2 * SLP : 3 * SLP] = (gkv * w).astype(BF)

    rows_loop(SEQ, 16, keys_back, unroll=2)
    poll(16)

    sent("g20", "g21", "g22", "g23", "g24", "g25")
    for k in ORDER:
        part = dot(gqkv[blk_rows(chip(k)), :], m.wqkv[...], 1, 1)
        if k == 0:
            m.own[...] = part
        else:
            m.pgh[k - 1] = part.astype(BF)
        if k == 3:
            scatter_diagonal("g1", m.pgh, m.rbg1, TOK)
        if k == 1:
            scatter_direct_x("g1", m.pgh, m.rbg1, TOK)
        if k == 2:
            scatter_direct_y("g1", m.pgh, m.rbg1, TOK)
        poll(17 + k)
    got("gqS")
    pair_sum_packed("zq", m.gqo, m.gqr, m.zqb)
    poll(21)

    def scattered(dst, mine, came, buf, half):
        for h in range(2):
            rows = pl.ds(h * half, half)
            dst[rows, :] = (
                mine[0, rows, :] + came[0, rows, :].astype(F32)
                + scatter_sum(buf, half, h, pl.ds(0, half))
            ).astype(BF)

    scatter_wait("wg")
    scattered(m.zob, m.goo, m.gor, m.rbo, ROWS // 2)
    z_start("zo0")
    z_start("zo1")
    poll(22)
    split_rows(m.h1, gqkv.at[:, SLP : 3 * SLP], m.gvo, m.gvs)
    send("gvS", m.gvs, m.gvr, SIB)
    poll(23)
    scatter_combine("kg", m.pk, m.rbk, TOK // 2)
    poll(24)
    scatter_combine("g1", m.pgh, m.rbg1, TOK)
    poll(25)
    got("gvS")
    pair_sum_packed("zv", m.gvo, m.gvr, m.zvb)
    poll(26)
    scatter_combine("ou", m.pout, m.rbout, TOK)
    poll(27)
    poll(28)
    scatter_wait("kg")
    scattered(m.zkb, m.gko, m.gkr, m.rbk, TOK // 2)
    z_start("zk0")
    z_start("zk1")

    poll(29)

    poll(30)
    scatter_wait("ou")
    for h in range(2):

        def out_rows(i, h=h):
            rows = pl.ds(pl.multiple_of(h * TOK + i, 32), 32)
            m.fout[rows, :] = (
                m.resid[rows, :] + scatter_sum(m.rbout, TOK, h, pl.ds(i, 32))
            ).astype(BF)

        rows_loop(TOK, 32, out_rows)
    send("outS", m.fout.at[other_half], out_out.at[c], SIB)
    local_copy(m.fout.at[own_half], out_out.at[c])

    scatter_wait("g1")
    for h in range(2):

        def back_one(i, h=h):
            at = pl.multiple_of(h * TOK + i, 32)
            rows = pl.ds(at, 32)
            total = m.own[rows, :] + scatter_sum(m.rbg1, TOK, h, pl.ds(i, 32))
            m.fgt[rows, :] = norm_back(total, 0, m.n1, m.r1, at, m.gresid[rows, :]).astype(BF)

        rows_loop(TOK, 32, back_one, unroll=2)
    send("gtS", m.fgt.at[other_half], gtok_out.at[c], SIB)
    local_copy(m.fgt.at[own_half], gtok_out.at[c])
    poll(31)

    for cp in locals_:
        if all(cp is not done for done in (l_tok, l_pb, l_wout, l_wup, l_wdn, l_cot, *l_w)):
            cp.wait()
    for name in begun:
        if name not in in_fetch:
            got(name)
            sent(name)

    @pl.when(fetch)
    def _():
        for name in in_fetch:
            sent(name)

    for name in zitems:
        z_close(name)


FIN_IN = dict(
    gq=((CHIPS, PACK, LANES), BF),
    gv=((CHIPS, 2 * PACK, LANES), BF),
    gup=((CHIPS, ROWS, FS), BF),
    gdn=((FF // (CHIPS * CORES), D), BF),
    gwout=((ROWS, D), BF),
    gpb=((TOK, BAND), BF),
    wq=((ROWS, D), BF),
    wk=((ROWS, D), BF),
    wv=((ROWS, D), BF),
    wup=((ROWS, FF), BF),
    pb=((TOK, BAND), BF),
    out=((2, TOK, D), BF),
    gtok=((2, TOK, D), BF),
)
FIN_OUT = dict(
    q=((ROWS, D), F32),
    k=((ROWS, D), F32),
    v=((ROWS, D), F32),
    o=((ROWS, D), F32),
    up=((ROWS, FF), F32),
    dn=((FF // (CHIPS * CORES), D), F32),
    bias=((TOK, SEQ), F32),
)


def finish_kernel(
    out_in, gtok_in, gq_in, gv_in, gwout_in, gup_in, gdn_in, gpb_in, ga_in, gm_in,
    wq_in, wk_in, wv_in, wup_in, pb_in,
    out_out, gtok_out, ga_out, q_out, k_out, v_out, o_out, gm_out, up_out, dn_out, bias_out,
    *scratch,
):
    m = types.SimpleNamespace(**dict(zip((*FIN_IN, *FIN_OUT), scratch)))
    in_sem, out_sem = scratch[len(FIN_IN) + len(FIN_OUT):]
    start = pl.multiple_of(
        jnp.minimum(jnp.maximum(lax.axis_index("dp") - 2, 0), 3) * LANES, LANES
    )
    stores = []

    def store(src, dst):
        stores.append(pltpu.make_async_copy(src, dst, out_sem.at[len(stores)]))
        stores[-1].start()

    sources = dict(
        gdn=gdn_in, gup=gup_in, wup=wup_in, out=out_in, gtok=gtok_in, gq=gq_in, wq=wq_in, gv=gv_in, wk=wk_in,
        wv=wv_in, gwout=gwout_in, gpb=gpb_in, pb=pb_in.at[:, pl.ds(start, BAND)],
    )
    loads = types.SimpleNamespace(
        **{
            name: pltpu.make_async_copy(src, vars(m)[name], in_sem.at[i])
            for i, (name, src) in enumerate(sources.items())
        }
    )
    for cp in vars(loads).values():
        cp.start()

    loads.gdn.wait()
    m.dn[...] = m.gdn[...].astype(F32)
    store(m.dn, dn_out)

    def as_row(column, gain):
        square = jnp.broadcast_to(column, (ROWS, LANES))
        return jnp.transpose(square)[0:1, :] / gain[...].astype(F32)

    loads.gup.wait()
    loads.wup.wait()
    column = jnp.zeros((ROWS, 1), F32)
    for j in range(CHIPS):
        cols = slice(j * FS, (j + 1) * FS)
        g = m.gup[j].astype(F32)
        m.up[:, cols] = g
        store(m.up.at[:, cols], up_out.at[:, cols])
        column += jnp.sum(g * m.wup[:, cols].astype(F32), axis=1, keepdims=True)
    loads.out.wait()
    store(m.out, out_out)
    loads.gtok.wait()
    store(m.gtok, gtok_out)
    gm_out[...] = as_row(column, gm_in)

    def unpack(ref, j, at):
        low = ref[j, at : at + ROWS, :].astype(F32)
        high = ref[j, at + ROWS : at + PACK, :].astype(F32)
        rest = SL - LANES
        return jnp.concatenate(
            [low, jnp.concatenate([high[:, :rest], high[:, rest:]], axis=0)], axis=1
        )

    column = jnp.zeros((ROWS, 1), F32)
    for needs, ref, at, w, mine, dst in (
        ((loads.gq, loads.wq), m.gq, 0, m.wq, m.q, q_out),
        ((loads.gv, loads.wk), m.gv, 0, m.wk, m.k, k_out),
        ((loads.wv,), m.gv, PACK, m.wv, m.v, v_out),
    ):
        for cp in needs:
            cp.wait()
        g = jnp.concatenate([unpack(ref, j, at) for j in range(CHIPS)], axis=1)
        mine[...] = g
        store(mine, dst)
        column += jnp.sum(g * w[...].astype(F32), axis=1, keepdims=True)
    ga_out[...] = as_row(column, ga_in)

    loads.gwout.wait()
    m.o[...] = m.gwout[...].astype(F32)
    store(m.o, o_out)
    loads.gpb.wait()
    loads.pb.wait()
    t_ids = lax.axis_index("dp") * TOK + lax.broadcasted_iota(jnp.int32, (TOK, BAND), 0)
    u_ids = start + lax.broadcasted_iota(jnp.int32, (TOK, BAND), 1)
    m.bias[...] = jnp.zeros((TOK, SEQ), F32)
    m.bias[:, pl.ds(start, BAND)] = jnp.where(
        jnp.abs(t_ids - u_ids) < WIN, m.gpb[...].astype(F32) * jnp.exp(m.pb[...].astype(F32)), 0.0
    )
    store(m.bias, bias_out)
    for cp in stores:
        cp.wait()


def plane_program(
    tokens, lengths, cotangent, gain_attn, w_query, w_key, w_value, w_out, gain_mlp, w_up, w_down, pos_bias
):
    anywhere = pl.BlockSpec(memory_space=pl.ANY)
    whole = pl.BlockSpec(memory_space=pltpu.VMEM)
    struct = jax.ShapeDtypeStruct
    results = pl.pallas_call(
        plane_kernel,
        out_shape=(
            struct((2, TOK, D), BF),
            struct((2, TOK, D), BF),
            struct((CHIPS, PACK, LANES), BF),
            struct((CHIPS, 2 * PACK, LANES), BF),
            struct((ROWS, D), BF),
            struct((CHIPS, ROWS, FS), BF),
            struct((CHIPS, ROWS, D), BF),
            struct((TOK, BAND), BF),
        ),
        in_specs=[anywhere, pl.BlockSpec(memory_space=pltpu.SMEM), anywhere, whole, whole] + [anywhere] * 7,
        out_specs=(anywhere,) * 8,
        scratch_shapes=[pltpu.VMEM(shape, kind) for shape, kind in SCRATCH.values()]
        + [
            pltpu.SemaphoreType.DMA((N_REMOTE,)),
            pltpu.SemaphoreType.DMA((N_REMOTE,)),
            pltpu.SemaphoreType.DMA((N_LOCAL,)),
        ],
        compiler_params=pltpu.CompilerParams(
            collective_id=0, has_side_effects=True, vmem_limit_bytes=VMEM_BYTES
        ),
        cost_estimate=pl.CostEstimate(
            flops=15_000_000_000, bytes_accessed=8_000_000, transcendentals=4_000_000
        ),
        name="aft_layer",
    )(
        tokens.reshape(2, TOK, D), lengths.reshape(2), cotangent.reshape(2, TOK, D),
        gain_attn.reshape(1, ROWS), gain_mlp.reshape(1, ROWS),
        w_query, w_key, w_value, w_out, w_up, w_down, pos_bias,
    )
    out, gtok, gq, gv, gwout, gup, gdn, gpb = results
    f32_out = [struct(shape, kind) for shape, kind in FIN_OUT.values()]
    row = struct((1, ROWS), F32)
    out, gtok, grad_gain_a, grad_q, grad_k, grad_v, grad_o, grad_gain_m, grad_up, grad_down, grad_bias = (
        pl.pallas_call(
            finish_kernel,
            out_shape=(struct((2, TOK, D), BF),) * 2 + (row, *f32_out[:4], row, *f32_out[4:]),
            in_specs=[anywhere] * 8 + [whole] * 2 + [anywhere] * 5,
            out_specs=(anywhere, anywhere, whole) + (anywhere,) * 4 + (whole,) + (anywhere,) * 3,
            scratch_shapes=[pltpu.VMEM(shape, kind) for shape, kind in (*FIN_IN.values(), *FIN_OUT.values())]
            + [pltpu.SemaphoreType.DMA((len(FIN_IN),)), pltpu.SemaphoreType.DMA((len(FIN_OUT) + 1 + CHIPS,))],
            compiler_params=pltpu.CompilerParams(vmem_limit_bytes=VMEM_BYTES),
            cost_estimate=pl.CostEstimate(flops=4_000_000, bytes_accessed=9_000_000, transcendentals=100_000),
            name="gradients_out",
        )(
            out, gtok, gq, gv, gwout, gup, gdn.reshape(FF // (CHIPS * CORES), D), gpb,
            gain_attn.reshape(1, ROWS), gain_mlp.reshape(1, ROWS),
            w_query, w_key, w_value, w_up, pos_bias,
        )
    )
    return (
        out.reshape(tokens.shape),
        gtok.reshape(tokens.shape),
        grad_gain_a.reshape(ROWS),
        grad_q,
        grad_k,
        grad_v,
        grad_o,
        grad_gain_m.reshape(ROWS),
        grad_up,
        grad_down,
        grad_bias,
    )


def solution(mesh):
    in_specs = (
        P(None, "pipe", "dp", None),
        P(None, "pipe", None),
        P(None, "pipe", "dp", None),
        P("dp"),
        P("dp", None),
        P("dp", None),
        P("dp", None),
        P("dp", None),
        P("dp"),
        P("dp", None),
        P("dp", None),
        P("dp", None),
    )
    out_specs = (
        P(None, "pipe", "dp", None),
        P(None, "pipe", "dp", None),
        P("dp"),
        P("dp", None),
        P("dp", None),
        P("dp", None),
        P("dp", None),
        P("dp"),
        P("dp", None),
        P("dp", None),
        P("dp", None),
    )
    fits = mesh.shape["dp"] == CHIPS * CORES and mesh.shape["pipe"] == DEPTH
    return jax.shard_map(plane_program if fits else local, mesh=mesh, in_specs=in_specs, out_specs=out_specs, check_vma=False)
```

```python
import types

import jax
import jax.numpy as jnp
from jax import lax
from jax.experimental import pallas as pl
from jax.experimental.pallas import tpu as pltpu
from jax.sharding import PartitionSpec as P

D = 768
FF = 3072
SEQ = 1024
WIN = 256


EPSILON = 1e-05
GELU_SCALE = 0.7978845608028654
GELU_CUBE = 0.044715
VMEM_BYTES = 63 * 2**20


def normalize(values, gain):
    centre = values - jnp.mean(values, axis=-1, keepdims=True)
    spread = jnp.mean(centre * centre, axis=-1, keepdims=True)
    return centre * lax.rsqrt(spread + EPSILON) * gain


def gelu_tanh(values):
    return jax.nn.gelu(values, approximate=True)


def band_ones(width):
    row_ids = jnp.arange(width)[:, None]
    col_ids = jnp.arange(3 * width)[None, :]
    return (jnp.abs(col_ids - width - row_ids) < width).astype(jnp.float32)


def band_blocks(bias, width):
    length = bias.shape[0]
    padded = jnp.pad(bias, ((0, 0), (width, width)))
    return jnp.stack(
        [
            padded[block * width : (block + 1) * width, block * width : block * width + 3 * width]
            for block in range(length // width)
        ]
    )


def windows(operand, width):
    blocks = operand.shape[0] // width
    padded = jnp.pad(operand, ((width, width), (0, 0))).reshape(blocks + 2, width, operand.shape[1])
    return jnp.concatenate([padded[:-2], padded[1:-1], padded[2:]], axis=1)


def unwindow(grad_windows, width):
    blocks = grad_windows.shape[0]
    leading = jnp.pad(grad_windows[:, :width], ((0, 2), (0, 0), (0, 0)))
    middle = jnp.pad(grad_windows[:, width : 2 * width], ((1, 1), (0, 0), (0, 0)))
    trailing = jnp.pad(grad_windows[:, 2 * width :], ((2, 0), (0, 0), (0, 0)))
    summed = leading + middle + trailing
    return summed[1:-1].reshape(blocks * width, grad_windows.shape[2])


def to_columns(matrix, seq_count, length):
    channels = matrix.shape[1]
    return (
        matrix.reshape(seq_count, length, channels)
        .transpose(1, 0, 2)
        .reshape(length, seq_count * channels)
    )


def from_columns(matrix, seq_count, length):
    channels = matrix.shape[1] // seq_count
    return (
        matrix.reshape(length, seq_count, channels)
        .transpose(1, 0, 2)
        .reshape(seq_count * length, channels)
    )


def outer_sum(left, right):
    return lax.dot_general(
        left, right, (((0,), (0,)), ((), ())), preferred_element_type=jnp.float32
    )


def times_transpose(left, right):
    return lax.dot_general(
        left, right, (((1,), (1,)), ((), ())), preferred_element_type=jnp.float32
    )


def local(
    tokens,
    lengths,
    cotangent,
    gain_attn,
    w_query,
    w_key,
    w_value,
    w_out,
    gain_mlp,
    w_up,
    w_down,
    pos_bias,
):
    gathered = (
        lax.all_gather(gain_attn, "dp", axis=0, tiled=True),
        lax.all_gather(w_query, "dp", axis=0, tiled=True),
        lax.all_gather(w_key, "dp", axis=0, tiled=True),
        lax.all_gather(w_value, "dp", axis=0, tiled=True),
        lax.all_gather(w_out, "dp", axis=0, tiled=True),
        lax.all_gather(gain_mlp, "dp", axis=0, tiled=True),
        lax.all_gather(w_up, "dp", axis=0, tiled=True),
        lax.all_gather(w_down, "dp", axis=0, tiled=True),
        lax.all_gather(pos_bias, "dp", axis=0, tiled=True),
    )
    gain_a = gathered[0].astype(jnp.float32)
    query_w, key_w, value_w, out_w = (gathered[1], gathered[2], gathered[3], gathered[4])
    gain_m = gathered[5].astype(jnp.float32)
    up_w, down_w = (gathered[6], gathered[7])
    bias_full = gathered[8].astype(jnp.float32)
    group_size = lax.axis_size("dp")
    tok_rows = tokens.shape[2]
    seq_count = group_size * tok_rows // SEQ
    band_mask = band_ones(WIN)
    bias_blocks = jnp.exp(band_blocks(bias_full, WIN))
    exp_band = bias_blocks * band_mask
    kernel = ((bias_blocks - 1.0) * band_mask).astype(jnp.bfloat16)
    positions = jnp.arange(SEQ)
    grad_gain_a = jnp.zeros((D,), jnp.float32)
    grad_gain_m = jnp.zeros((D,), jnp.float32)
    grad_query_w = jnp.zeros((D, D), jnp.float32)
    grad_key_w = jnp.zeros((D, D), jnp.float32)
    grad_value_w = jnp.zeros((D, D), jnp.float32)
    grad_out_w = jnp.zeros((D, D), jnp.float32)
    grad_up_w = jnp.zeros((D, FF), jnp.float32)
    grad_down_w = jnp.zeros((FF, D), jnp.float32)
    grad_kernel = jnp.zeros(exp_band.shape, jnp.float32)
    outputs_list = []
    grads_in_list = []
    for micro in range(tokens.shape[0]):
        inputs_f = tokens[micro, 0].astype(jnp.float32)
        normed_f, norm_back_a = jax.vjp(normalize, inputs_f, gain_a)
        normed = normed_f.astype(jnp.bfloat16)
        query = jnp.dot(normed, query_w, preferred_element_type=jnp.float32)
        keys = jnp.dot(normed, key_w, preferred_element_type=jnp.float32).astype(jnp.bfloat16)
        values = jnp.dot(normed, value_w, preferred_element_type=jnp.float32).astype(jnp.bfloat16)
        key_chan, value_chan = (
            lax.all_to_all(keys, "dp", split_axis=1, concat_axis=0, tiled=True),
            lax.all_to_all(values, "dp", split_axis=1, concat_axis=0, tiled=True),
        )
        seq_lengths = lengths[micro, 0]
        channels = key_chan.shape[1]
        valid_seq = (positions[:, None] < seq_lengths[None, :]).astype(jnp.float32)
        valid_cols = jnp.broadcast_to(valid_seq[:, :, None], (SEQ, seq_count, channels)).reshape(
            SEQ, seq_count * channels
        )
        key_cols = to_columns(key_chan, seq_count, SEQ).astype(jnp.float32)
        value_cols = to_columns(value_chan, seq_count, SEQ).astype(jnp.float32)
        weighted = jnp.exp(key_cols) * valid_cols
        col_count = weighted.shape[1]
        operand = jnp.concatenate(
            [(weighted * value_cols).astype(jnp.bfloat16), weighted.astype(jnp.bfloat16)], axis=1
        )
        windowed = windows(operand, WIN)
        banded = jnp.einsum(
            "nqk,nkc->nqc", kernel, windowed, preferred_element_type=jnp.float32
        ).reshape(SEQ, 2 * col_count)
        result = banded + jnp.sum(operand, axis=0, dtype=jnp.float32)[None, :]
        numerator = result[:, :col_count]
        denominator = result[:, col_count:] + 1.0 - valid_cols
        mixed_cols = numerator / denominator * valid_cols
        mixed_tok = lax.all_to_all(
            from_columns(mixed_cols.astype(jnp.bfloat16), seq_count, SEQ),
            "dp",
            split_axis=0,
            concat_axis=1,
            tiled=True,
        )
        sigmoid_q = jax.nn.sigmoid(query)
        mixed_f = mixed_tok.astype(jnp.float32)
        gated = (sigmoid_q * mixed_f).astype(jnp.bfloat16)
        resid = inputs_f + jnp.dot(gated, out_w, preferred_element_type=jnp.float32)
        normed_two_f, norm_back_m = jax.vjp(normalize, resid, gain_m)
        normed_two = normed_two_f.astype(jnp.bfloat16)
        upper = jnp.dot(normed_two, up_w, preferred_element_type=jnp.float32)
        hidden_f, gelu_back = jax.vjp(gelu_tanh, upper)
        hidden = hidden_f.astype(jnp.bfloat16)
        outputs_list.append(
            (resid + jnp.dot(hidden, down_w, preferred_element_type=jnp.float32)).astype(
                jnp.bfloat16
            )
        )
        grad_out = cotangent[micro, 0]
        grad_down_w = grad_down_w + outer_sum(hidden, grad_out)
        grad_hidden = times_transpose(grad_out, down_w)
        grad_upper = gelu_back(grad_hidden)[0].astype(jnp.bfloat16)
        grad_up_w = grad_up_w + outer_sum(normed_two, grad_upper)
        grad_normed_two = times_transpose(grad_upper, up_w)
        grad_resid_norm, grad_gain_part_m = norm_back_m(grad_normed_two)
        grad_gain_m = grad_gain_m + grad_gain_part_m
        grad_resid = grad_out.astype(jnp.float32) + grad_resid_norm
        grad_attn = grad_resid.astype(jnp.bfloat16)
        grad_out_w = grad_out_w + outer_sum(gated, grad_attn)
        grad_gated = times_transpose(grad_attn, out_w)
        grad_mixed = (grad_gated * sigmoid_q).astype(jnp.bfloat16)
        grad_query = (grad_gated * mixed_f * sigmoid_q * (1.0 - sigmoid_q)).astype(jnp.bfloat16)
        grad_mixed_chan = lax.all_to_all(grad_mixed, "dp", split_axis=1, concat_axis=0, tiled=True)
        grad_mixed_cols = to_columns(grad_mixed_chan, seq_count, SEQ).astype(jnp.float32)
        grad_numerator = grad_mixed_cols * valid_cols / denominator
        grad_denominator = -grad_numerator * (numerator / denominator)
        grad_flat = jnp.concatenate(
            [grad_numerator.astype(jnp.bfloat16), grad_denominator.astype(jnp.bfloat16)], axis=1
        )
        grad_result = grad_flat.reshape(SEQ // WIN, WIN, 2 * col_count)
        grad_windowed = jnp.einsum(
            "nqk,nqc->nkc", kernel, grad_result, preferred_element_type=jnp.float32
        )
        grad_kernel = grad_kernel + jnp.einsum(
            "nqc,nkc->nqk", grad_result, windowed, preferred_element_type=jnp.float32
        )
        grad_operand = (
            unwindow(grad_windowed, WIN) + jnp.sum(grad_flat, axis=0, dtype=jnp.float32)[None, :]
        )
        grad_key_value = grad_operand[:, :col_count]
        grad_key_weight = grad_operand[:, col_count:]
        grad_keys_cols = (grad_key_value * value_cols + grad_key_weight) * weighted
        grad_values_cols = grad_key_value * weighted
        grad_keys, grad_values = (
            lax.all_to_all(
                from_columns(grad_keys_cols.astype(jnp.bfloat16), seq_count, SEQ),
                "dp",
                split_axis=0,
                concat_axis=1,
                tiled=True,
            ),
            lax.all_to_all(
                from_columns(grad_values_cols.astype(jnp.bfloat16), seq_count, SEQ),
                "dp",
                split_axis=0,
                concat_axis=1,
                tiled=True,
            ),
        )
        grad_query_w = grad_query_w + outer_sum(normed, grad_query)
        grad_key_w = grad_key_w + outer_sum(normed, grad_keys)
        grad_value_w = grad_value_w + outer_sum(normed, grad_values)
        grad_normed = (
            times_transpose(grad_query, query_w)
            + times_transpose(grad_keys, key_w)
            + times_transpose(grad_values, value_w)
        )
        grad_input_norm, grad_gain_part_a = norm_back_a(grad_normed)
        grad_gain_a = grad_gain_a + grad_gain_part_a
        grads_in_list.append((grad_resid + grad_input_norm).astype(jnp.bfloat16))
    grad_kernel_bias = grad_kernel * exp_band
    grad_bias_pad = jnp.zeros((SEQ, SEQ + 2 * WIN), jnp.float32)
    for block in range(SEQ // WIN):
        grad_bias_pad = grad_bias_pad.at[
            block * WIN : (block + 1) * WIN, block * WIN : block * WIN + 3 * WIN
        ].add(grad_kernel_bias[block])
    grad_bias = grad_bias_pad[:, WIN : WIN + SEQ]
    shares = (
        lax.psum_scatter(grad_gain_a, "dp", scatter_dimension=0, tiled=True),
        lax.psum_scatter(grad_query_w, "dp", scatter_dimension=0, tiled=True),
        lax.psum_scatter(grad_key_w, "dp", scatter_dimension=0, tiled=True),
        lax.psum_scatter(grad_value_w, "dp", scatter_dimension=0, tiled=True),
        lax.psum_scatter(grad_out_w, "dp", scatter_dimension=0, tiled=True),
        lax.psum_scatter(grad_gain_m, "dp", scatter_dimension=0, tiled=True),
        lax.psum_scatter(grad_up_w, "dp", scatter_dimension=0, tiled=True),
        lax.psum_scatter(grad_down_w, "dp", scatter_dimension=0, tiled=True),
        lax.psum_scatter(grad_bias, "dp", scatter_dimension=0, tiled=True),
    )
    reduced = lax.psum(
        (
            shares[0],
            shares[1],
            shares[2],
            shares[3],
            shares[4],
            shares[5],
            shares[6],
            shares[7],
            shares[8],
        ),
        "pipe",
    )
    final_grads = (
        reduced[0],
        reduced[1],
        reduced[2],
        reduced[3],
        reduced[4],
        reduced[5],
        reduced[6],
        reduced[7],
        reduced[8],
    )
    output = jnp.stack(outputs_list)[:, None]
    grad_tokens = jnp.stack(grads_in_list)[:, None]
    return (
        output,
        grad_tokens,
        final_grads[0],
        final_grads[1],
        final_grads[2],
        final_grads[3],
        final_grads[4],
        final_grads[5],
        final_grads[6],
        final_grads[7],
        final_grads[8],
    )


CHIPS = 4
CORES = 2
DEPTH = 4
LANES = 128
TOK = 128
BLK = CORES * TOK
ROWS = D // (CHIPS * CORES)
SL = D // CHIPS
SLP = -(-SL // LANES) * LANES
FS = FF // CHIPS
BAND = 5 * LANES
HALF = D // 2
PACK = ROWS + ROWS // 2
MESH_ID = pl.DeviceIdType.MESH
F32 = jnp.float32
BF = jnp.bfloat16

SCRATCH = dict(
    tok=((BLK, D), BF),
    cot=((SEQ, D), BF),
    gains=((CHIPS * CORES, 16, LANES), BF),
    gain=((16, D), F32),
    wst=((3, ROWS, D), BF),
    wqs=((CHIPS, ROWS, 3 * SLP), BF),
    wqkv=((D, 3 * SLP), BF),
    wout=((CHIPS * SLP, D), BF),
    wup=((D, FS), BF),
    wdn=((FS, D), BF),
    pbw=((TOK, BAND), BF),
    kern=((CHIPS * CORES, TOK, BAND), BF),
    h1=((SEQ, D), BF),
    h2=((SEQ, D), BF),
    n1=((BLK, D), F32),
    r1=((BLK, LANES), F32),
    n2=((BLK, D), F32),
    r2=((BLK, LANES), F32),
    tmp=((HALF, D), F32),
    tmix=((TOK, 2 * SLP), F32),
    sums=((8, 2 * SLP), F32),
    sig=((SEQ, SLP), F32),
    wgt=((SEQ, SLP), F32),
    val=((SEQ, SLP), BF),
    op=((SEQ, 2 * SLP), BF),
    ratio=((SEQ, SLP), F32),
    rden=((SEQ, SLP), F32),
    mixed=((SEQ, SLP), BF),
    gated=((SEQ, SLP), BF),
    grecv=((CHIPS, BLK, SLP), BF),
    ghs=((CHIPS, TOK, LANES), BF),
    ghr=((CHIPS - 1, TOK, LANES), BF),
    gghs=((CHIPS - 1, TOK, LANES), BF),
    gghr=((CHIPS - 1, TOK, LANES), BF),
    resid=((BLK, D), F32),
    hid=((SEQ, FS), BF),
    dge=((3 * BLK, FS), F32),
    gop=((SEQ, 2 * SLP), F32),
    gupr=((SEQ, FS), BF),
    pout=((CHIPS - 1, BLK, D), BF),
    pgh=((CHIPS - 1, BLK, D), BF),
    own=((BLK, D), F32),
    rbout=((6, TOK, D), BF),
    rbg2=((6, TOK, D), BF),
    rbg1=((6, TOK, D), BF),
    gresid=((BLK, D), F32),
    gattn=((BLK, D), BF),
    ggs=((CHIPS - 1, BLK, LANES), BF),
    ggr=((CHIPS, BLK, SLP), BF),
    gdo=((HALF, D), F32),
    gdx=((HALF, D), F32),
    gds=((CHIPS, ROWS, D), BF),
    gdr=((CHIPS, ROWS, D), BF),
    guo=((D, FS), F32),
    gus=((CHIPS, ROWS, FS), BF),
    gur=((CHIPS, ROWS, FS), BF),
    gqo=((CHIPS, ROWS, SLP), F32),
    gqs=((CHIPS, ROWS, SLP), BF),
    gqr=((CHIPS, ROWS, SLP), BF),
    gvo=((CHIPS, ROWS, 2 * SLP), F32),
    gvs=((CHIPS, ROWS, 2 * SLP), BF),
    gvr=((CHIPS, ROWS, 2 * SLP), BF),
    goo=((CHIPS, ROWS, D), F32),
    gos=((CHIPS, ROWS, D), BF),
    gor=((CHIPS, ROWS, D), BF),
    po=((CHIPS - 1, ROWS, D), BF),
    rbo=((6, ROWS // 2, D), BF),
    gko=((CHIPS, TOK, BAND), F32),
    gks=((CHIPS, TOK, BAND), BF),
    gkr=((CHIPS, TOK, BAND), BF),
    pk=((CHIPS - 1, TOK, BAND), BF),
    rbk=((6, TOK // 2, BAND), BF),
    zdb=((CHIPS, ROWS, D), BF),
    zdr=((CHIPS, ROWS, D), BF),
    zdt=((CHIPS, ROWS, D), BF),
    zub=((CHIPS, ROWS, FS), BF),
    zur=((CHIPS, ROWS, FS), BF),
    zut=((CHIPS, ROWS, FS), BF),
    zqb=((CHIPS, PACK, LANES), BF),
    zqr=((CHIPS, PACK, LANES), BF),
    zqt=((CHIPS, PACK, LANES), BF),
    zvb=((CHIPS, 2 * PACK, LANES), BF),
    zvr=((CHIPS, 2 * PACK, LANES), BF),
    zvt=((CHIPS, 2 * PACK, LANES), BF),
    zob=((ROWS, D), BF),
    zor=((ROWS, D), BF),
    zot=((ROWS, D), BF),
    zkb=((TOK, BAND), BF),
    zkr=((TOK, BAND), BF),
    zkt=((TOK, BAND), BF),
    fout=((BLK, D), BF),
    fgt=((BLK, D), BF),
)
POLLS = {
    1: ("d3",),
    2: ("d1",),
    4: ("d2", "D3",),
    6: ("d0", "D1",),
    9: ("D2",),
    11: ("u3",),
    13: ("D0",),
    15: ("u1",),
    16: ("u2",),
    23: ("u0", "U3",),
    25: ("U1",),
    27: ("U2", "U0",),
    28: ("q3", "q1", "q2", "q0", "o0", "o1", "+U3", "+U1",),
    29: ("Q3", "v3", "Q1", "v1", "Q2", "v2", "Q0", "v0", "O0", "O1", "V3", "V1", "V2", "V0", "k0", "k1", "+U2", "+U0",),
    30: ("+Q3", "+Q1", "+Q2", "+Q0",),
    31: ("K0", "K1", "+V3", "+V1", "+V2", "+V0", "+O0", "+O1", "+D3", "+D1", "+D2", "+D0", "+K0", "+K1",),
}
N_REMOTE = 200
N_LOCAL = 40


def dot(left, right, left_dim, right_dim):
    return lax.dot_general(
        left, right, (((left_dim,), (right_dim,)), ((), ())), preferred_element_type=F32
    )


def rows_loop(count, step, body, unroll=1):
    def one(i, carry):
        body(pl.multiple_of(i * step, step))
        return carry

    lax.fori_loop(0, count // step, one, 0, unroll=unroll)


def plane_kernel(
    tok_in, len_in, cot_in, ga_in, gm_in, wq_in, wk_in, wv_in, wout_in, wup_in, wdn_in, pb_in,
    out_out, gtok_out, gq_out, gv_out, gwout_out, gup_out, gdn_out, gpb_out,
    *scratch,
):
    m = types.SimpleNamespace(**dict(zip(SCRATCH, scratch)))
    send_sem, recv_sem, local_sem = scratch[len(SCRATCH):]
    r = lax.axis_index("dp")
    z = lax.axis_index("pipe")
    c = lax.rem(r, 2)
    x = lax.rem(r // 2, 2)
    y = r // 4
    b = r // 2
    length = len_in[c]

    def chip(k):
        return 2 * (1 - y if k // 2 else y) + (1 - x if k % 2 else x)

    def peer(k, other=0):
        return (2 * chip(k) + (1 - c if other else c), z)

    jx, jy, jd = chip(1), chip(2), chip(3)
    SIB, PX, PY, PD = peer(0, 1), peer(1), peer(2), peer(3)
    z_near = z + 1 - 2 * lax.rem(z, 2)
    z_far = 3 - z
    ZN, ZF = (r, z_near), (r, z_far)
    outer = z * (3 - z) == 0
    inner = z * (3 - z) != 0

    remote, locals_ = {}, []
    waited = set()
    begun = []

    def make(name, src, dst, to):
        assert name not in remote, name
        i = len(remote)
        cp = pltpu.make_async_remote_copy(
            src_ref=src, dst_ref=dst, send_sem=send_sem.at[i], recv_sem=recv_sem.at[i],
            device_id=to, device_id_type=MESH_ID,
        )
        remote[name] = cp
        return cp

    def send(name, src, dst, to):
        make(name, src, dst, to)
        start(name)

    def start(*names):
        for name in names:
            begun.append(name)
            remote[name].start()

    def got(*names):
        for name in names:
            if name not in waited:
                waited.add(name)
                remote[name].wait_recv()

    def sent(*names):
        for name in names:
            if name + "/s" not in waited:
                waited.add(name + "/s")
                remote[name].wait_send()

    def local_copy(src, dst):
        cp = pltpu.make_async_copy(src, dst, local_sem.at[len(locals_)])
        locals_.append(cp)
        cp.start()
        return cp

    def ds(start, size, unit):
        return pl.ds(pl.multiple_of(start, unit), size)

    def band_at(d):
        return pl.multiple_of(jnp.minimum(jnp.maximum(d - 2, 0), 3) * LANES, LANES)

    def gather_open(name, blk):
        make(name + "X0", blk(b, 0), blk(b, 0), PX)
        make(name + "Y1", blk(b, 1), blk(b, 1), PY)
        make(name + "X1", blk(b, 1), blk(b, 1), PX)
        make(name + "Y0", blk(b, 0), blk(b, 0), PY)
        make(name + "F0", blk(jx, 0), blk(jx, 0), PY)
        make(name + "F1", blk(jy, 1), blk(jy, 1), PX)

    def gather_start(name):
        start(name + "X0", name + "Y1", name + "X1", name + "Y0")

    def gather_forward(name):
        got(name + "X0")
        start(name + "F0")
        got(name + "Y1")
        start(name + "F1")

    def gather_wait(name, k):
        got(*{1: (name + "X0", name + "X1"), 2: (name + "Y0", name + "Y1"), 3: (name + "F0", name + "F1")}[k])

    fetch = lax.rem(z, 2) == c
    passed = lax.rem(z, 2) != c
    in_fetch = []

    def relay_open(name, place):
        for k in (1, 2, 3):
            make(f"{name}Z{k}", place(k), place(k), ZN)
            in_fetch.append(f"{name}Z{k}")

    def relay(name, place, arrive):
        for k in (1, 2, 3):

            @pl.when(fetch)
            def _(k=k):
                arrive(k)
                start(f"{name}Z{k}")

            @pl.when(passed)
            def _(k=k):
                remote[f"{name}Z{k}"].wait_recv()

            waited.add(f"{name}Z{k}")
            send(f"{name}S{k}", place(k), place(k), SIB)

    def scatter_diagonal(name, part, buf, half):
        send(name + "0", part.at[2, pl.ds(half, half)], buf.at[0], PX)
        send(name + "1", part.at[2, pl.ds(0, half)], buf.at[1], PY)

    def scatter_direct_x(name, part, buf, half):
        send(name + "2", part.at[0, pl.ds(half, half)], buf.at[2], PX)

    def scatter_direct_y(name, part, buf, half):
        send(name + "3", part.at[1, pl.ds(0, half)], buf.at[3], PY)

    def scatter_combine(name, part, buf, half):
        got(name + "1")
        part[0, pl.ds(0, half), :] = (
            part[0, pl.ds(0, half), :].astype(F32) + buf[1].astype(F32)
        ).astype(BF)
        send(name + "4", part.at[0, pl.ds(0, half)], buf.at[4], PX)
        got(name + "0")
        part[1, pl.ds(half, half), :] = (
            part[1, pl.ds(half, half), :].astype(F32) + buf[0].astype(F32)
        ).astype(BF)
        send(name + "5", part.at[1, pl.ds(half, half)], buf.at[5], PY)

    def scatter_wait(name):
        got(name + "2", name + "3", name + "4", name + "5")

    def scatter_sum(buf, half, h, rows):
        if h == 0:
            return buf[3, rows, :].astype(F32) + buf[4, rows, :].astype(F32)
        return buf[2, rows, :].astype(F32) + buf[5, rows, :].astype(F32)

    zitems = {}

    def half_rows(which, h):
        size = (ROWS if which == "O" else TOK) // 2
        return pl.ds(h * size, size)


    def z_open(name, base, near, total):
        zitems[name] = (
            base,
            near,
            total,
            make(name + "a", base, near, ZN),
            make(name + "b", base, total, ZF),
            make(name + "c", total, total, ZN),
        )

    def z_start(name):
        item = zitems[name]

        @pl.when(outer)
        def _():
            item[3].start()

    def z_mid(name):
        base, near, total, into, across, back = zitems[name]

        @pl.when(inner)
        def _():
            into.wait_recv()
            base[...] = (base[...].astype(F32) + near[...].astype(F32)).astype(BF)
            across.start()

    def z_end(name):
        base, near, total, into, across, back = zitems[name]

        @pl.when(inner)
        def _():
            across.wait_recv()
            total[...] = (base[...].astype(F32) + total[...].astype(F32)).astype(BF)
            back.start()

    def z_take(name):
        back = zitems[name][5]

        @pl.when(outer)
        def _():
            back.wait_recv()

    def z_close(name):
        base, near, total, into, across, back = zitems[name]

        @pl.when(outer)
        def _():
            into.wait_send()

        @pl.when(inner)
        def _():
            across.wait_send()
            back.wait_send()

    for k in range(CHIPS):
        j = chip(k)
        z_open(f"zd{k}", m.zdb.at[j], m.zdr.at[j], m.zdt.at[j])
        z_open(f"zu{k}", m.zub.at[j], m.zur.at[j], m.zut.at[j])
        z_open(f"zq{k}", m.zqb.at[j], m.zqr.at[j], m.zqt.at[j])
        z_open(f"zv{k}", m.zvb.at[j], m.zvr.at[j], m.zvt.at[j])
    for h in range(2):
        half = half_rows("O", h)
        z_open(f"zo{h}", m.zob.at[half], m.zor.at[half], m.zot.at[half])
        half = half_rows("K", h)
        z_open(f"zk{h}", m.zkb.at[half], m.zkr.at[half], m.zkt.at[half])
    ORDER = (3, 1, 2, 0)

    onward = {}

    def prepare(which, k):
        j = chip(k)
        whole = dict(D=m.zdt, U=m.zut, Q=m.zqt, V=m.zvt, O=m.zot, K=m.zkt)[which]
        out = dict(D=gdn_out, U=gup_out, Q=gq_out, V=gv_out, O=gwout_out, K=gpb_out)[which]
        if which in "UQV" and k:
            name = f"f{which}{k}"
            begun.append(name)
            return make(name, whole.at[j], out.at[b], peer(k))
        part = half_rows(which, k) if which in "OK" else j
        src, dst = whole.at[part], out.at[part]
        locals_.append(pltpu.make_async_copy(src, dst, local_sem.at[len(locals_)]))
        return locals_[-1]

    def poll(place):
        for step in POLLS.get(place, ()):
            code = step.strip("+")
            name = "z" + code.lower()
            if code.islower():
                z_mid(name)
                continue
            if name not in onward:
                onward[name] = prepare(code[0], int(code[1]))
            if step == code:
                z_end(name)
                pl.when(inner)(onward[name].start)
            else:
                z_take(name)
                pl.when(outer)(onward[name].start)

    own_half = ds(c * TOK, TOK, TOK)
    other_half = ds((1 - c) * TOK, TOK, TOK)
    l_tok = local_copy(tok_in.at[c], m.tok.at[own_half])
    l_w = [local_copy(w, m.wst.at[i]) for i, w in enumerate((wq_in, wk_in, wv_in))]
    l_pb = local_copy(pb_in.at[:, ds(band_at(r), BAND, LANES)], m.pbw)

    def wout_rows(j, core):
        return m.wout.at[ds(j * SLP + core * ROWS, ROWS, 32)]

    l_wout = local_copy(wout_in, wout_rows(b, c))
    up_rows = ds(r * ROWS, ROWS, 32)
    l_wup = local_copy(wup_in.at[:, ds(b * FS, FS, LANES)], m.wup.at[up_rows])
    dn_rows = ds(c * HALF, HALF, LANES)
    l_wdn = local_copy(wdn_in, m.wdn.at[dn_rows])
    cot_half = ds(b * BLK + c * TOK, TOK, TOK)
    l_cot = local_copy(cot_in.at[c], m.cot.at[cot_half])

    line = lax.broadcasted_iota(jnp.int32, (16, LANES), 0)
    fill = jnp.zeros((1, LANES - ROWS), F32)
    both_gains = [
        jnp.broadcast_to(jnp.concatenate([g[...].astype(F32), fill], axis=1), (16, LANES)) for g in (ga_in, gm_in)
    ]
    m.gains[r] = jnp.where(line == 0, both_gains[0], both_gains[1]).astype(BF)

    barrier = pltpu.get_barrier_semaphore()
    everyone = [peer(k, o) for k in range(CHIPS) for o in range(CORES) if (k, o) != (0, 0)] + [ZN, ZF]
    for other in everyone:
        pl.semaphore_signal(barrier, inc=1, device_id=other, device_id_type=MESH_ID)
    l_pb.wait()
    t_ids = r * TOK + lax.broadcasted_iota(jnp.int32, (TOK, BAND), 0)
    u_ids = band_at(r) + lax.broadcasted_iota(jnp.int32, (TOK, BAND), 1)
    in_band = jnp.abs(t_ids - u_ids) < WIN
    m.kern[r] = jnp.where(in_band, jnp.exp(m.pbw[...].astype(F32)) - 1.0, 0.0).astype(BF)

    for cp in l_w:
        cp.wait()
    for i in range(3):
        w_rows = m.wst[i].astype(F32)
        for j in range(CHIPS):
            piece = w_rows[:, j * SL : (j + 1) * SL]
            m.wqs[j, :, i * SLP : (i + 1) * SLP] = jnp.concatenate(
                [piece, jnp.zeros((ROWS, SLP - SL), F32)], axis=1
            ).astype(BF)
    pl.semaphore_wait(barrier, len(everyone))

    send("tokS", tok_in.at[1 - c], m.tok.at[own_half], SIB)
    gain_names = []
    for k in range(CHIPS):
        for o in range(CORES):
            if (k, o) != (0, 0):
                gain_names.append(f"gain{k}{o}")
                send(gain_names[-1], m.gains.at[r], m.gains.at[r], peer(k, o))

    def wout_blk(j, h):
        return m.wout.at[ds(j * SLP + c * ROWS + h * (ROWS // 2), ROWS // 2, 16)]

    gather_open("wo", wout_blk)
    in_fetch.extend("wo" + part for part in ("X0", "X1", "Y0", "Y1", "F0", "F1"))
    l_wout.wait()

    @pl.when(fetch)
    def _():
        gather_start("wo")

    for k, to in ((1, PX), (2, PY), (3, PD)):
        make(f"wq{k}", m.wqs.at[chip(k)], m.wqkv.at[up_rows], to)
        in_fetch.append(f"wq{k}")

    @pl.when(fetch)
    def _():
        start("wq1", "wq2", "wq3")

    def kern_blk(j, h):
        return m.kern.at[2 * j + c, pl.ds(h * (TOK // 2), TOK // 2)]

    gather_open("kn", kern_blk)
    in_fetch.extend("kn" + part for part in ("X0", "X1", "Y0", "Y1", "F0", "F1"))

    @pl.when(fetch)
    def _():
        gather_start("kn")

    send("knS0", m.kern.at[r], m.kern.at[r], SIB)

    send("wqS0", m.wqs.at[b], m.wqkv.at[up_rows], SIB)
    m.wqkv[up_rows, :] = m.wqs[b]

    def norm(src, n_ref, r_ref):
        def body(i):
            rows = pl.ds(i, 32)
            values = src[rows, :].astype(F32)
            centre = values - jnp.mean(values, axis=-1, keepdims=True)
            spread = jnp.mean(centre * centre, axis=-1, keepdims=True)
            rinv = lax.rsqrt(spread + EPSILON)
            n_ref[rows, :] = centre * rinv
            r_ref[rows, :] = jnp.broadcast_to(rinv, (32, LANES))

        rows_loop(BLK, 32, body, unroll=2)

    def scale(n_ref, gain_row, dst, base):
        def body(i):
            dst[pl.ds(pl.multiple_of(base + i, 32), 32), :] = (
                n_ref[pl.ds(i, 32), :] * m.gain[gain_row : gain_row + 1, :]
            ).astype(BF)

        rows_loop(BLK, 32, body, unroll=2)

    l_tok.wait()
    got("tokS")
    norm(m.tok, m.n1, m.r1)
    got(*gain_names)
    m.gain[...] = jnp.concatenate(
        [m.gains[d].astype(F32)[:, :ROWS] for d in range(CHIPS * CORES)], axis=1
    )
    scale(m.n1, 0, m.h1, b * BLK)

    def h1_blk(j, h):
        return m.h1.at[ds(j * BLK + h * TOK, TOK, TOK)]

    gather_open("h1", h1_blk)
    gather_start("h1")

    def w_place(ref):
        return lambda k: ref.at[ds((2 * chip(k) + c) * ROWS, ROWS, 32)]

    wq_place = w_place(m.wqkv)
    relay_open("wq", wq_place)
    relay("wq", wq_place, lambda k: got(f"wq{k}"))

    @pl.when(fetch)
    def _():
        gather_forward("kn")

    gather_forward("h1")
    for j in range(CHIPS):
        m.wout[j * SLP + SL : (j + 1) * SLP, :] = jnp.zeros((SLP - SL, D), BF)

    for k, to in ((1, PX), (2, PY), (3, PD)):
        make(f"wu{k}", wup_in.at[:, ds(chip(k) * FS, FS, LANES)], m.wup.at[up_rows], to)
        in_fetch.append(f"wu{k}")

    @pl.when(fetch)
    def _():
        gather_forward("wo")
        start("wu1", "wu2", "wu3")

    send("woS0", wout_rows(b, c), wout_rows(b, c), SIB)
    l_wup.wait()
    send("wuS0", m.wup.at[up_rows], m.wup.at[up_rows], SIB)
    l_wdn.wait()
    send("wdS", m.wdn.at[dn_rows], m.wdn.at[dn_rows], SIB)
    send("cotS", cot_in.at[1 - c], m.cot.at[cot_half], SIB)
    got("wqS0", "wqS1", "wqS2", "wqS3")

    def blk_rows(j):
        return ds(j * BLK, BLK, BLK)

    def project(j):
        m.tmp[0:BLK, :] = dot(m.h1[blk_rows(j), :], m.wqkv[...], 1, 0)

        def body(i):
            rows = pl.ds(i, 16)
            at = pl.multiple_of(j * BLK + i, 16)
            to = pl.ds(at, 16)
            q = m.tmp[rows, 0:SLP]
            m.sig[to, :] = 1.0 / (1.0 + jnp.exp(-q))
            keys = m.tmp[rows, SLP : 2 * SLP].astype(BF).astype(F32)
            values = m.tmp[rows, 2 * SLP : 3 * SLP].astype(BF)
            pos = at + lax.broadcasted_iota(jnp.int32, (16, SLP), 0)
            weighted = jnp.where(pos < length, jnp.exp(keys), 0.0)
            m.wgt[to, :] = weighted
            m.val[to, :] = values
            m.op[to, 0:SLP] = (weighted * values.astype(F32)).astype(BF)
            m.op[to, SLP : 2 * SLP] = weighted.astype(BF)

        rows_loop(BLK, 16, body, unroll=2)

    project(b)
    kn_place = lambda k: m.kern.at[2 * chip(k) + c]
    relay_open("kn", kn_place)
    relay("kn", kn_place, lambda k: gather_wait("kn", k))
    for k in (1, 2):
        gather_wait("h1", k)
        project(chip(k))
    gather_wait("h1", 3)
    project(jd)
    l_cot.wait()
    got("cotS")

    def cot_blk(j, h):
        return m.cot.at[ds(j * BLK + h * TOK, TOK, TOK)]

    gather_open("ct", cot_blk)
    start("ctX0", "ctY1")

    got("knS0", "knS1", "knS2", "knS3")
    ones = jnp.ones((8, SEQ), BF)
    m.sums[...] = dot(ones, m.op[...], 1, 0)

    def mix(j, half):
        d = 2 * j + half
        m.tmix[...] = dot(m.kern[d], m.op[pl.ds(band_at(d), BAND), :], 1, 0)

        def body(i):
            rows = pl.ds(i, 32)
            at = pl.multiple_of(d * TOK + i, 32)
            to = pl.ds(at, 32)
            pos = at + lax.broadcasted_iota(jnp.int32, (32, SLP), 0)
            valid = jnp.where(pos < length, 1.0, 0.0)
            num = m.tmix[rows, 0:SLP] + m.sums[0:1, 0:SLP]
            den = m.tmix[rows, SLP : 2 * SLP] + m.sums[0:1, SLP : 2 * SLP] + 1.0 - valid
            rden = 1.0 / den
            ratio = num * rden
            mixed = (ratio * valid).astype(BF)
            m.ratio[to, :] = ratio
            m.rden[to, :] = rden * valid
            m.mixed[to, :] = mixed
            gated = m.sig[to, :] * mixed.astype(F32)
            m.gated[to, :] = gated.astype(BF)
            high = gated[:, LANES:]
            m.ghs[j, rows, :] = jnp.where(
                half == 0, high, m.ghs[j, rows, :].astype(F32) + pltpu.roll(high, SL - LANES, 1)
            ).astype(BF)

        rows_loop(TOK, 32, body, unroll=2)

    def mix_block(j):
        def one(i, carry):
            mix(j, i)
            return carry

        lax.fori_loop(0, CORES, one, 0)

    low_lanes = pl.ds(0, LANES)

    def unpack(dst, high):
        lane = lax.broadcasted_iota(jnp.int32, (TOK, LANES), 1)
        both = high[...].astype(F32)
        for h in range(2):
            part = both if h == 0 else pltpu.roll(both, LANES - (SL - LANES), 1)
            dst[h * TOK : (h + 1) * TOK, LANES:] = jnp.where(lane < SL - LANES, part, 0.0).astype(BF)

    for k, to in ((3, PD), (1, PX), (2, PY)):
        j = chip(k)
        mix_block(j)
        send(f"ga{k}", m.gated.at[blk_rows(j), low_lanes], m.grecv.at[k, :, low_lanes], to)
        send(f"gh{k}", m.ghs.at[j], m.ghr.at[k - 1], to)
    mix_block(b)
    m.grecv[0] = m.gated[blk_rows(b), :]

    gather_forward("ct")
    wo_place = lambda k: wout_rows(chip(k), c)
    relay_open("wo", wo_place)
    relay("wo", wo_place, lambda k: gather_wait("wo", k))
    wu_place = w_place(m.wup)
    relay_open("wu", wu_place)
    relay("wu", wu_place, lambda k: got(f"wu{k}"))

    got("woS0", "woS1", "woS2", "woS3")
    m.resid[...] = m.tok[...].astype(F32)
    for k in (0, 1, 2, 3):
        if k:
            got(f"ga{k}", f"gh{k}")
            unpack(m.grecv.at[k], m.ghr.at[k - 1])
        m.resid[...] += dot(m.grecv[k], m.wout[ds(chip(k) * SLP, SLP, SLP), :], 1, 0)
    norm(m.resid, m.n2, m.r2)
    scale(m.n2, 1, m.h2, b * BLK)

    def h2_blk(j, h):
        return m.h2.at[ds(j * BLK + h * TOK, TOK, TOK)]

    gather_open("h2", h2_blk)
    gather_start("h2")

    got("wuS0", "wuS1", "wuS2", "wuS3", "wdS")

    def ff_forward(k):
        j = chip(k)
        keep = (k % 3) * BLK
        m.tmp[0:BLK, :] = dot(m.h2[blk_rows(j), :], m.wup[...], 1, 0)

        def gelu(i):
            v = m.tmp[pl.ds(i, 16), :]
            square = v * v
            t = jnp.tanh(GELU_SCALE * v * (1.0 + GELU_CUBE * square))
            half = 0.5 * (1.0 + t)
            m.hid[pl.ds(pl.multiple_of(j * BLK + i, 16), 16), :] = (v * half).astype(BF)
            m.dge[pl.ds(pl.multiple_of(keep + i, 16), 16), :] = half + 0.5 * v * (1.0 - t * t) * (
                GELU_SCALE * (1.0 + 3.0 * GELU_CUBE * square)
            )

        rows_loop(BLK, 16, gelu, unroll=2)

    def ff_out(k):
        part = dot(m.hid[blk_rows(chip(k)), :], m.wdn[...], 1, 0)
        if k == 0:
            m.resid[...] += part
        else:
            m.pout[k - 1] = part.astype(BF)

    def ff_backward(k):
        j = chip(k)
        keep = (k % 3) * BLK
        m.tmp[0:BLK, :] = dot(m.cot[blk_rows(j), :], m.wdn[...], 1, 1)

        def back(i):
            m.gupr[pl.ds(pl.multiple_of(j * BLK + i, 16), 16), :] = (
                m.tmp[pl.ds(i, 16), :] * m.dge[pl.ds(pl.multiple_of(keep + i, 16), 16), :]
            ).astype(BF)

        rows_loop(BLK, 16, back, unroll=2)
        part = dot(m.gupr[blk_rows(j), :], m.wup[...], 1, 1)
        if k == 0:
            m.own[...] = part
        else:
            m.pgh[k - 1] = part.astype(BF)

    other_cols = ds((1 - c) * HALF, HALF, LANES)
    own_cols = ds(c * HALF, HALF, LANES)

    def add_product(first, dst, left, right):
        part = dot(left, right, 0, 0)
        if first:
            dst[...] = part
        else:
            dst[...] += part

    def down_grads(k):
        rows = blk_rows(chip(k))
        add_product(k == 0, m.gdx, m.hid[rows, other_cols], m.cot[rows, :])
        add_product(k == 0, m.gdo, m.hid[rows, own_cols], m.cot[rows, :])

    def up_grads(k):
        rows = blk_rows(chip(k))
        for at in (0, HALF):
            add_product(
                k == 0, m.guo.at[pl.ds(at, HALF)], m.h2[rows, at : at + HALF], m.gupr[rows, :]
            )

    ff_forward(0)
    ff_backward(0)
    gather_forward("h2")
    start("ctX1", "ctY0")
    ff_out(0)
    down_grads(0)
    up_grads(0)
    for k in (1, 2):
        gather_wait("h2", k)
        ff_forward(k)
    gather_wait("h2", 3)
    ff_forward(3)
    gather_wait("ct", 3)
    ff_backward(3)
    scatter_diagonal("g2", m.pgh, m.rbg2, TOK)
    gather_wait("ct", 1)
    ff_backward(1)
    scatter_direct_x("g2", m.pgh, m.rbg2, TOK)
    gather_wait("ct", 2)
    ff_backward(2)
    scatter_direct_y("g2", m.pgh, m.rbg2, TOK)
    for k in (3, 1, 2):
        down_grads(k)

    for j in range(CHIPS):
        m.gds[j] = m.gdx[j * ROWS : (j + 1) * ROWS, :].astype(BF)
    send("gdS", m.gds, m.gdr, SIB)

    def split_rows(left, right, kept, leaving):
        width = right.shape[1]
        for i in range(2):
            m.tmp[:, 0:width] = dot(left[:, i * HALF : (i + 1) * HALF], right[...], 0, 0)
            for q in range(2):
                kept[2 * i + q] = m.tmp[ds((2 * q + c) * ROWS, ROWS, 32), 0:width]
                leaving[2 * i + q] = m.tmp[ds((2 * q + 1 - c) * ROWS, ROWS, 32), 0:width].astype(BF)

    def pair_sum(name, kept, came, base):
        for k in ORDER:
            j = chip(k)
            base[j] = (kept(j) + came[j].astype(F32)).astype(BF)
            z_start(f"{name}{k}")

    def pack(dst, at, rows):
        n = rows.shape[0]
        dst[at : at + n, :] = rows[:, :LANES].astype(BF)
        dst[at + n : at + n + n // 2, :] = jnp.concatenate(
            [rows[: n // 2, LANES:SL], rows[n // 2 :, LANES:SL]], axis=1
        ).astype(BF)

    def pair_sum_packed(name, kept, came, base):
        for k in ORDER:
            j = chip(k)
            total = kept[j] + came[j].astype(F32)
            for i in range(total.shape[1] // SLP):
                pack(base.at[j], i * PACK, total[:, i * SLP : (i + 1) * SLP])
            z_start(f"{name}{k}")

    scatter_combine("g2", m.pgh, m.rbg2, TOK)
    up_grads(3)
    got("gdS")
    pair_sum("zd", lambda j: m.gdo[ds(j * ROWS, ROWS, 32), :], m.gdr, m.zdb)
    up_grads(1)
    up_grads(2)
    for j in range(CHIPS):
        m.gus[j] = m.guo[ds((2 * j + 1 - c) * ROWS, ROWS, 32), :].astype(BF)
    send("guS", m.gus, m.gur, SIB)
    ff_out(3)
    scatter_diagonal("ou", m.pout, m.rbout, TOK)
    got("guS")
    pair_sum("zu", lambda j: m.guo[ds((2 * j + c) * ROWS, ROWS, 32), :], m.gur, m.zub)
    for k in (1, 2):
        ff_out(k)
    poll(1)

    scatter_wait("g2")

    def norm_back(total, gain_row, n_ref, r_ref, i, base):
        rows = pl.ds(i, 32)
        e = total * m.gain[gain_row : gain_row + 1, :]
        n = n_ref[rows, :]
        mean_e = jnp.mean(e, axis=-1, keepdims=True)
        mean_en = jnp.mean(e * n, axis=-1, keepdims=True)
        return base + r_ref[rows, 0:1] * (e - mean_e - n * mean_en)

    for h in range(2):

        def back_two(i, h=h):
            at = pl.multiple_of(h * TOK + i, 32)
            rows = pl.ds(at, 32)
            total = m.own[rows, :] + scatter_sum(m.rbg2, TOK, h, pl.ds(i, 32))
            base = m.cot[pl.ds(pl.multiple_of(b * BLK + at, 32), 32), :].astype(F32)
            g = norm_back(total, 1, m.n2, m.r2, at, base)
            m.gresid[rows, :] = g
            m.gattn[rows, :] = g.astype(BF)

        rows_loop(TOK, 32, back_two, unroll=2)
    poll(2)

    for k, to in ((3, PD), (1, PX), (2, PY)):
        part = dot(m.gattn[...], m.wout[ds(chip(k) * SLP, SLP, SLP), :], 1, 1)
        m.ggs[k - 1] = part[:, :LANES].astype(BF)
        send(f"gg{k}", m.ggs.at[k - 1], m.ggr.at[k, :, low_lanes], to)
        high = part[:, LANES:]
        m.gghs[k - 1] = (high[:TOK] + pltpu.roll(high[TOK:], SL - LANES, 1)).astype(BF)
        send(f"gi{k}", m.gghs.at[k - 1], m.gghr.at[k - 1], to)
    m.ggr[0] = dot(m.gattn[...], m.wout[ds(b * SLP, SLP, SLP), :], 1, 1).astype(BF)
    poll(3)
    for k in range(CHIPS):
        m.tmp[0:SLP, :] = dot(m.grecv[k], m.gattn[...], 0, 0)
        m.goo[k] = m.tmp[ds(c * ROWS, ROWS, 32), :]
        m.gos[k] = m.tmp[ds((1 - c) * ROWS, ROWS, 32), :].astype(BF)
    send("goS", m.gos, m.gor, SIB)
    poll(4)

    gqkv = m.hid
    gres = m.h2
    sent("h2X0", "h2X1", "h2Y0", "h2Y1", "h2F0", "h2F1")

    def mix_back(k):
        j = chip(k)

        def body(i):
            at = pl.multiple_of(j * BLK + i, 16)
            rows = pl.ds(at, 16)
            gg = m.ggr[k, pl.ds(i, 16), :].astype(F32)
            sig = m.sig[rows, :]
            gm = (gg * sig).astype(BF).astype(F32)
            gqkv[rows, 0:SLP] = (
                gg * m.mixed[rows, :].astype(F32) * sig * (1.0 - sig)
            ).astype(BF)
            gnum = gm * m.rden[rows, :]
            gres[rows, 0:SLP] = gnum.astype(BF)
            gres[rows, SLP : 2 * SLP] = (-gnum * m.ratio[rows, :]).astype(BF)

        rows_loop(BLK, 16, body, unroll=2)

    mix_back(0)
    poll(5)
    got("goS")
    for k in (1, 2, 3):
        m.po[k - 1] = (m.goo[k] + m.gor[k].astype(F32)).astype(BF)
    scatter_diagonal("wg", m.po, m.rbo, ROWS // 2)
    scatter_direct_x("wg", m.po, m.rbo, ROWS // 2)
    scatter_direct_y("wg", m.po, m.rbo, ROWS // 2)
    scatter_direct_x("ou", m.pout, m.rbout, TOK)
    scatter_direct_y("ou", m.pout, m.rbout, TOK)
    poll(6)
    for k in (1, 2, 3):
        got(f"gg{k}", f"gi{k}")
        unpack(m.ggr.at[k], m.gghr.at[k - 1])
        mix_back(k)
        poll(6 + k)
    scatter_combine("wg", m.po, m.rbo, ROWS // 2)
    m.sums[...] = dot(ones, gres[:, 0 : 2 * SLP], 1, 0)
    m.gop[...] = jnp.broadcast_to(m.sums[0:1, :], (SEQ, 2 * SLP))
    poll(10)

    def kernel_grad(d):
        return dot(
            gres[ds(d * TOK, TOK, TOK), 0 : 2 * SLP], m.op[pl.ds(band_at(d), BAND), :], 1, 1
        )

    for k in range(CHIPS):
        m.gks[k] = kernel_grad(2 * chip(k) + 1 - c).astype(BF)
    send("gkS", m.gks, m.gkr, SIB)
    poll(11)
    split_rows(m.h1, gqkv.at[:, 0:SLP], m.gqo, m.gqs)
    send("gqS", m.gqs, m.gqr, SIB)
    poll(12)
    for k in range(CHIPS):
        m.gko[k] = kernel_grad(2 * chip(k) + c)
    poll(13)
    got("gkS")
    for k in (1, 2, 3):
        m.pk[k - 1] = (m.gko[k] + m.gkr[k].astype(F32)).astype(BF)
    scatter_diagonal("kg", m.pk, m.rbk, TOK // 2)
    scatter_direct_x("kg", m.pk, m.rbk, TOK // 2)
    scatter_direct_y("kg", m.pk, m.rbk, TOK // 2)
    poll(14)

    def mix_t(d, carry):
        at = pl.ds(band_at(d), BAND)
        m.gop[at, :] += dot(m.kern[d], gres[ds(d * TOK, TOK, TOK), 0 : 2 * SLP], 0, 0)
        return carry

    lax.fori_loop(0, CHIPS * CORES, mix_t, 0)
    poll(15)

    def keys_back(i):
        rows = pl.ds(i, 16)
        gkv = m.gop[rows, 0:SLP]
        w = m.wgt[rows, :]
        gqkv[rows, SLP : 2 * SLP] = (
            (gkv * m.val[rows, :].astype(F32) + m.gop[rows, SLP : 2 * SLP]) * w
        ).astype(BF)
        gqkv[rows, 2 * SLP : 3 * SLP] = (gkv * w).astype(BF)

    rows_loop(SEQ, 16, keys_back, unroll=2)
    poll(16)

    split_rows(m.h1, gqkv.at[:, SLP : 3 * SLP], m.gvo, m.gvs)
    send("gvS", m.gvs, m.gvr, SIB)
    sent("g20", "g21", "g22", "g23", "g24", "g25")
    for k in ORDER:
        part = dot(gqkv[blk_rows(chip(k)), :], m.wqkv[...], 1, 1)
        if k == 0:
            m.own[...] = part
        else:
            m.pgh[k - 1] = part.astype(BF)
        if k == 3:
            scatter_diagonal("g1", m.pgh, m.rbg1, TOK)
        if k == 1:
            scatter_direct_x("g1", m.pgh, m.rbg1, TOK)
        if k == 2:
            scatter_direct_y("g1", m.pgh, m.rbg1, TOK)
        poll(17 + k)
    got("gqS")
    pair_sum_packed("zq", m.gqo, m.gqr, m.zqb)
    poll(21)

    def scattered(dst, mine, came, buf, half):
        for h in range(2):
            rows = pl.ds(h * half, half)
            dst[rows, :] = (
                mine[0, rows, :] + came[0, rows, :].astype(F32)
                + scatter_sum(buf, half, h, pl.ds(0, half))
            ).astype(BF)

    scatter_wait("wg")
    scattered(m.zob, m.goo, m.gor, m.rbo, ROWS // 2)
    z_start("zo0")
    z_start("zo1")
    poll(22)
    poll(23)
    scatter_combine("kg", m.pk, m.rbk, TOK // 2)
    poll(24)
    scatter_combine("g1", m.pgh, m.rbg1, TOK)
    poll(25)
    got("gvS")
    pair_sum_packed("zv", m.gvo, m.gvr, m.zvb)
    poll(26)
    scatter_combine("ou", m.pout, m.rbout, TOK)
    poll(27)
    poll(28)
    scatter_wait("kg")
    scattered(m.zkb, m.gko, m.gkr, m.rbk, TOK // 2)
    z_start("zk0")
    z_start("zk1")

    poll(29)

    poll(30)
    scatter_wait("ou")
    for h in range(2):

        def out_rows(i, h=h):
            rows = pl.ds(pl.multiple_of(h * TOK + i, 32), 32)
            m.fout[rows, :] = (
                m.resid[rows, :] + scatter_sum(m.rbout, TOK, h, pl.ds(i, 32))
            ).astype(BF)

        rows_loop(TOK, 32, out_rows)
    send("outS", m.fout.at[other_half], out_out.at[c], SIB)
    local_copy(m.fout.at[own_half], out_out.at[c])

    scatter_wait("g1")
    for h in range(2):

        def back_one(i, h=h):
            at = pl.multiple_of(h * TOK + i, 32)
            rows = pl.ds(at, 32)
            total = m.own[rows, :] + scatter_sum(m.rbg1, TOK, h, pl.ds(i, 32))
            m.fgt[rows, :] = norm_back(total, 0, m.n1, m.r1, at, m.gresid[rows, :]).astype(BF)

        rows_loop(TOK, 32, back_one, unroll=2)
    send("gtS", m.fgt.at[other_half], gtok_out.at[c], SIB)
    local_copy(m.fgt.at[own_half], gtok_out.at[c])
    poll(31)

    for cp in locals_:
        if all(cp is not done for done in (l_tok, l_pb, l_wout, l_wup, l_wdn, l_cot, *l_w)):
            cp.wait()
    for name in begun:
        if name not in in_fetch:
            got(name)
            sent(name)

    @pl.when(fetch)
    def _():
        for name in in_fetch:
            sent(name)

    for name in zitems:
        z_close(name)


FIN_IN = dict(
    gq=((CHIPS, PACK, LANES), BF),
    gv=((CHIPS, 2 * PACK, LANES), BF),
    gup=((CHIPS, ROWS, FS), BF),
    gdn=((FF // (CHIPS * CORES), D), BF),
    gwout=((ROWS, D), BF),
    gpb=((TOK, BAND), BF),
    wq=((ROWS, D), BF),
    wk=((ROWS, D), BF),
    wv=((ROWS, D), BF),
    wup=((ROWS, FF), BF),
    pb=((TOK, BAND), BF),
    out=((2, TOK, D), BF),
    gtok=((2, TOK, D), BF),
)
FIN_OUT = dict(
    q=((ROWS, D), F32),
    k=((ROWS, D), F32),
    v=((ROWS, D), F32),
    o=((ROWS, D), F32),
    up=((ROWS, FF), F32),
    dn=((FF // (CHIPS * CORES), D), F32),
    bias=((TOK, SEQ), F32),
)


def finish_kernel(
    out_in, gtok_in, gq_in, gv_in, gwout_in, gup_in, gdn_in, gpb_in, ga_in, gm_in,
    wq_in, wk_in, wv_in, wup_in, pb_in,
    out_out, gtok_out, ga_out, q_out, k_out, v_out, o_out, gm_out, up_out, dn_out, bias_out,
    *scratch,
):
    m = types.SimpleNamespace(**dict(zip((*FIN_IN, *FIN_OUT), scratch)))
    in_sem, out_sem = scratch[len(FIN_IN) + len(FIN_OUT):]
    start = pl.multiple_of(
        jnp.minimum(jnp.maximum(lax.axis_index("dp") - 2, 0), 3) * LANES, LANES
    )
    stores = []

    def store(src, dst):
        stores.append(pltpu.make_async_copy(src, dst, out_sem.at[len(stores)]))
        stores[-1].start()

    sources = dict(
        gdn=gdn_in, gup=gup_in, wup=wup_in, out=out_in, gtok=gtok_in, gq=gq_in, wq=wq_in, gv=gv_in, wk=wk_in,
        wv=wv_in, gwout=gwout_in, gpb=gpb_in, pb=pb_in.at[:, pl.ds(start, BAND)],
    )
    loads = types.SimpleNamespace(
        **{
            name: pltpu.make_async_copy(src, vars(m)[name], in_sem.at[i])
            for i, (name, src) in enumerate(sources.items())
        }
    )
    for cp in vars(loads).values():
        cp.start()

    loads.gdn.wait()
    m.dn[...] = m.gdn[...].astype(F32)
    store(m.dn, dn_out)

    def as_row(column, gain):
        square = jnp.broadcast_to(column, (ROWS, LANES))
        return jnp.transpose(square)[0:1, :] / gain[...].astype(F32)

    loads.gup.wait()
    loads.wup.wait()
    column = jnp.zeros((ROWS, 1), F32)
    for j in range(CHIPS):
        cols = slice(j * FS, (j + 1) * FS)
        g = m.gup[j].astype(F32)
        m.up[:, cols] = g
        store(m.up.at[:, cols], up_out.at[:, cols])
        column += jnp.sum(g * m.wup[:, cols].astype(F32), axis=1, keepdims=True)
    loads.out.wait()
    store(m.out, out_out)
    loads.gtok.wait()
    store(m.gtok, gtok_out)
    gm_out[...] = as_row(column, gm_in)

    def unpack(ref, j, at):
        low = ref[j, at : at + ROWS, :].astype(F32)
        high = ref[j, at + ROWS : at + PACK, :].astype(F32)
        rest = SL - LANES
        return jnp.concatenate(
            [low, jnp.concatenate([high[:, :rest], high[:, rest:]], axis=0)], axis=1
        )

    column = jnp.zeros((ROWS, 1), F32)
    for needs, ref, at, w, mine, dst in (
        ((loads.gq, loads.wq), m.gq, 0, m.wq, m.q, q_out),
        ((loads.gv, loads.wk), m.gv, 0, m.wk, m.k, k_out),
        ((loads.wv,), m.gv, PACK, m.wv, m.v, v_out),
    ):
        for cp in needs:
            cp.wait()
        g = jnp.concatenate([unpack(ref, j, at) for j in range(CHIPS)], axis=1)
        mine[...] = g
        store(mine, dst)
        column += jnp.sum(g * w[...].astype(F32), axis=1, keepdims=True)
    ga_out[...] = as_row(column, ga_in)

    loads.gwout.wait()
    m.o[...] = m.gwout[...].astype(F32)
    store(m.o, o_out)
    loads.gpb.wait()
    loads.pb.wait()
    t_ids = lax.axis_index("dp") * TOK + lax.broadcasted_iota(jnp.int32, (TOK, BAND), 0)
    u_ids = start + lax.broadcasted_iota(jnp.int32, (TOK, BAND), 1)
    m.bias[...] = jnp.zeros((TOK, SEQ), F32)
    m.bias[:, pl.ds(start, BAND)] = jnp.where(
        jnp.abs(t_ids - u_ids) < WIN, m.gpb[...].astype(F32) * jnp.exp(m.pb[...].astype(F32)), 0.0
    )
    store(m.bias, bias_out)
    for cp in stores:
        cp.wait()


def plane_program(
    tokens, lengths, cotangent, gain_attn, w_query, w_key, w_value, w_out, gain_mlp, w_up, w_down, pos_bias
):
    anywhere = pl.BlockSpec(memory_space=pl.ANY)
    whole = pl.BlockSpec(memory_space=pltpu.VMEM)
    struct = jax.ShapeDtypeStruct
    results = pl.pallas_call(
        plane_kernel,
        out_shape=(
            struct((2, TOK, D), BF),
            struct((2, TOK, D), BF),
            struct((CHIPS, PACK, LANES), BF),
            struct((CHIPS, 2 * PACK, LANES), BF),
            struct((ROWS, D), BF),
            struct((CHIPS, ROWS, FS), BF),
            struct((CHIPS, ROWS, D), BF),
            struct((TOK, BAND), BF),
        ),
        in_specs=[anywhere, pl.BlockSpec(memory_space=pltpu.SMEM), anywhere, whole, whole] + [anywhere] * 7,
        out_specs=(anywhere,) * 8,
        scratch_shapes=[pltpu.VMEM(shape, kind) for shape, kind in SCRATCH.values()]
        + [
            pltpu.SemaphoreType.DMA((N_REMOTE,)),
            pltpu.SemaphoreType.DMA((N_REMOTE,)),
            pltpu.SemaphoreType.DMA((N_LOCAL,)),
        ],
        compiler_params=pltpu.CompilerParams(
            collective_id=0, has_side_effects=True, vmem_limit_bytes=VMEM_BYTES
        ),
        cost_estimate=pl.CostEstimate(
            flops=15_000_000_000, bytes_accessed=8_000_000, transcendentals=4_000_000
        ),
        name="aft_layer",
    )(
        tokens.reshape(2, TOK, D), lengths.reshape(2), cotangent.reshape(2, TOK, D),
        gain_attn.reshape(1, ROWS), gain_mlp.reshape(1, ROWS),
        w_query, w_key, w_value, w_out, w_up, w_down, pos_bias,
    )
    out, gtok, gq, gv, gwout, gup, gdn, gpb = results
    f32_out = [struct(shape, kind) for shape, kind in FIN_OUT.values()]
    row = struct((1, ROWS), F32)
    out, gtok, grad_gain_a, grad_q, grad_k, grad_v, grad_o, grad_gain_m, grad_up, grad_down, grad_bias = (
        pl.pallas_call(
            finish_kernel,
            out_shape=(struct((2, TOK, D), BF),) * 2 + (row, *f32_out[:4], row, *f32_out[4:]),
            in_specs=[anywhere] * 8 + [whole] * 2 + [anywhere] * 5,
            out_specs=(anywhere, anywhere, whole) + (anywhere,) * 4 + (whole,) + (anywhere,) * 3,
            scratch_shapes=[pltpu.VMEM(shape, kind) for shape, kind in (*FIN_IN.values(), *FIN_OUT.values())]
            + [pltpu.SemaphoreType.DMA((len(FIN_IN),)), pltpu.SemaphoreType.DMA((len(FIN_OUT) + 1 + CHIPS,))],
            compiler_params=pltpu.CompilerParams(vmem_limit_bytes=VMEM_BYTES),
            cost_estimate=pl.CostEstimate(flops=4_000_000, bytes_accessed=9_000_000, transcendentals=100_000),
            name="gradients_out",
        )(
            out, gtok, gq, gv, gwout, gup, gdn.reshape(FF // (CHIPS * CORES), D), gpb,
            gain_attn.reshape(1, ROWS), gain_mlp.reshape(1, ROWS),
            w_query, w_key, w_value, w_up, pos_bias,
        )
    )
    return (
        out.reshape(tokens.shape),
        gtok.reshape(tokens.shape),
        grad_gain_a.reshape(ROWS),
        grad_q,
        grad_k,
        grad_v,
        grad_o,
        grad_gain_m.reshape(ROWS),
        grad_up,
        grad_down,
        grad_bias,
    )


def solution(mesh):
    in_specs = (
        P(None, "pipe", "dp", None),
        P(None, "pipe", None),
        P(None, "pipe", "dp", None),
        P("dp"),
        P("dp", None),
        P("dp", None),
        P("dp", None),
        P("dp", None),
        P("dp"),
        P("dp", None),
        P("dp", None),
        P("dp", None),
    )
    out_specs = (
        P(None, "pipe", "dp", None),
        P(None, "pipe", "dp", None),
        P("dp"),
        P("dp", None),
        P("dp", None),
        P("dp", None),
        P("dp", None),
        P("dp"),
        P("dp", None),
        P("dp", None),
        P("dp", None),
    )
    fits = mesh.shape["dp"] == CHIPS * CORES and mesh.shape["pipe"] == DEPTH
    return jax.shard_map(plane_program if fits else local, mesh=mesh, in_specs=in_specs, out_specs=out_specs, check_vma=False)
```
